32 devices in a mesh: img: 8 (over y, x, core), strip: 4 (over z).
Axes of the slice: x: 2, y: 2, z: 4, core: 2. Of those that a mesh axis runs over, the one named last changes fastest.
Arguments:
- pixels: bfloat16 [16, 48, 32, 3072], P('img', 'strip'), may hold values from -6 to 6
- cotangent: bfloat16 [16, 48, 32, 768], P('img', 'strip'), may hold values from -1.5 to 1.5
- resize: float32 [4, 32, 32], replicated, may hold values from -1 to 1
- patch_index: int32 [16], replicated, may hold values from 0 to 3
- slot_image: int32 [16], replicated, may hold values from 0 to 15, each once
- strip_rows: int32 [16, 4], replicated, may hold values from 1 to 12, 32 in all within a row
- patch_weight: bfloat16 [3072, 768], P(('img', 'strip')), may hold values from -0.109375 to 0.109375
- pos_grid: bfloat16 [49, 768], P(None, ('img', 'strip')), may hold values from -3 to 3
- patch_bias: bfloat16 [768], P(('img', 'strip')), may hold values from -1 to 1
- attention_norm_gain: bfloat16 [768], P(('img', 'strip')), may hold values from 0.5 to 1.5
- attn_shift: bfloat16 [768], P(('img', 'strip')), may hold values from -0.5 to 0.5
- query_weight: bfloat16 [768, 768], P(('img', 'strip')), may hold values from -0.21875 to 0.21875
- query_bias: bfloat16 [768], P(('img', 'strip')), may hold values from -1 to 1
- key_weight: bfloat16 [768, 768], P(('img', 'strip')), may hold values from -0.21875 to 0.21875
- value_weight: bfloat16 [768, 768], P(('img', 'strip')), may hold values from -0.21875 to 0.21875
- value_bias: bfloat16 [768], P(('img', 'strip')), may hold values from -0.25 to 0.25
- out_weight: bfloat16 [768, 768], P(('img', 'strip')), may hold values from -3 to 3
- out_bias: bfloat16 [768], P(('img', 'strip')), may hold values from -2.5 to 2.5
- mlp_gain: bfloat16 [768], P(('img', 'strip')), may hold values from 0.099609375 to 1.8984375
- mlp_shift: bfloat16 [768], P(('img', 'strip')), may hold values from -1.5 to 1.5
- up_weight: bfloat16 [768, 3072], P(('img', 'strip')), may hold values from -0.21875 to 0.21875
- up_bias: bfloat16 [3072], P(('img', 'strip')), may hold values from -1 to 1
- down_weight: bfloat16 [3072, 768], P(('img', 'strip')), may hold values from -0.109375 to 0.109375
- down_bias: bfloat16 [768], P(('img', 'strip')), may hold values from -2.5 to 2.5
Outputs:
- block_out: bfloat16 [16, 48, 32, 768], P('img', 'strip')
- pixel_grad: float32 [16, 48, 32, 3072], P('img', 'strip')
- grad_patch_weight: float32 [3072, 768], P(('img', 'strip'))
- grad_pos_grid: float32 [49, 768], P(None, ('img', 'strip'))
- grad_patch_bias: float32 [768], P(('img', 'strip'))
- grad_attn_gain: float32 [768], P(('img', 'strip'))
- grad_attn_shift: float32 [768], P(('img', 'strip'))
- grad_query_weight: float32 [768, 768], P(('img', 'strip'))
- grad_query_bias: float32 [768], P(('img', 'strip'))
- grad_key_weight: float32 [768, 768], P(('img', 'strip'))
- grad_value_weight: float32 [768, 768], P(('img', 'strip'))
- grad_value_bias: float32 [768], P(('img', 'strip'))
- output_weight_gradient: float32 [768, 768], P(('img', 'strip'))
- grad_out_bias: float32 [768], P(('img', 'strip'))
- grad_mlp_gain: float32 [768], P(('img', 'strip'))
- grad_mlp_shift: float32 [768], P(('img', 'strip'))
- grad_up_weight: float32 [768, 3072], P(('img', 'strip'))
- grad_up_bias: float32 [3072], P(('img', 'strip'))
- grad_down_weight: float32 [3072, 768], P(('img', 'strip'))
- grad_down_bias: float32 [768], P(('img', 'strip'))
The draws below stay inside these ranges and needn't reach their ends.
Inputs may be any that keep to these rules, and one draw needn't show every extreme that they name: `patch_index`: the patch size of an image is (its index + 1) * 8 pixels. `slot_image`: every image is held by exactly one slot. `strip_rows`: each slot's entries sum to 32; in every draw some entry equals 12.
All inputs are finite; a program needn't handle non-finite values.
Results may differ from the reference program's by a relative error of at most 0.015.
Values may be sent and summed in bfloat16 or wider, within the bound.
No kernel may reach another device: no remote copies, remote signals or barrier semaphores. Data moves between devices by JAX's collectives and lax.ppermute only.
A program may use at most 256 MiB of HBM per device.

```python
import math
import jax
import jax.numpy as jnp
import numpy as np
from jax import lax

D = 768
HEADS = 12
HD = 64
FF = 3072
PM = 32
BASE = 7
NPS = 4
GRID = 32
CAPR = 12
PIX = 3072
PSTEP = 8
SLOTS = 16
N_STRIP = 4


def with_ends(drawn, key, smallest, largest):
    longest = drawn.shape.index(max(drawn.shape))
    spots = []
    for shift in (0, 1):
        where = [jax.random.randint(jax.random.fold_in(key, axis), (), 0, length) for axis, length in enumerate(drawn.shape)]
        where[longest] = (where[longest] + shift) % drawn.shape[longest]
        spots.append(tuple(where))
    return drawn.at[spots[0]].set(smallest).at[spots[1]].set(largest)


def block_levels(stream_key, dims, shards, least, top_value):
    def one(dim, blocks):
        draws = jax.random.uniform(jax.random.fold_in(jax.random.fold_in(stream_key, 6), dim), (blocks,), jnp.float32, least / len(shards), top_value / len(shards))
        return jnp.repeat(jnp.exp(draws), dims[dim] // blocks).reshape((-1,) + (1,) * (len(dims) - dim - 1))

    factor_of = one(*shards[0])
    for cut in shards[1:]:
        factor_of = factor_of * one(*cut)
    return factor_of


def split_up(number_of, total, bound, lean):
    loads = [(1 << 20) // math.isqrt(standing ** lean) + 1 for standing in range(2, number_of + 1)]
    rest, given = total - bound - (number_of - 1), [1] * (number_of - 1)
    while rest > 0:
        movable = [i for i in range(number_of - 1) if given[i] < bound]
        pool, left = sum([loads[i] for i in movable]), rest
        for i in movable:
            addition = min(bound - given[i], max(1, left * loads[i] // pool), rest)
            given[i] = given[i] + addition
            rest = rest - addition
    return np.array([bound] + given)


def uneven(rng, number_of, total, limit, skew):
    if number_of == 2:
        one = jax.random.randint(rng, (), max(1, total - limit), min(limit, total - 1) + 1)
        return jnp.stack([one, total - one])
    sizes = jnp.asarray(split_up(number_of, total, limit, skew), jnp.int32)
    twos = (number_of - 1) // 2
    giver, receiver = sizes[1:1 + 2 * twos:2], sizes[2:2 + 2 * twos:2]
    slack = jnp.minimum(giver - 1, limit - receiver)
    moved = jax.random.randint(jax.random.fold_in(rng, 1), (twos,), 0, 1 << 20) % (slack + 1)
    sizes = sizes.at[1:1 + 2 * twos:2].set(giver - moved).at[2:2 + 2 * twos:2].set(receiver + moved)
    return sizes[jax.random.permutation(jax.random.fold_in(rng, 2), number_of)]


def scatter_about(key, shape, scale, most, split=(), dtype=jnp.bfloat16):
    level = block_levels(key, shape, split, -0.22, 0.18) if split else 1.0
    values = jax.random.normal(key, shape, jnp.float32) * scale * level
    return jnp.minimum(jnp.maximum(values, -most), most).astype(dtype)


def setup_inputs(seed: int = 0) -> dict:
    streams_of = jax.random.split(jax.random.key(seed), 25)
    pixels = scatter_about(streams_of[0], (SLOTS, N_STRIP * CAPR, GRID, PIX), 1.0, 6.0, ((0, 8), (1, 4)))
    cotangent = scatter_about(streams_of[1], (SLOTS, N_STRIP * CAPR, GRID, D), 0.25, 1.5, ((0, 8), (1, 4)))
    resize = scatter_about(streams_of[2], (NPS, PM, PM), PM ** -0.5, 1.0, (), jnp.float32)
    patch_index = with_ends(jax.random.randint(streams_of[3], (SLOTS,), 0, NPS), jax.random.fold_in(streams_of[3], 1), 0, NPS - 1).astype(jnp.int32)
    slot_image = jax.random.permutation(streams_of[4], SLOTS).astype(jnp.int32)
    strip_rows = jax.vmap(lambda own: uneven(own, N_STRIP, GRID, CAPR, 1))(jax.random.split(streams_of[5], SLOTS)).reshape((SLOTS, N_STRIP)).astype(jnp.int32)
    patch_weight = scatter_about(streams_of[6], (PIX, D), PIX ** -0.5, 0.109375, ((0, 32),))
    pos_grid = scatter_about(streams_of[7], (BASE * BASE, D), 0.5, 3.0, ((1, 32),))
    patch_bias = scatter_about(streams_of[8], (D,), 0.2, 1.0, ((0, 32),))
    attention_norm_gain = jnp.clip(1.0 + 0.1 * jax.random.normal(streams_of[9], (D,), jnp.float32), 0.5, 1.5).astype(jnp.bfloat16)
    attn_shift = scatter_about(streams_of[10], (D,), 0.1, 0.5, ((0, 32),))
    query_weight = scatter_about(streams_of[11], (D, D), D ** -0.5, 0.21875, ((0, 32),))
    query_bias = scatter_about(streams_of[12], (D,), 0.2, 1.0, ((0, 32),))
    key_weight = scatter_about(streams_of[13], (D, D), D ** -0.5, 0.21875, ((0, 32),))
    value_weight = scatter_about(streams_of[14], (D, D), D ** -0.5, 0.21875, ((0, 32),))
    value_bias = scatter_about(streams_of[15], (D,), 0.05, 0.25, ((0, 32),))
    out_weight = scatter_about(streams_of[16], (D, D), 4 ** -0.5, 3.0, ((0, 32),))
    out_bias = scatter_about(streams_of[17], (D,), 0.5, 2.5, ((0, 32),))
    mlp_gain = jnp.clip(1.0 + 0.18 * jax.random.normal(streams_of[18], (D,), jnp.float32), 0.099609375, 1.8984375).astype(jnp.bfloat16)
    mlp_shift = scatter_about(streams_of[19], (D,), 0.3, 1.5, ((0, 32),))
    up_weight = scatter_about(streams_of[20], (D, FF), D ** -0.5, 0.21875, ((0, 32),))
    up_bias = scatter_about(streams_of[21], (FF,), 0.2, 1.0, ((0, 32),))
    down_weight = scatter_about(streams_of[22], (FF, D), FF ** -0.5, 0.109375, ((0, 32),))
    down_bias = scatter_about(streams_of[23], (D,), 0.5, 2.5, ((0, 32),))
    return {"pixels": pixels, "cotangent": cotangent, "resize": resize, "patch_index": patch_index, "slot_image": slot_image, "strip_rows": strip_rows, "patch_weight": patch_weight, "pos_grid": pos_grid, "patch_bias": patch_bias, "attention_norm_gain": attention_norm_gain, "attn_shift": attn_shift, "query_weight": query_weight, "query_bias": query_bias, "key_weight": key_weight, "value_weight": value_weight, "value_bias": value_bias, "out_weight": out_weight, "out_bias": out_bias, "mlp_gain": mlp_gain, "mlp_shift": mlp_shift, "up_weight": up_weight, "up_bias": up_bias, "down_weight": down_weight, "down_bias": down_bias}


@jax.custom_vjp
def low(v):
    return lax.optimization_barrier(v.astype(jnp.bfloat16)).astype(jnp.float32)

@jax.custom_vjp
def low_back(v):
    return v

def low_keep(v):
    return (low(v), None)

def low_pass(kept, grad):
    return (grad,)

def back_keep(v):
    return (v, None)

def back_low(kept, grad):
    return (low(grad),)
low.defvjp(low_keep, low_pass)
low_back.defvjp(back_keep, back_low)
HIGH_ACCURACY = lax.Precision.HIGHEST

def bilinear(out_count, in_count):
    source = (jnp.arange(out_count).astype(jnp.float32) + 0.5) * (in_count / out_count) - 0.5
    source = jnp.clip(source, 0.0, in_count - 1.0)
    target = jnp.arange(in_count).astype(jnp.float32)
    return jnp.maximum(1.0 - jnp.abs(source[:, None] - target[None, :]), 0.0)

def layer_norm(values, gain, shift):
    centred = values - lax.optimization_barrier(jnp.mean(values, axis=-1, keepdims=True))
    token_spread = lax.optimization_barrier(jnp.mean(centred * centred, axis=-1, keepdims=True))
    return centred * lax.rsqrt(token_spread + 1e-06) * gain + shift

def matmul(left, right):
    return jnp.dot(left, right, precision=HIGH_ACCURACY, preferred_element_type=jnp.float32)

def image_forward_pass(params, pix, mixer, token_spread):
    patch_weight, pos_grid, patch_bias, attention_norm_gain, attn_shift, query_weight, query_bias, key_weight, value_weight, value_bias, out_weight, out_bias, mlp_gain, mlp_shift, up_weight, up_bias, down_weight, down_bias = params
    patches = pix.shape[0]
    mixed = jnp.einsum('tcj,jk->tck', pix.reshape(patches, 3, PM * PM), mixer, precision=HIGH_ACCURACY)
    base_pixels = low(low_back(mixed.reshape(patches, PIX)))
    place = jnp.einsum('ga,hb,abd->ghd', token_spread, token_spread, pos_grid.reshape(BASE, BASE, D), precision=HIGH_ACCURACY)
    embed = low_back(matmul(base_pixels, patch_weight)) + patch_bias + place.reshape(patches, D)
    attn_in = low(layer_norm(embed, attention_norm_gain, attn_shift))
    query = low(low_back((matmul(attn_in, query_weight) + query_bias) * 0.125))
    key = low(low_back(matmul(attn_in, key_weight)))
    value = low(low_back(matmul(attn_in, value_weight) + value_bias))
    q_heads = query.reshape(patches, HEADS, HD).transpose(1, 0, 2)
    k_heads = key.reshape(patches, HEADS, HD).transpose(1, 0, 2)
    v_heads = value.reshape(patches, HEADS, HD).transpose(1, 0, 2)
    scores = low_back(jnp.einsum('hqd,hkd->hqk', q_heads, k_heads, precision=HIGH_ACCURACY))
    probs = low(jax.nn.softmax(scores, axis=-1))
    heads_out = jnp.einsum('hqk,hkd->hqd', probs, v_heads, precision=HIGH_ACCURACY)
    attended = low(low_back(heads_out.transpose(1, 0, 2).reshape(patches, D)))
    resid = embed + low_back(matmul(attended, out_weight)) + out_bias
    mlp_in = low(layer_norm(resid, mlp_gain, mlp_shift))
    upper = low_back(matmul(mlp_in, up_weight)) + up_bias
    hidden_features = low(jax.nn.gelu(upper, approximate=False))
    return resid + low_back(matmul(hidden_features, down_weight)) + down_bias

def reference(pixels, cotangent, resize, patch_index, slot_image, strip_rows, patch_weight, pos_grid, patch_bias, attention_norm_gain, attn_shift, query_weight, query_bias, key_weight, value_weight, value_bias, out_weight, out_bias, mlp_gain, mlp_shift, up_weight, up_bias, down_weight, down_bias):
    params = tuple((w.astype(jnp.float32) for w in (patch_weight, pos_grid, patch_bias, attention_norm_gain, attn_shift, query_weight, query_bias, key_weight, value_weight, value_bias, out_weight, out_bias, mlp_gain, mlp_shift, up_weight, up_bias, down_weight, down_bias)))
    token_spread = bilinear(GRID, BASE)
    side_iota = jnp.arange(PM).astype(jnp.int32)

    def one_slot(totals, slot):
        image = slot_image[slot]
        size_index = patch_index[image]
        patch_side = PSTEP * (size_index + 1)
        table = resize[size_index] * (side_iota < patch_side).astype(jnp.float32)[:, None]
        mixer = (table[:, None, :, None] * table[None, :, None, :]).reshape(PM * PM, PM * PM)
        mixer = lax.optimization_barrier(mixer.astype(jnp.bfloat16)).astype(jnp.float32)
        counts = strip_rows[slot].astype(jnp.int32)
        ends = jnp.cumsum(counts).astype(jnp.int32)
        rows = jnp.arange(GRID).astype(jnp.int32)
        owner = lax.optimization_barrier(jnp.sum((rows[:, None] >= ends[None, :-1]).astype(jnp.int32), axis=1)).astype(jnp.int32)
        first = (ends - counts)[owner]
        padded_row = (owner * CAPR + rows - first).astype(jnp.int32)
        pix = pixels[slot][padded_row].astype(jnp.float32).reshape(GRID * GRID, PIX)
        cot = cotangent[slot][padded_row].astype(jnp.float32).reshape(GRID * GRID, D)
        out, pullback = jax.vjp(lambda p, x: image_forward_pass(p, x, mixer, token_spread), params, pix)
        grads, pix_grad = pullback(cot)
        totals = jax.tree.map(lambda a, b: a + b, totals, grads)
        out_pad = jnp.zeros((N_STRIP * CAPR, GRID, D), jnp.float32).at[padded_row].set(out.reshape(GRID, GRID, D))
        grad_pad = jnp.zeros((N_STRIP * CAPR, GRID, PIX), jnp.float32).at[padded_row].set(pix_grad.reshape(GRID, GRID, PIX))
        return (totals, (out_pad.astype(jnp.bfloat16), grad_pad))
    zeros = tuple((jnp.zeros(w.shape, jnp.float32) for w in params))
    totals, (block_out, pixel_grad) = lax.scan(one_slot, zeros, jnp.arange(SLOTS).astype(jnp.int32))
    g_patch_weight, g_pos_grid, g_patch_bias, g_attn_gain, g_attn_shift, g_query_weight, g_query_bias, g_key_weight, g_value_weight, g_value_bias, g_out_weight, g_out_bias, g_mlp_gain, g_mlp_shift, g_up_weight, g_up_bias, g_down_weight, g_down_bias = totals
    return (block_out, pixel_grad, g_patch_weight, g_pos_grid, g_patch_bias, g_attn_gain, g_attn_shift, g_query_weight, g_query_bias, g_key_weight, g_value_weight, g_value_bias, g_out_weight, g_out_bias, g_mlp_gain, g_mlp_shift, g_up_weight, g_up_bias, g_down_weight, g_down_bias)
```

```python
import jax
import jax.numpy as jnp
import numpy as np
from jax import lax
from jax.sharding import PartitionSpec as P

HEADS = 12
BASE = 7
HIGH_ACCURACY = lax.Precision.HIGHEST
AXES = ("img", "strip")


def bilinear(out_count, in_count):
    source = (np.arange(out_count, dtype=np.float32) + 0.5) * (in_count / out_count) - 0.5
    source = np.clip(source, 0.0, in_count - 1.0)
    target = np.arange(in_count, dtype=np.float32)
    return np.maximum(1.0 - np.abs(source[:, None] - target[None, :]), 0.0).astype(np.float32)


def layer_norm(values, gain, shift):
    centred = values - jnp.mean(values, axis=-1, keepdims=True)
    token_spread = jnp.mean(centred * centred, axis=-1, keepdims=True)
    return centred * lax.rsqrt(token_spread + 1e-06) * gain + shift


def gelu_exact(values):
    return jax.nn.gelu(values, approximate=False)


def matmul(left, right):
    return jnp.dot(left, right, preferred_element_type=jnp.float32)


def left_trans(left, right):
    return lax.dot_general(
        left, right, (((0,), (0,)), ((), ())), preferred_element_type=jnp.float32
    )


def right_trans(left, right):
    return lax.dot_general(
        left, right, (((1,), (1,)), ((), ())), preferred_element_type=jnp.float32
    )


class Place:
    def __init__(self, group):
        self.group = group
        self.images = lax.axis_size("img")
        self.strips = lax.axis_size("strip")
        assert 2 * group == self.strips
        self.img = lax.axis_index("img")
        self.core = self.img % 2
        self.z = lax.axis_index("strip")
        self.host = self.z // group == self.core

    def flat(self, img, z):
        return img * self.strips + z

    def swap_core(self, values):
        return lax.ppermute(values, "img", [(i, i ^ 1) for i in range(self.images)])

    def across_img(self, values, bit):
        return lax.ppermute(values, "img", [(i, i ^ bit) for i in range(self.images)])

    def along_z(self, values, r):
        return lax.ppermute(values, "strip", [(z, z ^ r) for z in range(self.strips)])

    def route(self, r, back):
        pairs = [
            (self.flat(i, z), self.flat(i, z ^ r))
            for i in range(self.images)
            for z in range(self.strips)
            if (z ^ r) // self.group == i % 2
        ]
        return [(b, a) for a, b in pairs] if back else pairs

    def half(self, to_host):
        return [
            (self.flat(i, z), self.flat(i ^ 1, z))
            for i in range(self.images)
            for z in range(self.strips)
            if (z // self.group == i % 2) != to_host
        ]


def pick(values, index, axis=0):
    return lax.dynamic_index_in_dim(values, index, axis, keepdims=False)


def to_image(place, values, starts):
    group, capacity, grid, width = values.shape
    blocks = [pick(values, place.z % group)]
    for r in range(1, place.strips):
        send = pick(values, (place.z ^ r) % group)
        blocks.append(lax.ppermute(send, AXES, place.route(r, False)))
    stacked = jnp.stack(blocks)
    rows = jnp.zeros((grid + capacity, grid, width), values.dtype)
    for j in range(place.strips):
        rows = lax.dynamic_update_slice(rows, pick(stacked, place.z ^ j), (starts[j], 0, 0))
    half = grid // 2
    kept = lax.dynamic_slice_in_dim(rows, place.core * half, half, 0)
    sent = lax.dynamic_slice_in_dim(rows, (1 - place.core) * half, half, 0)
    received = lax.ppermute(sent, AXES, place.half(False))
    return jnp.where(place.host, kept, received).reshape(half * grid, width)


def to_strips(place, values, starts, capacity, grid):
    tokens, width = values.shape
    received = lax.ppermute(values, AXES, place.half(True))
    low = jnp.where(place.core == 0, values, received)
    high = jnp.where(place.core == 0, received, values)
    pad = jnp.zeros((capacity, grid, width), values.dtype)
    rows = jnp.concatenate(
        [low.reshape(-1, grid, width), high.reshape(-1, grid, width), pad], axis=0
    )
    pieces = []
    for r in range(place.strips):
        piece = lax.dynamic_slice(
            rows, (pick(starts, place.z ^ r), 0, 0), (capacity, grid, width)
        )
        if r:
            piece = lax.ppermute(piece, AXES, place.route(r, True))
        pieces.append(piece)
    out = []
    for g in range(place.group):
        owner = (place.img % 2) * place.group + g
        block = pieces[0]
        for r in range(1, place.strips):
            block = jnp.where(place.z ^ r == owner, pieces[r], block)
        out.append(block)
    return jnp.stack(out)


def scatter_sum(place, grad, low):
    f32 = jnp.float32
    width = grad.shape[-1]
    hi = place.images // 2
    grad = grad.reshape(hi, 2, -1, width)
    send = pick(grad, 1 - place.core, 1).astype(low)
    total = pick(grad, place.core, 1).astype(f32) + place.swap_core(send).astype(f32)
    bits = []
    bit = 2
    while bit < place.images:
        bits.append(bit)
        bit *= 2
    cuts = len(bits) if width % (128 * len(bits)) == 0 else 1
    done = []
    for cut in range(cuts):
        part = total[..., cut * (width // cuts) : (cut + 1) * (width // cuts)]
        part = part.reshape((2,) * len(bits) + part.shape[1:])
        axes = list(reversed(bits))
        order = bits[cut:] + bits[:cut]
        for bit in order:
            axis = axes.index(bit)
            mine = (place.img // bit) % 2
            sent = pick(part, 1 - mine, axis).astype(low)
            part = pick(part, mine, axis) + place.across_img(sent, bit).astype(f32)
            axes.pop(axis)
        part = part.reshape(place.strips, -1, width // cuts)
        mine = pick(part, place.z)
        for r in range(1, place.strips):
            sent = pick(part, place.z ^ r).astype(low)
            mine = mine + place.along_z(sent, r).astype(f32)
        done.append(mine)
    return jnp.concatenate(done, axis=-1)


def body(
    pixels,
    cotangent,
    resize,
    patch_index,
    slot_image,
    strip_rows,
    patch_weight,
    pos_grid,
    patch_bias,
    attention_norm_gain,
    attn_shift,
    query_weight,
    query_bias,
    key_weight,
    value_weight,
    value_bias,
    out_weight,
    out_bias,
    mlp_gain,
    mlp_shift,
    up_weight,
    up_bias,
    down_weight,
    down_bias,
):
    group, capacity, grid, pixel_len = pixels.shape
    width = cotangent.shape[3]
    ff = up_weight.shape[1]
    local_rows = capacity * grid
    tokens = group * local_rows
    f32 = jnp.float32
    bf16 = jnp.bfloat16
    place = Place(group)
    devices = place.images * place.strips
    first_slot = place.img * group
    shard = patch_bias.shape[0]

    vectors = (
        patch_bias,
        attention_norm_gain,
        attn_shift,
        query_bias,
        value_bias,
        out_bias,
        mlp_gain,
        mlp_shift,
        down_bias,
    )
    small = jnp.concatenate(vectors + (up_bias, pos_grid.reshape(-1)))
    pad = -small.shape[0] % width
    small = jnp.pad(small, (0, pad)).reshape(-1, width)
    small_rows = small.shape[0]
    extra = 16 * (-(-small_rows // 16))
    small = jnp.pad(small, ((0, extra - small_rows), (0, 0)))
    w_patch = lax.all_gather(patch_weight, AXES, axis=0, tiled=True)
    packed = lax.all_gather(
        jnp.concatenate([query_weight, key_weight, value_weight, out_weight, small]), AXES, axis=0
    )
    w_up = lax.all_gather(up_weight, AXES, axis=0, tiled=True)
    w_down = lax.all_gather(down_weight, AXES, axis=0, tiled=True)
    w_query, w_key, w_value, w_out = (
        packed[:, i * shard : (i + 1) * shard].reshape(width, width) for i in range(4)
    )
    flat_small = packed[:, 4 * shard :].reshape(devices, -1)
    full_vectors = [
        flat_small[:, i * shard : (i + 1) * shard].reshape(1, width).astype(f32)
        for i in range(len(vectors))
    ]
    b_patch, g_one, c_one, b_query, b_value, b_out, g_two, c_two, b_down = full_vectors
    at = len(vectors) * shard
    ups = up_bias.shape[0]
    b_up = flat_small[:, at : at + ups].reshape(1, ff).astype(f32)
    at += ups
    grid_pos = (
        flat_small[:, at : at + BASE * BASE * shard]
        .reshape(devices, BASE * BASE, shard)
        .transpose(1, 0, 2)
        .reshape(BASE * BASE, width)
        .astype(f32)
    )

    size_count = resize.shape[0]
    side = resize.shape[1]
    step_px = side // size_count
    slot_ids = lax.dynamic_slice_in_dim(slot_image, first_slot, group)
    picked = slot_ids[:, None] == jnp.arange(patch_index.shape[0], dtype=jnp.int32)[None, :]
    size_index = jnp.sum(jnp.where(picked, patch_index[None, :], 0), axis=1)
    limit = step_px * (size_index + 1)
    tables = jnp.stack([pick(resize, size_index[g]) for g in range(group)])
    tables = jnp.where(
        jnp.arange(side, dtype=jnp.int32)[None, :, None] < limit[:, None, None], tables, 0.0
    )
    wide_rows = jnp.repeat(tables, side, axis=2)
    wide_columns = jnp.tile(tables, (1, 1, side))
    mixers = (
        (wide_rows[:, :, None, :] * wide_columns[:, None, :, :])
        .reshape(group, side * side, side * side)
        .astype(bf16)
    )
    counts = lax.dynamic_slice_in_dim(strip_rows, first_slot, group, 0)
    row_iota = jnp.arange(capacity, dtype=jnp.int32)
    live = row_iota[None, :] < pick(counts, place.z, 1)[:, None]
    token_live = jnp.broadcast_to(live[:, :, None, None], (group, capacity, grid, 1))
    image_counts = pick(strip_rows, (place.img // 2) * 2 * group + place.z)
    starts = jnp.cumsum(image_counts) - image_counts

    pix = pixels.reshape(group, local_rows, 3, side * side)
    base = [
        jnp.einsum(
            "gtj,gjk->gtk", pix[:, :, c], mixers, preferred_element_type=f32
        ).astype(bf16)
        for c in range(3)
    ]
    base_pixels = jnp.concatenate(base, axis=-1).reshape(tokens, pixel_len)
    patches = matmul(base_pixels, w_patch).astype(bf16)
    patches = to_image(place, patches.reshape(group, capacity, grid, width), starts).astype(f32)
    g_out_low = to_image(place, cotangent, starts)

    half = grid // 2
    spread = bilinear(grid, BASE)
    spread_all = jnp.asarray((spread[:, None, :, None] * spread[None, :, None, :]).reshape(2, half * grid, BASE * BASE))
    spread_here = pick(spread_all, place.core)
    place_rows = jnp.dot(spread_here, grid_pos, precision=HIGH_ACCURACY)
    embed = patches + b_patch + place_rows
    normed_one, norm_one_back = jax.vjp(layer_norm, embed, g_one, c_one)
    attn_in = normed_one.astype(bf16)
    query = ((matmul(attn_in, w_query) + b_query) * 0.125).astype(bf16)
    key = matmul(attn_in, w_key).astype(bf16)
    value = (matmul(attn_in, w_value) + b_value).astype(bf16)
    rows = query.shape[0]
    size = width // HEADS

    def split(values):
        return values.reshape(-1, HEADS, size).transpose(1, 0, 2)

    def join(values):
        return values.transpose(1, 0, 2).reshape(-1, width)

    keys = jnp.concatenate([key, place.swap_core(key)], axis=0)
    values = jnp.concatenate([value, place.swap_core(value)], axis=0)
    q_heads, k_heads, v_heads = split(query), split(keys), split(values)
    scores = jnp.einsum("hqd,hkd->hqk", q_heads, k_heads, preferred_element_type=f32)
    peak = jnp.max(scores, axis=-1, keepdims=True)
    expd = jnp.exp(scores - peak)
    denom = jnp.sum(expd, axis=-1, keepdims=True)
    probs = expd / denom
    probs_low = probs.astype(bf16)
    attended = join(
        jnp.einsum("hqk,hkd->hqd", probs_low, v_heads, preferred_element_type=f32).astype(bf16)
    )
    resid = embed + matmul(attended, w_out) + b_out
    normed_two, norm_two_back = jax.vjp(layer_norm, resid, g_two, c_two)
    mlp_in = normed_two.astype(bf16)
    upper = matmul(mlp_in, w_up) + b_up
    activ, gelu_back = jax.vjp(gelu_exact, upper)
    hidden = activ.astype(bf16)
    final = (resid + matmul(hidden, w_down) + b_down).astype(bf16)
    block_out = to_strips(place, final, starts, capacity, grid)
    block_out = jnp.where(token_live, block_out, 0.0)

    def column_sum(values):
        return jnp.sum(values, axis=0)

    g_out = g_out_low.astype(f32)
    grad_down_bias = column_sum(g_out)
    grad_down_weight = left_trans(hidden, g_out_low).astype(bf16)
    down_sum = scatter_sum(place, grad_down_weight, bf16)
    (g_upper,) = gelu_back(right_trans(g_out_low, w_down))
    grad_up_bias = column_sum(g_upper)
    g_upper_low = g_upper.astype(bf16)
    grad_up_weight = left_trans(mlp_in, g_upper_low).astype(bf16)
    up_sum = scatter_sum(place, grad_up_weight, bf16)
    g_resid_norm, grad_mlp_gain, grad_mlp_shift = norm_two_back(right_trans(g_upper_low, w_up))
    g_resid = g_out + g_resid_norm
    grad_out_bias = column_sum(g_resid)
    g_resid_low = g_resid.astype(bf16)
    grad_out_weight = left_trans(attended, g_resid_low).astype(bf16)
    g_att = split(right_trans(g_resid_low, w_out).astype(bf16))

    g_probs = jnp.einsum("hqd,hkd->hqk", g_att, v_heads, preferred_element_type=f32)
    inner = jnp.sum(probs * g_probs, axis=-1, keepdims=True)
    g_scores = (probs * (g_probs - inner)).astype(bf16)
    g_query = join(jnp.einsum("hqk,hkd->hqd", g_scores, k_heads, preferred_element_type=f32))
    g_keys = join(jnp.einsum("hqk,hqd->hkd", g_scores, q_heads, preferred_element_type=f32))
    g_values = join(jnp.einsum("hqk,hqd->hkd", probs_low, g_att, preferred_element_type=f32))
    g_key = g_keys[:rows] + place.swap_core(g_keys[rows:].astype(bf16)).astype(f32)
    g_value = g_values[:rows] + place.swap_core(g_values[rows:].astype(bf16)).astype(f32)
    g_key_low = g_key.astype(bf16)
    g_value_low = g_value.astype(bf16)
    g_qin = g_query.astype(bf16).astype(f32) * 0.125
    grad_query_bias = column_sum(g_qin)
    g_qin_low = g_qin.astype(bf16)
    grad_query_weight = left_trans(attn_in, g_qin_low).astype(bf16)
    grad_key_weight = left_trans(attn_in, g_key_low).astype(bf16)
    grad_value_weight = left_trans(attn_in, g_value_low).astype(bf16)
    grad_value_bias = column_sum(g_value_low.astype(f32))
    qkvo = jnp.concatenate(
        [
            w.reshape(devices, shard, width)
            for w in (grad_query_weight, grad_key_weight, grad_value_weight, grad_out_weight)
        ],
        axis=1,
    ).reshape(-1, width)
    qkvo_sum = scatter_sum(place, qkvo, bf16)
    g_norm_in = (
        right_trans(g_qin_low, w_query)
        + right_trans(g_key_low, w_key)
        + right_trans(g_value_low, w_value)
    )
    g_embed_norm, grad_attn_gain, grad_attn_shift = norm_one_back(g_norm_in)
    g_embed = g_resid + g_embed_norm
    grad_patch_bias = column_sum(g_embed)
    grad_pos = lax.dot_general(
        spread_here, g_embed, (((0,), (0,)), ((), ())), precision=HIGH_ACCURACY
    )
    back = to_strips(place, g_embed.astype(bf16), starts, capacity, grid)
    g_embed_low = jnp.where(token_live, back, 0.0).reshape(tokens, width)
    grad_patch_weight = left_trans(base_pixels, g_embed_low).astype(bf16)
    patch_sum = scatter_sum(place, grad_patch_weight, bf16)

    pieces = [
        g.reshape(devices, shard)
        for g in (
            grad_patch_bias,
            grad_attn_gain,
            grad_attn_shift,
            grad_query_bias,
            grad_value_bias,
            grad_out_bias,
            grad_mlp_gain,
            grad_mlp_shift,
            grad_down_bias,
        )
    ]
    pieces.append(grad_up_bias.reshape(devices, ups))
    pieces.append(
        grad_pos.reshape(BASE * BASE, devices, shard).transpose(1, 0, 2).reshape(devices, -1)
    )
    small_grads = jnp.concatenate(pieces, axis=1)
    small_grads = jnp.pad(small_grads, ((0, 0), (0, pad))).reshape(devices * small_rows, width)
    small_sum = scatter_sum(place, small_grads, f32).reshape(-1)

    g_base = right_trans(g_embed_low, w_patch).astype(bf16).reshape(group, local_rows, pixel_len)
    wide = side * side
    pixel_grad = jnp.concatenate(
        [
            jnp.einsum(
                "gtk,gjk->gtj",
                g_base[:, :, c * wide : (c + 1) * wide],
                mixers,
                preferred_element_type=f32,
            )
            for c in range(3)
        ],
        axis=-1,
    ).reshape(pixels.shape)

    sums = [small_sum[i * shard : (i + 1) * shard] for i in range(len(vectors))]
    at = len(vectors) * shard
    s_up_bias = small_sum[at : at + ups]
    at += ups
    s_pos = small_sum[at : at + BASE * BASE * shard].reshape(BASE * BASE, shard)
    s_query, s_key, s_value, s_out = (qkvo_sum[i * shard : (i + 1) * shard] for i in range(4))
    return (
        block_out,
        pixel_grad,
        patch_sum,
        s_pos,
        sums[0],
        sums[1],
        sums[2],
        s_query,
        sums[3],
        s_key,
        s_value,
        sums[4],
        s_out,
        sums[5],
        sums[6],
        sums[7],
        up_sum,
        s_up_bias,
        down_sum,
        sums[8],
    )


def solution(mesh):
    rows = P(("img", "strip"))
    split_rows = P(("img", "strip"), None)
    split_columns = P(None, ("img", "strip"))
    held = P("img", "strip", None, None)
    return jax.shard_map(
        body,
        mesh=mesh,
        in_specs=(
            held,
            held,
            P(),
            P(),
            P(),
            P(),
            split_rows,
            split_columns,
            rows,
            rows,
            rows,
            split_rows,
            rows,
            split_rows,
            split_rows,
            rows,
            split_rows,
            rows,
            rows,
            rows,
            split_rows,
            rows,
            split_rows,
            rows,
        ),
        out_specs=(
            held,
            held,
            split_rows,
            split_columns,
            rows,
            rows,
            rows,
            split_rows,
            rows,
            split_rows,
            split_rows,
            rows,
            split_rows,
            rows,
            rows,
            rows,
            split_rows,
            rows,
            split_rows,
            rows,
        ),
        check_vma=False,
    )
```

```python
import functools

import jax
import jax.numpy as jnp
import numpy as np
from jax import lax
from jax.experimental import pallas as pl
from jax.experimental.pallas import tpu as pltpu
from jax.sharding import PartitionSpec as P

HEADS = 12
BASE = 7
HIGH_ACCURACY = lax.Precision.HIGHEST
AXES = ("img", "strip")


def bilinear(out_count, in_count):
    source = (np.arange(out_count, dtype=np.float32) + 0.5) * (in_count / out_count) - 0.5
    source = np.clip(source, 0.0, in_count - 1.0)
    target = np.arange(in_count, dtype=np.float32)
    return np.maximum(1.0 - np.abs(source[:, None] - target[None, :]), 0.0).astype(np.float32)


def matmul(left, right):
    return jnp.dot(left, right, preferred_element_type=jnp.float32)


def left_trans(left, right):
    return lax.dot_general(
        left, right, (((0,), (0,)), ((), ())), preferred_element_type=jnp.float32
    )


def right_trans(left, right):
    return lax.dot_general(
        left, right, (((1,), (1,)), ((), ())), preferred_element_type=jnp.float32
    )


f32 = jnp.float32
bf16 = jnp.bfloat16
VMEM_LIMIT = 56 << 20


def params(*semantics):
    return pltpu.CompilerParams(
        dimension_semantics=semantics or None, vmem_limit_bytes=VMEM_LIMIT
    )


def shaped(shape, dtype):
    return jax.ShapeDtypeStruct(shape, dtype)


def cost(light=False):
    flops = 1024 if light else 1 << 32
    return pl.CostEstimate(flops=flops, bytes_accessed=1024, transcendentals=0)


def fill_mixer(mixer, table, size, turned):
    side = table.shape[0]
    span = side * side
    live = lax.broadcasted_iota(jnp.int32, table.shape, 0) < size
    table = jnp.where(live, table, 0.0)
    column = lax.broadcasted_iota(jnp.int32, (side, span), 1)
    row = lax.broadcasted_iota(jnp.int32, (side, span), 0)

    def widen(chosen):
        return lax.dot_general(
            table,
            chosen.astype(f32),
            (((0 if turned else 1,), (0,)), ((), ())),
            precision=HIGH_ACCURACY,
            preferred_element_type=f32,
        )

    wide = widen(column // side == row)
    tall = widen(column % side == row)
    for i in range(side):
        mixer[i * side : (i + 1) * side, :] = (wide[i : i + 1, :] * tall).astype(bf16)


def mix_kernel(sizes_ref, table_ref, pix_ref, out_ref, mixer):
    step = table_ref.shape[0] // sizes_ref[2]
    size = (sizes_ref[pl.program_id(0)] + 1) * step
    fill_mixer(mixer, table_ref[...], size, False)
    span = mixer.shape[0]
    for c in range(pix_ref.shape[-1] // span):
        columns = slice(c * span, (c + 1) * span)
        out_ref[:, columns] = matmul(pix_ref[:, columns], mixer[...]).astype(bf16)


def mix(sizes, resize, pixels):
    group, rows, length = pixels.shape
    side = resize.shape[1]
    span = side * side
    block = pl.BlockSpec((None, rows, length), lambda g, p: (g, 0, 0))
    return pl.pallas_call(
        mix_kernel,
        grid_spec=pltpu.PrefetchScalarGridSpec(
            num_scalar_prefetch=1,
            grid=(group,),
            in_specs=[pl.BlockSpec((None, side, side), lambda g, p: (p[g], 0, 0)), block],
            out_specs=block,
            scratch_shapes=[pltpu.VMEM((span, span), bf16)],
        ),
        out_shape=shaped(pixels.shape, bf16),
        compiler_params=params("arbitrary"),
        cost_estimate=cost(),
        name="mix",
    )(sizes, resize, pixels)


def unmix_kernel(sizes_ref, table_ref, left_ref, right_ref, grad_ref, out_ref, mixer):
    group = grad_ref.shape[0]

    @pl.when(pl.program_id(0) == 0)
    def _():
        step = table_ref.shape[1] // table_ref.shape[0]
        for g in range(group):
            index = sizes_ref[g]
            fill_mixer(mixer.at[g], table_ref[index], (index + 1) * step, True)

    half = left_ref.shape[1]
    for g in range(group):
        grad = grad_ref[g]
        g_base = (
            right_trans(grad[:, :half], left_ref[...]) + right_trans(grad[:, half:], right_ref[...])
        ).astype(bf16)
        out_ref[g] = matmul(g_base, mixer[g])


def unmix(sizes, resize, left, right, grad):
    group, rows, width = grad.shape
    side = resize.shape[1]
    span = side * side
    length, columns = left.shape
    return pl.pallas_call(
        unmix_kernel,
        grid_spec=pltpu.PrefetchScalarGridSpec(
            num_scalar_prefetch=1,
            grid=(length // span,),
            in_specs=[
                pl.BlockSpec(resize.shape, lambda c, p: (0, 0, 0)),
                pl.BlockSpec((span, columns), lambda c, p: (c, 0)),
                pl.BlockSpec((span, columns), lambda c, p: (c, 0)),
                pl.BlockSpec((group, rows, width), lambda c, p: (0, 0, 0)),
            ],
            out_specs=pl.BlockSpec((group, rows, span), lambda c, p: (0, 0, c)),
            scratch_shapes=[pltpu.VMEM((group, span, span), bf16)],
        ),
        out_shape=shaped((group, rows, length), f32),
        compiler_params=params("arbitrary"),
        cost_estimate=cost(),
        name="unmix",
    )(sizes, resize, left, right, grad)


def attend_kernel(q_ref, ko_ref, kp_ref, vo_ref, vp_ref, out_ref, lse_ref, *, size, chunk):
    first = lax.broadcasted_iota(jnp.int32, (1, 2 * size), 1) < size
    keys = jnp.concatenate([ko_ref[...], kp_ref[...]], axis=0)
    values = jnp.concatenate([vo_ref[...], vp_ref[...]], axis=0)
    for i in range(q_ref.shape[0] // chunk):
        rows = slice(i * chunk, (i + 1) * chunk)
        query = q_ref[rows, :]
        none = jnp.zeros_like(query)
        outs, sums = [], []
        for e in range(2):
            head = jnp.where(first, query, none) if e == 0 else jnp.where(first, none, query)
            scores = right_trans(head, keys)
            peak = jnp.max(scores, axis=-1, keepdims=True)
            expd = jnp.exp(scores - peak)
            denom = jnp.sum(expd, axis=-1, keepdims=True)
            outs.append(matmul(expd.astype(bf16), values) / denom)
            sums.append(peak + jnp.log(denom))
        out_ref[rows, :] = jnp.where(first, outs[0], outs[1]).astype(bf16)
        lse_ref[rows, :] = jnp.where(first, sums[0], sums[1])


def attend(query, key, key_peer, value, value_peer):
    rows, width = query.shape
    size = width // HEADS
    spec = pl.BlockSpec((rows, 2 * size), lambda h: (0, h))
    return pl.pallas_call(
        functools.partial(attend_kernel, size=size, chunk=min(256, rows)),
        grid=(HEADS // 2,),
        in_specs=[spec] * 5,
        out_specs=[spec] * 2,
        out_shape=[shaped((rows, width), bf16), shaped((rows, width), f32)],
        compiler_params=params("arbitrary"),
        cost_estimate=cost(),
        name="attend",
    )(query, key, key_peer, value, value_peer)


def attend_back_kernel(
    q_ref,
    ko_ref,
    kp_ref,
    vo_ref,
    vp_ref,
    g_ref,
    o_ref,
    lse_ref,
    gq_ref,
    gko_ref,
    gkp_ref,
    gvo_ref,
    gvp_ref,
    *,
    size,
    chunk,
):
    rows = q_ref.shape[0]
    upper = lax.broadcasted_iota(jnp.int32, (2 * size, 1), 0) < size
    first = lax.broadcasted_iota(jnp.int32, (1, 2 * size), 1) < size
    query = q_ref[...]
    grad = g_ref[...]
    query_t = query.astype(f32).T
    grad_t = grad.astype(f32).T
    inner_t = grad_t * o_ref[...].astype(f32).T
    lse_t = lse_ref[...].T
    queries, grads, inners, sums, g_query = [], [], [], [], []
    for e in range(2):
        mine = upper if e == 0 else jnp.logical_not(upper)
        queries.append(jnp.where(mine, query_t, 0.0).astype(bf16))
        grads.append(jnp.where(mine, grad_t, 0.0).astype(bf16))
        inners.append(jnp.sum(inner_t[e * size : (e + 1) * size], axis=0, keepdims=True))
        sums.append(lse_t[e * size : e * size + 1])
        g_query.append(jnp.zeros((size, rows), f32))
    for k_ref, v_ref, gk_ref, gv_ref in (
        (ko_ref, vo_ref, gko_ref, gvo_ref),
        (kp_ref, vp_ref, gkp_ref, gvp_ref),
    ):
        for i in range(k_ref.shape[0] // chunk):
            part = slice(i * chunk, (i + 1) * chunk)
            key = k_ref[part, :]
            value = v_ref[part, :]
            key_t = key.astype(f32).T.astype(bf16)
            g_key, g_value = [], []
            for e in range(2):
                probs = jnp.exp(matmul(key, queries[e]) - sums[e])
                g_scores = (probs * (matmul(value, grads[e]) - inners[e])).astype(bf16)
                g_key.append(matmul(g_scores, query))
                g_value.append(matmul(probs.astype(bf16), grad))
                g_query[e] = g_query[e] + matmul(key_t[e * size : (e + 1) * size], g_scores)
            gk_ref[part, :] = jnp.where(first, g_key[0], g_key[1]).astype(gk_ref.dtype)
            gv_ref[part, :] = jnp.where(first, g_value[0], g_value[1]).astype(gv_ref.dtype)
    gq_ref[...] = jnp.concatenate(g_query, axis=0).T.astype(gq_ref.dtype)


def attend_back(query, key, key_peer, value, value_peer, grad, attended, lse):
    rows, width = query.shape
    size = width // HEADS
    spec = pl.BlockSpec((rows, 2 * size), lambda h: (0, h))
    low, full = shaped((rows, width), bf16), shaped((rows, width), f32)
    return pl.pallas_call(
        functools.partial(attend_back_kernel, size=size, chunk=rows),
        grid=(HEADS // 2,),
        in_specs=[spec] * 8,
        out_specs=[spec] * 5,
        out_shape=[low, full, low, full, low],
        compiler_params=params("arbitrary"),
        cost_estimate=cost(),
        name="attend_back",
    )(query, key, key_peer, value, value_peer, grad, attended, lse)


def whole(shape):
    return pl.BlockSpec(shape, lambda i, s: (0,) * len(shape))


def gather_rows_kernel(at_ref, own_ref, peer_ref, out_ref, rows_ref):
    core = at_ref[0]
    strips, part = own_ref.shape[:2]
    half = out_ref.shape[0]
    for j in range(strips):
        start, count = at_ref[1 + j], at_ref[1 + strips + j]
        for ref, which in ((own_ref, core), (peer_ref, 1 - core)):
            for i in range(part):
                local = which * part + i
                row = start + local - core * half
                here = jnp.logical_and(local < count, jnp.logical_and(row >= 0, row < half))
                rows_ref[jnp.where(here, row, half)] = ref[j, i]
    out_ref[...] = rows_ref[:half]


def gather_rows(at, own, peer, half):
    strips, part, grid, width = own.shape
    out = (half, grid, width)
    return pl.pallas_call(
        gather_rows_kernel,
        grid_spec=pltpu.PrefetchScalarGridSpec(
            num_scalar_prefetch=1,
            grid=(1,),
            in_specs=[whole(own.shape)] * 2,
            out_specs=whole(out),
            scratch_shapes=[pltpu.VMEM((half + 1, grid, width), bf16)],
        ),
        out_shape=shaped(out, bf16),
        compiler_params=params("arbitrary"),
        cost_estimate=cost(),
        name="gather_rows",
    )(at, own, peer)


def spread_rows_kernel(at_ref, own_ref, peer_ref, out_ref, rows_ref):
    core = at_ref[0]
    strips, part = out_ref.shape[:2]
    half = own_ref.shape[0]
    rows_ref[pl.ds(core * half, half)] = own_ref[...]
    rows_ref[pl.ds((1 - core) * half, half)] = peer_ref[...]
    rows_ref[2 * half] = jnp.zeros(rows_ref.shape[1:], bf16)
    for j in range(strips):
        start, count = at_ref[1 + j], at_ref[1 + strips + j]
        for i in range(part):
            local = core * part + i
            out_ref[j, i] = rows_ref[jnp.where(local < count, start + local, 2 * half)]


def spread_rows(at, own, peer, strips, capacity):
    half, grid, width = own.shape
    out = (strips, capacity // 2, grid, width)
    return pl.pallas_call(
        spread_rows_kernel,
        grid_spec=pltpu.PrefetchScalarGridSpec(
            num_scalar_prefetch=1,
            grid=(1,),
            in_specs=[whole(own.shape)] * 2,
            out_specs=whole(out),
            scratch_shapes=[pltpu.VMEM((2 * half + 1, grid, width), bf16)],
        ),
        out_shape=shaped(out, bf16),
        compiler_params=params("arbitrary"),
        cost_estimate=cost(),
        name="spread_rows",
    )(at, own, peer)


def normalise(values):
    centred = values - jnp.mean(values, axis=-1, keepdims=True)
    scale = lax.rsqrt(jnp.mean(centred * centred, axis=-1, keepdims=True) + 1e-06)
    return centred * scale, scale


def norm_back(grad, normed, scale):
    return scale * (
        grad
        - jnp.mean(grad, axis=-1, keepdims=True)
        - normed * jnp.mean(grad * normed, axis=-1, keepdims=True)
    )


def column_sum(values):
    return jnp.sum(values, axis=0, keepdims=True)


PATCH, GAIN1, SHIFT1, QUERY, VALUE, OUT, GAIN2, SHIFT2, DOWN = range(9)
VECTORS = 9
UP_AT = 9
POS_AT = 16
TABLE = 96
POS_ROWS = 64


def patch_kernel(base_ref, left_ref, right_ref, out_ref):
    half = left_ref.shape[1]
    out_ref[:, :half] = matmul(base_ref[...], left_ref[...]).astype(bf16)
    out_ref[:, half:] = matmul(base_ref[...], right_ref[...]).astype(bf16)


def embed_patches(base, left, right):
    group, rows, length = base.shape
    half = left.shape[1]
    return pl.pallas_call(
        patch_kernel,
        grid=(group,),
        in_specs=[
            pl.BlockSpec((None, rows, length), lambda t: (t, 0, 0)),
            pl.BlockSpec((length, half), lambda t: (0, 0)),
            pl.BlockSpec((length, half), lambda t: (0, 0)),
        ],
        out_specs=pl.BlockSpec((None, rows, 2 * half), lambda t: (t, 0, 0)),
        out_shape=shaped((group, rows, 2 * half), bf16),
        compiler_params=params("arbitrary"),
        cost_estimate=cost(),
        name="embed_patches",
    )(base, left, right)


def enter_kernel(
    at_ref, patches_ref, spread_ref, table_ref, ql_ref, qr_ref, kl_ref, kr_ref, vl_ref, vr_ref,
    embed_ref, in_ref, q_ref, k_ref, v_ref,
):
    def vector(row):
        return table_ref[row : row + 1, :]

    place_rows = jnp.dot(
        spread_ref[...],
        table_ref[POS_AT : POS_AT + POS_ROWS, :],
        precision=HIGH_ACCURACY,
        preferred_element_type=f32,
    )
    embed = patches_ref[...].astype(f32) + vector(PATCH) + place_rows
    embed_ref[...] = embed
    normed, _ = normalise(embed)
    attn_in = (normed * vector(GAIN1) + vector(SHIFT1)).astype(bf16)
    in_ref[...] = attn_in
    half = ql_ref.shape[1]
    for ref, weights, bias, scale in (
        (q_ref, (ql_ref, qr_ref), vector(QUERY), 0.125),
        (k_ref, (kl_ref, kr_ref), None, None),
        (v_ref, (vl_ref, vr_ref), vector(VALUE), None),
    ):
        for columns, weight in zip((slice(0, half), slice(half, 2 * half)), weights):
            rows = matmul(attn_in, weight[...])
            if bias is not None:
                rows = rows + bias[:, columns]
            if scale is not None:
                rows = rows * scale
            ref[:, columns] = rows.astype(bf16)


def enter(at, patches, spread, table, weights, blocks=2):
    rows, width = patches.shape
    block = rows // blocks
    part = pl.BlockSpec((block, width), lambda t, a: (t, 0))
    weight = pl.BlockSpec(weights[0].shape, lambda t, a: (0, 0))
    low = shaped((rows, width), bf16)
    return pl.pallas_call(
        enter_kernel,
        grid_spec=pltpu.PrefetchScalarGridSpec(
            num_scalar_prefetch=1,
            grid=(blocks,),
            in_specs=[
                part,
                pl.BlockSpec((None, block, POS_ROWS), lambda t, a: (a[0], t, 0)),
                pl.BlockSpec(table.shape, lambda t, a: (0, 0)),
                *([weight] * 6),
            ],
            out_specs=[part] * 5,
        ),
        out_shape=[shaped((rows, width), f32), low, low, low, low],
        compiler_params=params("arbitrary"),
        cost_estimate=cost(),
        name="enter",
    )(at, patches, spread, table, *weights)


def mlp_kernel(
    attended_ref, embed_ref, table_ref, ol_ref, or_ref, up_ref, bias_ref, down_ref,
    resid_ref, in_ref, hidden_ref, slope_ref, out_ref, total,
):
    step = pl.program_id(0)

    def vector(row):
        return table_ref[row : row + 1, :]

    @pl.when(step == 0)
    def _():
        half = ol_ref.shape[1]
        for columns, weight in ((slice(0, half), ol_ref), (slice(half, 2 * half), or_ref)):
            resid_ref[:, columns] = (
                embed_ref[:, columns]
                + matmul(attended_ref[...], weight[...])
                + vector(OUT)[:, columns]
            )
        resid = resid_ref[...]
        normed, _ = normalise(resid)
        in_ref[...] = (normed * vector(GAIN2) + vector(SHIFT2)).astype(bf16)
        total[...] = resid + vector(DOWN)

    upper = matmul(in_ref[...], up_ref[...]) + bias_ref[...]
    below = 0.5 + 0.5 * lax.erf(upper * 0.7071067811865476)
    hidden = (upper * below).astype(bf16)
    hidden_ref[...] = hidden
    slope_ref[...] = (below + upper * (0.3989422804014327 * jnp.exp(-0.5 * upper * upper))).astype(
        slope_ref.dtype
    )
    total[...] += matmul(hidden, down_ref[...])

    @pl.when(step == pl.num_programs(0) - 1)
    def _():
        out_ref[...] = total[...].astype(bf16)


def mlp(attended, embed, table, w_out, w_up, b_up, w_down):
    rows, width = embed.shape
    blocks = w_up.shape[0]
    ff = blocks * width
    fixed = pl.BlockSpec((rows, width), lambda t: (0, 0))
    columns = pl.BlockSpec((rows, width), lambda t: (0, t))
    return pl.pallas_call(
        mlp_kernel,
        grid=(blocks,),
        in_specs=[
            fixed,
            fixed,
            pl.BlockSpec(table.shape, lambda t: (0, 0)),
            *([pl.BlockSpec(w_out[0].shape, lambda t: (0, 0))] * 2),
            pl.BlockSpec((None, width, width), lambda t: (t, 0, 0)),
            pl.BlockSpec((1, width), lambda t: (0, t)),
            pl.BlockSpec((width, width), lambda t: (t, 0)),
        ],
        out_specs=[fixed, fixed, columns, columns, fixed],
        out_shape=[
            shaped((rows, width), f32),
            shaped((rows, width), bf16),
            shaped((rows, ff), bf16),
            shaped((rows, ff), f32),
            shaped((rows, width), bf16),
        ],
        scratch_shapes=[pltpu.VMEM((rows, width), f32)],
        compiler_params=params("arbitrary"),
        cost_estimate=cost(),
        name="mlp",
    )(attended, embed, table, *w_out, w_up, b_up, w_down)


def mlp_back_kernel(
    g_ref, slope_ref, resid_ref, table_ref, ol_ref, or_ref, up_ref, down_ref,
    upper_ref, resid_grad_ref, low_ref, att_ref, sums_ref, total,
):
    step = pl.program_id(0)

    @pl.when(step == 0)
    def _():
        total[...] = jnp.zeros_like(total)
        sums_ref[...] = jnp.zeros_like(sums_ref)

    g_upper = slope_ref[...].astype(f32) * right_trans(g_ref[...], down_ref[...])
    sums_ref[pl.ds(8 + step, 1), :] = column_sum(g_upper)
    g_upper_low = g_upper.astype(bf16)
    upper_ref[...] = g_upper_low
    total[...] += right_trans(g_upper_low, up_ref[...])

    @pl.when(step == pl.num_programs(0) - 1)
    def _():
        grad = total[...]
        g_out = g_ref[...].astype(f32)
        normed, scale = normalise(resid_ref[...])
        g_resid = g_out + norm_back(grad * table_ref[GAIN2 : GAIN2 + 1, :], normed, scale)
        resid_grad_ref[...] = g_resid
        g_resid_low = g_resid.astype(bf16)
        low_ref[...] = g_resid_low
        half = ol_ref.shape[1]
        att_ref[...] = (
            right_trans(g_resid_low[:, :half], ol_ref[...])
            + right_trans(g_resid_low[:, half:], or_ref[...])
        ).astype(bf16)
        sums_ref[0:1, :] = column_sum(g_resid)
        sums_ref[1:2, :] = column_sum(grad * normed)
        sums_ref[2:3, :] = column_sum(grad)
        sums_ref[3:4, :] = column_sum(g_out)


def mlp_back(g_out, slope, resid, table, w_out, w_up, w_down):
    rows, width = g_out.shape
    blocks = w_up.shape[0]
    ff = blocks * width
    fixed = pl.BlockSpec((rows, width), lambda t: (0, 0))
    columns = pl.BlockSpec((rows, width), lambda t: (0, t))
    sums = (8 + 8 * (-(-blocks // 8)), width)
    return pl.pallas_call(
        mlp_back_kernel,
        grid=(blocks,),
        in_specs=[
            fixed,
            columns,
            fixed,
            pl.BlockSpec(table.shape, lambda t: (0, 0)),
            *([pl.BlockSpec(w_out[0].shape, lambda t: (0, 0))] * 2),
            pl.BlockSpec((None, width, width), lambda t: (t, 0, 0)),
            pl.BlockSpec((width, width), lambda t: (t, 0)),
        ],
        out_specs=[columns, fixed, fixed, fixed, pl.BlockSpec(sums, lambda t: (0, 0))],
        out_shape=[
            shaped((rows, ff), bf16),
            shaped((rows, width), f32),
            shaped((rows, width), bf16),
            shaped((rows, width), bf16),
            shaped(sums, f32),
        ],
        scratch_shapes=[pltpu.VMEM((rows, width), f32)],
        compiler_params=params("arbitrary"),
        cost_estimate=cost(),
        name="mlp_back",
    )(g_out, slope, resid, table, *w_out, w_up, w_down)


def leave_kernel(
    at_ref, gq_ref, gk_ref, gkp_ref, gv_ref, gvp_ref, embed_ref, resid_ref, spread_ref, table_ref,
    ql_ref, qr_ref, kl_ref, kr_ref, vl_ref, vr_ref, q_ref, k_ref, v_ref, out_ref, sums_ref, pos_ref,
):
    @pl.when(pl.program_id(0) == 0)
    def _():
        sums_ref[...] = jnp.zeros_like(sums_ref)
        pos_ref[...] = jnp.zeros_like(pos_ref)

    g_query = gq_ref[...].astype(f32) * 0.125
    g_query_low = g_query.astype(bf16)
    g_key_low = (gk_ref[...] + gkp_ref[...].astype(f32)).astype(bf16)
    g_value_low = (gv_ref[...] + gvp_ref[...].astype(f32)).astype(bf16)
    q_ref[...] = g_query_low
    k_ref[...] = g_key_low
    v_ref[...] = g_value_low
    half = ql_ref.shape[1]
    grad = jnp.zeros(embed_ref.shape, f32)
    for low, weights in (
        (g_query_low, (ql_ref, qr_ref)),
        (g_key_low, (kl_ref, kr_ref)),
        (g_value_low, (vl_ref, vr_ref)),
    ):
        grad = grad + right_trans(low[:, :half], weights[0][...])
        grad = grad + right_trans(low[:, half:], weights[1][...])
    normed, scale = normalise(embed_ref[...])
    g_embed = resid_ref[...] + norm_back(grad * table_ref[GAIN1 : GAIN1 + 1, :], normed, scale)
    out_ref[...] = g_embed.astype(bf16)
    sums_ref[0:1, :] += column_sum(g_embed)
    sums_ref[1:2, :] += column_sum(grad * normed)
    sums_ref[2:3, :] += column_sum(grad)
    sums_ref[3:4, :] += column_sum(g_query)
    sums_ref[4:5, :] += column_sum(g_value_low.astype(f32))
    pos_ref[...] += jnp.dot(
        spread_ref[...], g_embed, precision=HIGH_ACCURACY, preferred_element_type=f32
    )


def leave(
    at, g_query, g_key, g_key_peer, g_value, g_value_peer, embed, g_resid, spread, table,
    weights, blocks=2,
):
    rows, width = embed.shape
    block = rows // blocks
    part = pl.BlockSpec((block, width), lambda t, a: (t, 0))
    weight = pl.BlockSpec(weights[0].shape, lambda t, a: (0, 0))
    low = shaped((rows, width), bf16)
    return pl.pallas_call(
        leave_kernel,
        grid_spec=pltpu.PrefetchScalarGridSpec(
            num_scalar_prefetch=1,
            grid=(blocks,),
            in_specs=[part] * 7
            + [
                pl.BlockSpec((None, POS_ROWS, block), lambda t, a: (a[0], 0, t)),
                pl.BlockSpec(table.shape, lambda t, a: (0, 0)),
                *([weight] * 6),
            ],
            out_specs=[part] * 4
            + [
                pl.BlockSpec((8, width), lambda t, a: (0, 0)),
                pl.BlockSpec((POS_ROWS, width), lambda t, a: (0, 0)),
            ],
        ),
        out_shape=[low] * 4 + [shaped((8, width), f32), shaped((POS_ROWS, width), f32)],
        compiler_params=params("arbitrary"),
        cost_estimate=cost(),
        name="leave",
    )(
        at, g_query, g_key, g_key_peer, g_value, g_value_peer, embed, g_resid, spread, table,
        *weights,
    )


def weight_grad_kernel(at_ref, left_ref, right_ref, send_ref, keep_ref, total):
    core = at_ref[0]
    group, rows, _ = send_ref.shape
    total[...] = left_trans(left_ref[...], right_ref[...])
    for h in range(group):
        sent = pl.multiple_of((2 * h + 1 - core) * rows, 8)
        kept = pl.multiple_of((2 * h + core) * rows, 8)
        send_ref[h] = total[pl.ds(sent, rows), :].astype(bf16)
        keep_ref[h] = total[pl.ds(kept, rows), :]


def weight_grad(at, left, right, his, light=False):
    tokens, m = left.shape
    n = right.shape[1]
    rows = m // (2 * his)
    tall = min(m, 768)
    h = tall // (2 * rows)
    wide = 768
    blocks = n // wide
    out = pl.BlockSpec((h, None, rows, wide), lambda i, j, a: (i, j, 0, 0))
    shape = (his, blocks, rows, wide)
    return pl.pallas_call(
        weight_grad_kernel,
        grid_spec=pltpu.PrefetchScalarGridSpec(
            num_scalar_prefetch=1,
            grid=(m // tall, blocks),
            in_specs=[
                pl.BlockSpec((tokens, tall), lambda i, j, a: (0, i)),
                pl.BlockSpec((tokens, wide), lambda i, j, a: (0, j)),
            ],
            out_specs=[out, out],
            scratch_shapes=[pltpu.VMEM((tall, wide), f32)],
        ),
        out_shape=[shaped(shape, bf16), shaped(shape, f32)],
        compiler_params=params("arbitrary", "arbitrary"),
        cost_estimate=cost(light),
        name="weight_grad",
    )(at, left, right)


def proj_grad_kernel(
    at_ref, in_ref, att_ref, gq_ref, gk_ref, gv_ref, go_ref, send_ref, keep_ref, total
):
    core = at_ref[0]
    his, _, rows, _ = send_ref.shape
    pairs = ((in_ref, gq_ref), (in_ref, gk_ref), (in_ref, gv_ref), (att_ref, go_ref))
    for i, (left, right) in enumerate(pairs):
        total[...] = left_trans(left[...], right[...])
        for h in range(his):
            sent = pl.multiple_of((2 * h + 1 - core) * rows, 8)
            kept = pl.multiple_of((2 * h + core) * rows, 8)
            send_ref[h, i] = total[pl.ds(sent, rows), :].astype(bf16)
            keep_ref[h, i] = total[pl.ds(kept, rows), :]


def proj_grad(at, attn_in, attended, g_query, g_key, g_value, g_resid, his):
    tokens, width = attn_in.shape
    rows = width // (2 * his)
    out = (his, 4, rows, width)
    return pl.pallas_call(
        proj_grad_kernel,
        grid_spec=pltpu.PrefetchScalarGridSpec(
            num_scalar_prefetch=1,
            grid=(1,),
            in_specs=[whole(attn_in.shape)] * 6,
            out_specs=[whole(out)] * 2,
            scratch_shapes=[pltpu.VMEM((width, width), f32)],
        ),
        out_shape=[shaped(out, bf16), shaped(out, f32)],
        compiler_params=params("arbitrary"),
        cost_estimate=cost(),
        name="proj_grad",
    )(at, attn_in, attended, g_query, g_key, g_value, g_resid)


class Place:
    def __init__(self, group):
        self.group = group
        self.images = lax.axis_size("img")
        self.strips = lax.axis_size("strip")
        assert group == 2 and self.strips == 4
        self.img = lax.axis_index("img")
        self.core = self.img % 2
        self.z = lax.axis_index("strip")
        self.bits = [1 << k for k in range(1, self.images.bit_length() - 1)]
        assert self.images == 2 << len(self.bits)

    def flat(self, img, z):
        return img * self.strips + z

    def swap_core(self, values):
        return lax.ppermute(values, "img", [(i, i ^ 1) for i in range(self.images)])

    def across_img(self, values, bit):
        return lax.ppermute(values, "img", [(i, i ^ bit) for i in range(self.images)])

    def along_z(self, values, r):
        return lax.ppermute(values, "strip", [(z, z ^ r) for z in range(self.strips)])


def pick(values, index, axis=0):
    return lax.dynamic_index_in_dim(values, index, axis, keepdims=False)


def after(values, *others):
    return lax.optimization_barrier((values,) + others)[0]


def collect(values, *others):
    values = tuple(values)
    return lax.optimization_barrier(values + others)[: len(values)]


def exchange(values):
    return lax.all_to_all(values, "strip", 0, 0, tiled=True)


class Gather:
    def __init__(self, place, held, bits=()):
        self.place = place
        self.held = held
        self.bits = list(bits)

    def halves(self):
        middle = self.held.shape[-1] // 2
        return [
            Gather(self.place, self.held[..., columns], self.bits)
            for columns in (slice(0, middle), slice(middle, None))
        ]

    def along_z(self, *others):
        if others:
            self.held = after(self.held, *others)
        self.held = exchange(jnp.broadcast_to(self.held, (self.place.strips,) + self.held.shape))

    def z_done(self, *others):
        (self.held,) = collect([self.held], *others)

    def over(self, bit, *others):
        if others:
            self.held = after(self.held, *others)
        self.bit = bit
        self.got = self.place.across_img(self.held, bit)

    def done(self, *others):
        (got,) = collect([self.got], *others)
        self.bits = sorted(self.bits + [self.bit], reverse=True)
        axis = self.bits.index(self.bit)
        self.held = join(self.held, got, axis, (self.place.img // self.bit) % 2)

    def last(self, *others):
        if others:
            self.held = after(self.held, *others)
        self.other = self.place.swap_core(self.held)

    def last_done(self, *others):
        (self.other,) = collect([self.other], *others)

    def rows(self, start=0, stop=None):
        axis = len(self.bits)
        full = join(self.held[..., start:stop, :], self.other[..., start:stop, :], axis, self.place.core)
        return full.reshape((-1,) + full.shape[-2:])


def join(mine, other, axis, at):
    spot = [1] * (mine.ndim + 1)
    spot[axis] = 2
    where = jnp.arange(2, dtype=jnp.int32).reshape(spot) == at
    return jnp.where(where, jnp.expand_dims(mine, axis), jnp.expand_dims(other, axis))


class Scatter:
    def __init__(self, place, send, keep):
        self.place = place
        self.bits = place.bits[::-1]
        self.send = send
        self.keep = keep

    def first(self):
        self.got = self.place.swap_core(self.send)

    def first_done(self, *others):
        (got,) = collect([self.got], *others)
        shape = (2,) * len(self.bits) + self.send.shape[1:]
        self.part = self.keep.reshape(shape) + got.reshape(shape).astype(f32)

    def halves(self, axis=None):
        axis = len(self.bits) if axis is None else axis % self.part.ndim
        parts = []
        middle = self.part.shape[axis] // 2
        for start, stop in ((0, middle), (middle, self.part.shape[axis])):
            one = Scatter(self.place, None, None)
            one.part = lax.slice_in_dim(self.part, start, stop, axis=axis)
            parts.append(one)
        return parts

    def over(self, bit):
        self.bit = bit
        axis = self.bits.index(bit)
        self.sent = pick(self.part, 1 - (self.place.img // bit) % 2, axis).astype(bf16)
        self.got = self.place.across_img(self.sent, bit)

    def done(self, *others):
        (got,) = collect([self.got], *others)
        axis = self.bits.index(self.bit)
        self.part = pick(self.part, (self.place.img // self.bit) % 2, axis) + got.astype(f32)
        self.bits = [b for b in self.bits if b != self.bit]

    def by_strip(self):
        blocks, rows, columns = self.part.shape
        part = self.part.reshape(blocks, self.place.strips, -1, columns)
        return part.transpose(1, 0, 2, 3).reshape(self.place.strips, -1, columns)


class Last:
    def __init__(self, values):
        self.sent = values.astype(bf16)
        self.got = exchange(self.sent)

    def done(self, *others):
        (got,) = collect([self.got], *others)
        return jnp.sum(got.astype(f32), axis=0)


def split_rows(place, values):
    images, rows = values.shape[:2]
    values = values.reshape((images, 2, rows // 2) + values.shape[2:])
    return pick(values, place.core, 1), pick(values, 1 - place.core, 1)


def pair_up(place, mine, other):
    return jnp.where(
        place.core == 0, jnp.concatenate([mine, other]), jnp.concatenate([other, mine])
    )


def from_chip(place, moved, shape):
    images, rows = shape[0], shape[1] // 2
    moved = moved.reshape((2, images) + moved.shape[1:])
    mine, sent = pick(moved, place.core), pick(moved, 1 - place.core)
    got = place.swap_core(sent)
    low = jnp.where(place.core == 0, mine, got)
    high = jnp.where(place.core == 0, got, mine)
    return jnp.concatenate([low, high], axis=1)


def body(
    pixels,
    cotangent,
    resize,
    patch_index,
    slot_image,
    strip_rows,
    patch_weight,
    pos_grid,
    patch_bias,
    attention_norm_gain,
    attn_shift,
    query_weight,
    query_bias,
    key_weight,
    value_weight,
    value_bias,
    out_weight,
    out_bias,
    mlp_gain,
    mlp_shift,
    up_weight,
    up_bias,
    down_weight,
    down_bias,
):
    group, capacity, grid, pixel_len = pixels.shape
    width = cotangent.shape[3]
    ff = up_weight.shape[1]
    local_rows = capacity * grid
    tokens = group * local_rows
    place = Place(group)
    devices = place.images * place.strips
    his = place.images // 2
    first_slot = place.img * group
    shard = patch_bias.shape[0]
    ups = up_bias.shape[0]
    columns = width // 2
    bits = place.bits

    vectors = (
        patch_bias,
        attention_norm_gain,
        attn_shift,
        query_bias,
        value_bias,
        out_bias,
        mlp_gain,
        mlp_shift,
        down_bias,
    )
    pieces = ups // shard
    small = jnp.concatenate(
        [
            jnp.stack(vectors + tuple(up_bias[i * shard : (i + 1) * shard] for i in range(pieces))),
            jnp.zeros((POS_AT - VECTORS - pieces, shard), bf16),
            pos_grid,
            jnp.zeros((TABLE - POS_AT - BASE * BASE, shard), bf16),
        ]
    )
    lane = width // (TABLE // 16)
    small = jnp.pad(small, ((0, 0), (0, lane - shard))).reshape(-1, 16, lane)
    small = jnp.concatenate(list(small), axis=1)
    proj = jnp.concatenate([query_weight, key_weight, value_weight, out_weight, small])

    size_count = resize.shape[0]
    slot_ids = lax.dynamic_slice_in_dim(slot_image, first_slot, group)
    picked = slot_ids[:, None] == jnp.arange(patch_index.shape[0], dtype=jnp.int32)[None, :]
    size_index = jnp.sum(jnp.where(picked, patch_index[None, :], 0), axis=1)
    sizes = jnp.append(size_index, size_count).astype(jnp.int32)
    half = grid // 2
    image_counts = pick(strip_rows, (place.img // 2) * 2 * group + place.z)
    starts = jnp.cumsum(image_counts) - image_counts
    at = jnp.concatenate([place.core[None], starts, image_counts]).astype(jnp.int32)

    spread = bilinear(grid, BASE)
    spread = (spread[:, None, :, None] * spread[None, :, None, :]).reshape(2, half * grid, -1)
    spread = np.pad(spread, ((0, 0), (0, 0), (0, POS_ROWS - BASE * BASE)))
    spread_t = jnp.asarray(np.ascontiguousarray(spread.transpose(0, 2, 1)))
    spread = jnp.asarray(spread)

    whole_patch, packed = Gather(place, patch_weight), Gather(place, proj)
    blocks = ff // width
    both = Gather(
        place,
        jnp.concatenate(
            [down_weight]
            + [up_weight[:, i * width : (i + 1) * width] for i in range(blocks)]
        ),
    )
    whole_patch.along_z()
    base_pixels = mix(sizes, resize, pixels.reshape(group, local_rows, pixel_len))
    whole_patch.z_done(base_pixels)
    left, right = whole_patch.halves()
    for k in range(len(bits)):
        if k == len(bits) - 1:
            packed.along_z(left.held, right.held)
        left.over(bits[k])
        right.over(bits[-1 - k])
        left.done()
        right.done()
    packed.z_done()
    left.last(packed.held, right.held)
    right.last(packed.held, left.held)
    left.last_done()
    right.last_done()
    w_left, w_right = left.rows().reshape(-1, columns), right.rows().reshape(-1, columns)
    packs = packed.halves()
    packs[0].over(bits[0], left.other)
    packs[1].over(bits[-1], left.other)
    both.along_z(left.other, right.other)
    patches = embed_patches(base_pixels, w_left, w_right).reshape(group, capacity, grid, width)
    packs[0].done()
    packs[1].done()
    for k in range(1, len(bits)):
        packs[0].over(bits[k])
        packs[1].over(bits[-1 - k])
        packs[0].done(patches)
        packs[1].done(patches)
    both.z_done(patches)
    downs_w = Gather(place, both.held[:, : down_weight.shape[0]], both.bits)
    ups_w = Gather(place, both.held[:, down_weight.shape[0] :], both.bits)
    patch_mine, patch_sent = split_rows(place, patches)
    patch_got = place.swap_core(after(patch_sent, packs[0].held, packs[1].held))
    patch_moved = exchange(pair_up(place, patch_mine, patch_got))
    packs[0].last(patch_got)
    packs[1].last(patch_got)
    ups_w.over(bits[-1], patch_got)
    downs_w.over(bits[0], patch_got)
    for k in range(1, len(bits) - 1):
        ups_w.done()
        downs_w.done()
        ups_w.over(bits[-1 - k])
        downs_w.over(bits[k])
    cot_mine, cot_sent = split_rows(place, cotangent)
    cot_got = place.swap_core(after(cot_sent, patch_got))
    cot_pair = pair_up(place, cot_mine, cot_got)

    halves = [
        [p.rows(i * shard, (i + 1) * shard).reshape(width, columns) for p in packs]
        for i in range(4)
    ]
    in_weights = [*halves[0], *halves[1], *halves[2]]
    w_out = halves[3]
    flat = jnp.concatenate([p.rows(4 * shard) for p in packs], axis=-1)
    table = (
        flat.reshape(devices, 16, TABLE // 16, lane)[..., :shard]
        .transpose(2, 1, 0, 3)
        .reshape(TABLE, width)
        .astype(f32)
    )
    b_up = (
        table[UP_AT : UP_AT + pieces]
        .reshape(pieces, devices, shard)
        .transpose(1, 0, 2)
        .reshape(1, ff)
    )
    (patch_moved,) = collect([patch_moved], table, b_up, cot_pair, *in_weights, *w_out)
    ups_w.done(patch_moved)
    downs_w.done(patch_moved)
    patch_peer = place.swap_core(patch_moved)
    patches = gather_rows(at, patch_moved, patch_peer, half).reshape(-1, width)
    if len(bits) > 1:
        ups_w.over(bits[0], patch_moved)
        downs_w.over(bits[-1], patch_moved)
    cot_moved = exchange(after(cot_pair, patch_moved))

    embed, attn_in, query, key, value = enter(at, patches, spread, table, in_weights)
    if len(bits) > 1:
        ups_w.done(query)
        downs_w.done(query)
    (cot_moved,) = collect([cot_moved], query)
    key_peer = place.swap_core(after(key, ups_w.held, downs_w.held, cot_moved))
    value_peer = place.swap_core(after(value, ups_w.held, downs_w.held, cot_moved))
    ups_w.last(key_peer, value_peer)
    downs_w.last(key_peer, value_peer)
    cot_peer = place.swap_core(after(cot_moved, key_peer, value_peer))
    attended, lse = attend(query, key, key_peer, value, value_peer)
    ups_w.last_done(attended)
    downs_w.last_done(attended)
    (cot_peer,) = collect([cot_peer], attended)
    w_up = (
        ups_w.rows()
        .reshape(devices, blocks, shard, width)
        .transpose(1, 0, 2, 3)
        .reshape(blocks, width, width)
    )
    w_down = downs_w.rows().reshape(ff, width)
    resid, mlp_in, hidden, slope, final = mlp(attended, embed, table, w_out, w_up, b_up, w_down)
    final_peer = place.swap_core(final)
    g_out = gather_rows(after(at, final), cot_moved, cot_peer, half).reshape(-1, width)

    early, late = bits[: len(bits) // 2], bits[len(bits) // 2 :][::-1]
    down = Scatter(place, *weight_grad(at, hidden, g_out, his))
    (final_peer,) = collect([final_peer], down.send)
    down.send = after(down.send, final_peer)
    down.first()
    image = (half, grid, width)
    final_pieces = spread_rows(
        at, final.reshape(image), final_peer.reshape(image), place.strips, capacity
    )
    down.first_done(final_pieces)
    for bit in late[:-1]:
        down.over(bit)
        down.done()
    down.over(late[-1])
    final_moved = exchange(after(final_pieces, down.sent))
    g_upper, g_resid, g_resid_low, g_att, sums_two = mlp_back(
        after(g_out, final_pieces, down.sent), slope, resid, table, w_out, w_up, w_down
    )
    up = Scatter(place, *weight_grad(at, mlp_in, g_upper, his, True))
    down.done(up.send)
    (final_moved,) = collect([final_moved], up.send)
    up.send = after(up.send, final_moved, down.part)
    up.first()
    up.first_done()
    for bit in late[:-1]:
        up.over(bit)
        up.done()
    up.over(late[-1])
    for bit in early[:-1]:
        down.over(bit)
        down.done()
    if early:
        down.over(early[-1])
    g_query, g_key, g_key_peer, g_value, g_value_peer = attend_back(
        query, key, key_peer, value, value_peer, after(g_att, up.sent, down.sent), attended, lse
    )
    up.done(g_query)
    if early:
        down.done(g_query)
    g_key_got = place.swap_core(after(g_key_peer, up.part, down.part))
    g_value_got = place.swap_core(g_value_peer)
    for bit in early[:-1]:
        up.over(bit)
        up.done()
    if early:
        up.over(early[-1])
    g_query, g_key, g_value, g_embed, sums_one, g_pos = leave(
        at,
        after(g_query, up.sent),
        g_key,
        g_key_got,
        g_value,
        g_value_got,
        embed,
        g_resid,
        spread_t,
        table,
        in_weights,
    )
    if early:
        up.done(g_embed)
    g_embed_peer = place.swap_core(g_embed)
    pieces_back = spread_rows(
        at, g_embed.reshape(image), g_embed_peer.reshape(image), place.strips, capacity
    )
    back = exchange(pieces_back)
    small = after(jnp.concatenate([sums_one, sums_two, g_pos]), pieces_back)
    small_got = place.swap_core(small)
    block_out = from_chip(place, after(final_moved, pieces_back), cotangent.shape)
    proj = Scatter(
        place,
        *proj_grad(
            after(at, pieces_back), attn_in, attended, g_query, g_key, g_value, g_resid_low, his
        ),
    )
    back, small_got = collect([back, small_got], proj.send, block_out)
    small = small + small_got
    sent = jnp.concatenate([down.by_strip(), up.by_strip()], axis=1)
    last = Last(after(sent, back))
    proj.send = after(proj.send, back)
    proj.first()
    g_patches = from_chip(place, back, cotangent.shape).reshape(tokens, width)
    small_got = place.along_z(after(small, back), 1)
    patch = Scatter(
        place,
        *weight_grad(
            at,
            base_pixels.reshape(tokens, pixel_len),
            after(g_patches, last.sent),
            his,
        ),
    )
    small = small + collect([small_got], patch.send)[0]
    proj.first_done(patch.send)
    projs = proj.halves()
    patch.first()
    projs[0].over(bits[-1])
    projs[1].over(bits[0])
    patch.first_done()
    patches = patch.halves(-1)
    patches[0].over(bits[-1])
    patches[1].over(bits[0])
    small_got = place.along_z(after(small, patch.part), 2)
    pixel_grad = unmix(
        sizes,
        resize,
        w_left,
        w_right,
        after(
            g_patches, small, patches[0].sent, patches[1].sent, projs[0].sent, projs[1].sent
        ).reshape(group, local_rows, width),
    )
    for scatter in (*patches, *projs):
        scatter.done(pixel_grad)
    small = small + collect([small_got], pixel_grad)[0]
    sums = last.done(pixel_grad)
    patches[0].part = after(patches[0].part, small)
    patches[1].part = after(patches[1].part, small)
    for k in range(1, len(bits)):
        small_got = place.across_img(small, bits[k])
        patches[0].over(bits[-1 - k])
        patches[1].over(bits[k])
        projs[0].over(bits[-1 - k])
        projs[1].over(bits[k])
        small = small + small_got
        for scatter in (*patches, *projs):
            scatter.done()
    small_last = place.across_img(small, bits[0])
    patches[0].part = after(patches[0].part, small)
    tail = Last(
        jnp.concatenate(
            [
                jnp.concatenate([p.by_strip() for p in patches], axis=-1),
                *(p.by_strip() for p in projs),
            ],
            axis=1,
        )
    )
    small = small + small_last
    tail = tail.done(small)
    pixel_grad = pixel_grad.reshape(pixels.shape)

    flat_index = place.flat(place.img, place.z)
    own = lax.dynamic_slice_in_dim(small, flat_index * shard, shard, axis=1)
    ahead = sums_one.shape[0]
    behind = ahead + sums_two.shape[0]
    up_sums = small[ahead + 8 : ahead + 8 + ff // width].reshape(-1)
    s_up_bias = lax.dynamic_slice_in_dim(up_sums, flat_index * ups, ups)
    down_rows = down_weight.shape[0]
    s_down = sums[:down_rows]
    s_up = sums[down_rows:].reshape(ff // width, shard, width).transpose(1, 0, 2).reshape(shard, ff)
    patch_rows = patch_weight.shape[0]
    s_patch = tail[:patch_rows]
    s_proj = tail[patch_rows:].reshape(4, shard, width)

    return (
        block_out,
        pixel_grad,
        s_patch,
        own[behind : behind + BASE * BASE],
        own[0],
        own[1],
        own[2],
        s_proj[0],
        own[3],
        s_proj[1],
        s_proj[2],
        own[4],
        s_proj[3],
        own[ahead],
        own[ahead + 1],
        own[ahead + 2],
        s_up,
        s_up_bias,
        s_down,
        own[ahead + 3],
    )


def solution(mesh):
    rows = P(("img", "strip"))
    split_rows = P(("img", "strip"), None)
    split_columns = P(None, ("img", "strip"))
    held = P("img", "strip", None, None)
    return jax.shard_map(
        body,
        mesh=mesh,
        in_specs=(
            held,
            held,
            P(),
            P(),
            P(),
            P(),
            split_rows,
            split_columns,
            rows,
            rows,
            rows,
            split_rows,
            rows,
            split_rows,
            split_rows,
            rows,
            split_rows,
            rows,
            rows,
            rows,
            split_rows,
            rows,
            split_rows,
            rows,
        ),
        out_specs=(
            held,
            held,
            split_rows,
            split_columns,
            rows,
            rows,
            rows,
            split_rows,
            rows,
            split_rows,
            split_rows,
            rows,
            split_rows,
            rows,
            rows,
            rows,
            split_rows,
            rows,
            split_rows,
            rows,
        ),
        check_vma=False,
    )
```

```python
import functools

import jax
import jax.numpy as jnp
import numpy as np
from jax import lax
from jax.experimental import pallas as pl
from jax.experimental.pallas import tpu as pltpu
from jax.sharding import PartitionSpec as P

HEADS = 12
BASE = 7
HIGH_ACCURACY = lax.Precision.HIGHEST
AXES = ("img", "strip")


def bilinear(out_count, in_count):
    source = (np.arange(out_count, dtype=np.float32) + 0.5) * (in_count / out_count) - 0.5
    source = np.clip(source, 0.0, in_count - 1.0)
    target = np.arange(in_count, dtype=np.float32)
    return np.maximum(1.0 - np.abs(source[:, None] - target[None, :]), 0.0).astype(np.float32)


def matmul(left, right):
    return jnp.dot(left, right, preferred_element_type=jnp.float32)


def left_trans(left, right):
    return lax.dot_general(
        left, right, (((0,), (0,)), ((), ())), preferred_element_type=jnp.float32
    )


def right_trans(left, right):
    return lax.dot_general(
        left, right, (((1,), (1,)), ((), ())), preferred_element_type=jnp.float32
    )


f32 = jnp.float32
bf16 = jnp.bfloat16
VMEM_LIMIT = 56 << 20


def params(*semantics):
    return pltpu.CompilerParams(
        dimension_semantics=semantics or None, vmem_limit_bytes=VMEM_LIMIT
    )


def shaped(shape, dtype):
    return jax.ShapeDtypeStruct(shape, dtype)


def cost(light=False):
    flops = 1024 if light else 1 << 32
    return pl.CostEstimate(flops=flops, bytes_accessed=1024, transcendentals=0)


def fill_mixer(mixer, table, size, turned):
    side = table.shape[0]
    span = side * side
    live = lax.broadcasted_iota(jnp.int32, table.shape, 0) < size
    table = jnp.where(live, table, 0.0)
    column = lax.broadcasted_iota(jnp.int32, (side, span), 1)
    row = lax.broadcasted_iota(jnp.int32, (side, span), 0)

    def widen(chosen):
        return lax.dot_general(
            table,
            chosen.astype(f32),
            (((0 if turned else 1,), (0,)), ((), ())),
            precision=HIGH_ACCURACY,
            preferred_element_type=f32,
        )

    wide = widen(column // side == row)
    tall = widen(column % side == row)
    for i in range(side):
        mixer[i * side : (i + 1) * side, :] = (wide[i : i + 1, :] * tall).astype(bf16)


def mix_kernel(sizes_ref, table_ref, pix_ref, out_ref, mixer):
    step = table_ref.shape[0] // sizes_ref[2]
    size = (sizes_ref[pl.program_id(0)] + 1) * step
    fill_mixer(mixer, table_ref[...], size, False)
    span = mixer.shape[0]
    for c in range(pix_ref.shape[-1] // span):
        columns = slice(c * span, (c + 1) * span)
        out_ref[:, columns] = matmul(pix_ref[:, columns], mixer[...]).astype(bf16)


def mix(sizes, resize, pixels):
    group, rows, length = pixels.shape
    side = resize.shape[1]
    span = side * side
    block = pl.BlockSpec((None, rows, length), lambda g, p: (g, 0, 0))
    return pl.pallas_call(
        mix_kernel,
        grid_spec=pltpu.PrefetchScalarGridSpec(
            num_scalar_prefetch=1,
            grid=(group,),
            in_specs=[pl.BlockSpec((None, side, side), lambda g, p: (p[g], 0, 0)), block],
            out_specs=block,
            scratch_shapes=[pltpu.VMEM((span, span), bf16)],
        ),
        out_shape=shaped(pixels.shape, bf16),
        compiler_params=params("arbitrary"),
        cost_estimate=cost(),
        name="mix",
    )(sizes, resize, pixels)


def unmix_kernel(sizes_ref, table_ref, left_ref, right_ref, grad_ref, out_ref, mixer):
    group = grad_ref.shape[0]

    @pl.when(pl.program_id(0) == 0)
    def _():
        step = table_ref.shape[1] // table_ref.shape[0]
        for g in range(group):
            index = sizes_ref[g]
            fill_mixer(mixer.at[g], table_ref[index], (index + 1) * step, True)

    half = left_ref.shape[1]
    for g in range(group):
        grad = grad_ref[g]
        g_base = (
            right_trans(grad[:, :half], left_ref[...]) + right_trans(grad[:, half:], right_ref[...])
        ).astype(bf16)
        out_ref[g] = matmul(g_base, mixer[g])


def unmix(sizes, resize, left, right, grad):
    group, rows, width = grad.shape
    side = resize.shape[1]
    span = side * side
    length, columns = left.shape
    return pl.pallas_call(
        unmix_kernel,
        grid_spec=pltpu.PrefetchScalarGridSpec(
            num_scalar_prefetch=1,
            grid=(length // span,),
            in_specs=[
                pl.BlockSpec(resize.shape, lambda c, p: (0, 0, 0)),
                pl.BlockSpec((span, columns), lambda c, p: (c, 0)),
                pl.BlockSpec((span, columns), lambda c, p: (c, 0)),
                pl.BlockSpec((group, rows, width), lambda c, p: (0, 0, 0)),
            ],
            out_specs=pl.BlockSpec((group, rows, span), lambda c, p: (0, 0, c)),
            scratch_shapes=[pltpu.VMEM((group, span, span), bf16)],
        ),
        out_shape=shaped((group, rows, length), f32),
        compiler_params=params("arbitrary"),
        cost_estimate=cost(),
        name="unmix",
    )(sizes, resize, left, right, grad)


def attend_kernel(q_ref, ko_ref, kp_ref, vo_ref, vp_ref, out_ref, lse_ref, *, size, chunk):
    first = lax.broadcasted_iota(jnp.int32, (1, 2 * size), 1) < size
    keys = jnp.concatenate([ko_ref[...], kp_ref[...]], axis=0)
    values = jnp.concatenate([vo_ref[...], vp_ref[...]], axis=0)
    for i in range(q_ref.shape[0] // chunk):
        rows = slice(i * chunk, (i + 1) * chunk)
        query = q_ref[rows, :]
        none = jnp.zeros_like(query)
        outs, sums = [], []
        for e in range(2):
            head = jnp.where(first, query, none) if e == 0 else jnp.where(first, none, query)
            scores = right_trans(head, keys)
            peak = jnp.max(scores, axis=-1, keepdims=True)
            expd = jnp.exp(scores - peak)
            denom = jnp.sum(expd, axis=-1, keepdims=True)
            outs.append(matmul(expd.astype(bf16), values) / denom)
            sums.append(peak + jnp.log(denom))
        out_ref[rows, :] = jnp.where(first, outs[0], outs[1]).astype(bf16)
        lse_ref[rows, :] = jnp.where(first, sums[0], sums[1])


def attend(query, key, key_peer, value, value_peer):
    rows, width = query.shape
    size = width // HEADS
    spec = pl.BlockSpec((rows, 2 * size), lambda h: (0, h))
    return pl.pallas_call(
        functools.partial(attend_kernel, size=size, chunk=min(256, rows)),
        grid=(HEADS // 2,),
        in_specs=[spec] * 5,
        out_specs=[spec] * 2,
        out_shape=[shaped((rows, width), bf16), shaped((rows, width), f32)],
        compiler_params=params("arbitrary"),
        cost_estimate=cost(),
        name="attend",
    )(query, key, key_peer, value, value_peer)


def attend_back_kernel(
    q_ref,
    ko_ref,
    kp_ref,
    vo_ref,
    vp_ref,
    g_ref,
    o_ref,
    lse_ref,
    gq_ref,
    gko_ref,
    gkp_ref,
    gvo_ref,
    gvp_ref,
    *,
    size,
    chunk,
):
    rows = q_ref.shape[0]
    upper = lax.broadcasted_iota(jnp.int32, (2 * size, 1), 0) < size
    first = lax.broadcasted_iota(jnp.int32, (1, 2 * size), 1) < size
    query = q_ref[...]
    grad = g_ref[...]
    query_t = query.astype(f32).T
    grad_t = grad.astype(f32).T
    inner_t = grad_t * o_ref[...].astype(f32).T
    lse_t = lse_ref[...].T
    queries, grads, inners, sums, g_query = [], [], [], [], []
    for e in range(2):
        mine = upper if e == 0 else jnp.logical_not(upper)
        queries.append(jnp.where(mine, query_t, 0.0).astype(bf16))
        grads.append(jnp.where(mine, grad_t, 0.0).astype(bf16))
        inners.append(jnp.sum(inner_t[e * size : (e + 1) * size], axis=0, keepdims=True))
        sums.append(lse_t[e * size : e * size + 1])
        g_query.append(jnp.zeros((size, rows), f32))
    for k_ref, v_ref, gk_ref, gv_ref in (
        (ko_ref, vo_ref, gko_ref, gvo_ref),
        (kp_ref, vp_ref, gkp_ref, gvp_ref),
    ):
        for i in range(k_ref.shape[0] // chunk):
            part = slice(i * chunk, (i + 1) * chunk)
            key = k_ref[part, :]
            value = v_ref[part, :]
            key_t = key.astype(f32).T.astype(bf16)
            g_key, g_value = [], []
            for e in range(2):
                probs = jnp.exp(matmul(key, queries[e]) - sums[e])
                g_scores = (probs * (matmul(value, grads[e]) - inners[e])).astype(bf16)
                g_key.append(matmul(g_scores, query))
                g_value.append(matmul(probs.astype(bf16), grad))
                g_query[e] = g_query[e] + matmul(key_t[e * size : (e + 1) * size], g_scores)
            gk_ref[part, :] = jnp.where(first, g_key[0], g_key[1]).astype(gk_ref.dtype)
            gv_ref[part, :] = jnp.where(first, g_value[0], g_value[1]).astype(gv_ref.dtype)
    gq_ref[...] = jnp.concatenate(g_query, axis=0).T.astype(gq_ref.dtype)


def attend_back(query, key, key_peer, value, value_peer, grad, attended, lse):
    rows, width = query.shape
    size = width // HEADS
    spec = pl.BlockSpec((rows, 2 * size), lambda h: (0, h))
    low, full = shaped((rows, width), bf16), shaped((rows, width), f32)
    return pl.pallas_call(
        functools.partial(attend_back_kernel, size=size, chunk=rows),
        grid=(HEADS // 2,),
        in_specs=[spec] * 8,
        out_specs=[spec] * 5,
        out_shape=[low, full, low, full, low],
        compiler_params=params("arbitrary"),
        cost_estimate=cost(True),
        name="attend_back",
    )(query, key, key_peer, value, value_peer, grad, attended, lse)


def whole(shape):
    return pl.BlockSpec(shape, lambda i, s: (0,) * len(shape))


def gather_rows_kernel(at_ref, own_ref, peer_ref, out_ref, rows_ref):
    core = at_ref[0]
    strips, part = own_ref.shape[:2]
    half = out_ref.shape[0]
    for j in range(strips):
        start, count = at_ref[1 + j], at_ref[1 + strips + j]
        for ref, which in ((own_ref, core), (peer_ref, 1 - core)):
            for i in range(part):
                local = which * part + i
                row = start + local - core * half
                here = jnp.logical_and(local < count, jnp.logical_and(row >= 0, row < half))
                rows_ref[jnp.where(here, row, half)] = ref[j, i]
    out_ref[...] = rows_ref[:half]


def gather_rows(at, own, peer, half):
    strips, part, grid, width = own.shape
    out = (half, grid, width)
    return pl.pallas_call(
        gather_rows_kernel,
        grid_spec=pltpu.PrefetchScalarGridSpec(
            num_scalar_prefetch=1,
            grid=(1,),
            in_specs=[whole(own.shape)] * 2,
            out_specs=whole(out),
            scratch_shapes=[pltpu.VMEM((half + 1, grid, width), bf16)],
        ),
        out_shape=shaped(out, bf16),
        compiler_params=params("arbitrary"),
        cost_estimate=cost(),
        name="gather_rows",
    )(at, own, peer)


def spread_rows_kernel(at_ref, own_ref, peer_ref, out_ref, rows_ref):
    core = at_ref[0]
    strips, part = out_ref.shape[:2]
    half = own_ref.shape[0]
    rows_ref[pl.ds(core * half, half)] = own_ref[...]
    rows_ref[pl.ds((1 - core) * half, half)] = peer_ref[...]
    rows_ref[2 * half] = jnp.zeros(rows_ref.shape[1:], bf16)
    for j in range(strips):
        start, count = at_ref[1 + j], at_ref[1 + strips + j]
        for i in range(part):
            local = core * part + i
            out_ref[j, i] = rows_ref[jnp.where(local < count, start + local, 2 * half)]


def spread_rows(at, own, peer, strips, capacity):
    half, grid, width = own.shape
    out = (strips, capacity // 2, grid, width)
    return pl.pallas_call(
        spread_rows_kernel,
        grid_spec=pltpu.PrefetchScalarGridSpec(
            num_scalar_prefetch=1,
            grid=(1,),
            in_specs=[whole(own.shape)] * 2,
            out_specs=whole(out),
            scratch_shapes=[pltpu.VMEM((2 * half + 1, grid, width), bf16)],
        ),
        out_shape=shaped(out, bf16),
        compiler_params=params("arbitrary"),
        cost_estimate=cost(),
        name="spread_rows",
    )(at, own, peer)


def normalise(values):
    centred = values - jnp.mean(values, axis=-1, keepdims=True)
    scale = lax.rsqrt(jnp.mean(centred * centred, axis=-1, keepdims=True) + 1e-06)
    return centred * scale, scale


def norm_back(grad, normed, scale):
    return scale * (
        grad
        - jnp.mean(grad, axis=-1, keepdims=True)
        - normed * jnp.mean(grad * normed, axis=-1, keepdims=True)
    )


def column_sum(values):
    return jnp.sum(values, axis=0, keepdims=True)


PATCH, GAIN1, SHIFT1, QUERY, VALUE, OUT, GAIN2, SHIFT2, DOWN = range(9)
VECTORS = 9
UP_AT = 9
POS_AT = 16
TABLE = 96
POS_ROWS = 64


def patch_kernel(base_ref, left_ref, right_ref, out_ref):
    half = left_ref.shape[1]
    out_ref[:, :half] = matmul(base_ref[...], left_ref[...]).astype(bf16)
    out_ref[:, half:] = matmul(base_ref[...], right_ref[...]).astype(bf16)


def embed_patches(base, left, right):
    group, rows, length = base.shape
    half = left.shape[1]
    return pl.pallas_call(
        patch_kernel,
        grid=(group,),
        in_specs=[
            pl.BlockSpec((None, rows, length), lambda t: (t, 0, 0)),
            pl.BlockSpec((length, half), lambda t: (0, 0)),
            pl.BlockSpec((length, half), lambda t: (0, 0)),
        ],
        out_specs=pl.BlockSpec((None, rows, 2 * half), lambda t: (t, 0, 0)),
        out_shape=shaped((group, rows, 2 * half), bf16),
        compiler_params=params("arbitrary"),
        cost_estimate=cost(),
        name="embed_patches",
    )(base, left, right)


def enter_kernel(
    at_ref, patches_ref, spread_ref, table_ref, ql_ref, qr_ref, kl_ref, kr_ref, vl_ref, vr_ref,
    embed_ref, in_ref, q_ref, k_ref, v_ref,
):
    def vector(row):
        return table_ref[row : row + 1, :]

    place_rows = jnp.dot(
        spread_ref[...],
        table_ref[POS_AT : POS_AT + POS_ROWS, :],
        precision=HIGH_ACCURACY,
        preferred_element_type=f32,
    )
    embed = patches_ref[...].astype(f32) + vector(PATCH) + place_rows
    embed_ref[...] = embed
    normed, _ = normalise(embed)
    attn_in = (normed * vector(GAIN1) + vector(SHIFT1)).astype(bf16)
    in_ref[...] = attn_in
    half = ql_ref.shape[1]
    for ref, weights, bias, scale in (
        (q_ref, (ql_ref, qr_ref), vector(QUERY), 0.125),
        (k_ref, (kl_ref, kr_ref), None, None),
        (v_ref, (vl_ref, vr_ref), vector(VALUE), None),
    ):
        for columns, weight in zip((slice(0, half), slice(half, 2 * half)), weights):
            rows = matmul(attn_in, weight[...])
            if bias is not None:
                rows = rows + bias[:, columns]
            if scale is not None:
                rows = rows * scale
            ref[:, columns] = rows.astype(bf16)


def enter(at, patches, spread, table, weights, blocks=2):
    rows, width = patches.shape
    block = rows // blocks
    part = pl.BlockSpec((block, width), lambda t, a: (t, 0))
    weight = pl.BlockSpec(weights[0].shape, lambda t, a: (0, 0))
    low = shaped((rows, width), bf16)
    return pl.pallas_call(
        enter_kernel,
        grid_spec=pltpu.PrefetchScalarGridSpec(
            num_scalar_prefetch=1,
            grid=(blocks,),
            in_specs=[
                part,
                pl.BlockSpec((None, block, POS_ROWS), lambda t, a: (a[0], t, 0)),
                pl.BlockSpec(table.shape, lambda t, a: (0, 0)),
                *([weight] * 6),
            ],
            out_specs=[part] * 5,
        ),
        out_shape=[shaped((rows, width), f32), low, low, low, low],
        compiler_params=params("arbitrary"),
        cost_estimate=cost(),
        name="enter",
    )(at, patches, spread, table, *weights)


def mlp_kernel(
    attended_ref, embed_ref, table_ref, ol_ref, or_ref, up_ref, bias_ref, down_ref,
    resid_ref, in_ref, hidden_ref, slope_ref, out_ref, total,
):
    step = pl.program_id(0)

    def vector(row):
        return table_ref[row : row + 1, :]

    @pl.when(step == 0)
    def _():
        half = ol_ref.shape[1]
        for columns, weight in ((slice(0, half), ol_ref), (slice(half, 2 * half), or_ref)):
            resid_ref[:, columns] = (
                embed_ref[:, columns]
                + matmul(attended_ref[...], weight[...])
                + vector(OUT)[:, columns]
            )
        resid = resid_ref[...]
        normed, _ = normalise(resid)
        in_ref[...] = (normed * vector(GAIN2) + vector(SHIFT2)).astype(bf16)
        total[...] = resid + vector(DOWN)

    upper = matmul(in_ref[...], up_ref[...]) + bias_ref[...]
    below = 0.5 + 0.5 * lax.erf(upper * 0.7071067811865476)
    hidden = (upper * below).astype(bf16)
    hidden_ref[...] = hidden
    slope_ref[...] = (below + upper * (0.3989422804014327 * jnp.exp(-0.5 * upper * upper))).astype(
        slope_ref.dtype
    )
    total[...] += matmul(hidden, down_ref[...])

    @pl.when(step == pl.num_programs(0) - 1)
    def _():
        out_ref[...] = total[...].astype(bf16)


def mlp(attended, embed, table, w_out, w_up, b_up, w_down):
    rows, width = embed.shape
    blocks = w_up.shape[0]
    ff = blocks * width
    fixed = pl.BlockSpec((rows, width), lambda t: (0, 0))
    columns = pl.BlockSpec((rows, width), lambda t: (0, t))
    return pl.pallas_call(
        mlp_kernel,
        grid=(blocks,),
        in_specs=[
            fixed,
            fixed,
            pl.BlockSpec(table.shape, lambda t: (0, 0)),
            *([pl.BlockSpec(w_out[0].shape, lambda t: (0, 0))] * 2),
            pl.BlockSpec((None, width, width), lambda t: (t, 0, 0)),
            pl.BlockSpec((1, width), lambda t: (0, t)),
            pl.BlockSpec((width, width), lambda t: (t, 0)),
        ],
        out_specs=[fixed, fixed, columns, columns, fixed],
        out_shape=[
            shaped((rows, width), f32),
            shaped((rows, width), bf16),
            shaped((rows, ff), bf16),
            shaped((rows, ff), f32),
            shaped((rows, width), bf16),
        ],
        scratch_shapes=[pltpu.VMEM((rows, width), f32)],
        compiler_params=params("arbitrary"),
        cost_estimate=cost(),
        name="mlp",
    )(attended, embed, table, *w_out, w_up, b_up, w_down)


def mlp_back_kernel(
    g_ref, slope_ref, resid_ref, table_ref, ol_ref, or_ref, up_ref, down_ref,
    upper_ref, resid_grad_ref, low_ref, att_ref, sums_ref, total,
):
    step = pl.program_id(0)

    @pl.when(step == 0)
    def _():
        total[...] = jnp.zeros_like(total)
        sums_ref[...] = jnp.zeros_like(sums_ref)

    g_upper = slope_ref[...].astype(f32) * right_trans(g_ref[...], down_ref[...])
    sums_ref[pl.ds(8 + step, 1), :] = column_sum(g_upper)
    g_upper_low = g_upper.astype(bf16)
    upper_ref[...] = g_upper_low
    total[...] += right_trans(g_upper_low, up_ref[...])

    @pl.when(step == pl.num_programs(0) - 1)
    def _():
        grad = total[...]
        g_out = g_ref[...].astype(f32)
        normed, scale = normalise(resid_ref[...])
        g_resid = g_out + norm_back(grad * table_ref[GAIN2 : GAIN2 + 1, :], normed, scale)
        resid_grad_ref[...] = g_resid
        g_resid_low = g_resid.astype(bf16)
        low_ref[...] = g_resid_low
        half = ol_ref.shape[1]
        att_ref[...] = (
            right_trans(g_resid_low[:, :half], ol_ref[...])
            + right_trans(g_resid_low[:, half:], or_ref[...])
        ).astype(bf16)
        sums_ref[0:1, :] = column_sum(g_resid)
        sums_ref[1:2, :] = column_sum(grad * normed)
        sums_ref[2:3, :] = column_sum(grad)
        sums_ref[3:4, :] = column_sum(g_out)


def mlp_back(g_out, slope, resid, table, w_out, w_up, w_down):
    rows, width = g_out.shape
    blocks = w_up.shape[0]
    ff = blocks * width
    fixed = pl.BlockSpec((rows, width), lambda t: (0, 0))
    columns = pl.BlockSpec((rows, width), lambda t: (0, t))
    sums = (8 + 8 * (-(-blocks // 8)), width)
    return pl.pallas_call(
        mlp_back_kernel,
        grid=(blocks,),
        in_specs=[
            fixed,
            columns,
            fixed,
            pl.BlockSpec(table.shape, lambda t: (0, 0)),
            *([pl.BlockSpec(w_out[0].shape, lambda t: (0, 0))] * 2),
            pl.BlockSpec((None, width, width), lambda t: (t, 0, 0)),
            pl.BlockSpec((width, width), lambda t: (t, 0)),
        ],
        out_specs=[columns, fixed, fixed, fixed, pl.BlockSpec(sums, lambda t: (0, 0))],
        out_shape=[
            shaped((rows, ff), bf16),
            shaped((rows, width), f32),
            shaped((rows, width), bf16),
            shaped((rows, width), bf16),
            shaped(sums, f32),
        ],
        scratch_shapes=[pltpu.VMEM((rows, width), f32)],
        compiler_params=params("arbitrary"),
        cost_estimate=cost(True),
        name="mlp_back",
    )(g_out, slope, resid, table, *w_out, w_up, w_down)


def leave_kernel(
    at_ref, gq_ref, gk_ref, gkp_ref, gv_ref, gvp_ref, embed_ref, resid_ref, spread_ref, table_ref,
    ql_ref, qr_ref, kl_ref, kr_ref, vl_ref, vr_ref, q_ref, k_ref, v_ref, out_ref, sums_ref, pos_ref,
):
    @pl.when(pl.program_id(0) == 0)
    def _():
        sums_ref[...] = jnp.zeros_like(sums_ref)
        pos_ref[...] = jnp.zeros_like(pos_ref)

    g_query = gq_ref[...].astype(f32) * 0.125
    g_query_low = g_query.astype(bf16)
    g_key_low = (gk_ref[...] + gkp_ref[...].astype(f32)).astype(bf16)
    g_value_low = (gv_ref[...] + gvp_ref[...].astype(f32)).astype(bf16)
    q_ref[...] = g_query_low
    k_ref[...] = g_key_low
    v_ref[...] = g_value_low
    half = ql_ref.shape[1]
    grad = jnp.zeros(embed_ref.shape, f32)
    for low, weights in (
        (g_query_low, (ql_ref, qr_ref)),
        (g_key_low, (kl_ref, kr_ref)),
        (g_value_low, (vl_ref, vr_ref)),
    ):
        grad = grad + right_trans(low[:, :half], weights[0][...])
        grad = grad + right_trans(low[:, half:], weights[1][...])
    normed, scale = normalise(embed_ref[...])
    g_embed = resid_ref[...] + norm_back(grad * table_ref[GAIN1 : GAIN1 + 1, :], normed, scale)
    out_ref[...] = g_embed.astype(bf16)
    sums_ref[0:1, :] += column_sum(g_embed)
    sums_ref[1:2, :] += column_sum(grad * normed)
    sums_ref[2:3, :] += column_sum(grad)
    sums_ref[3:4, :] += column_sum(g_query)
    sums_ref[4:5, :] += column_sum(g_value_low.astype(f32))
    pos_ref[...] += jnp.dot(
        spread_ref[...], g_embed, precision=HIGH_ACCURACY, preferred_element_type=f32
    )


def leave(
    at, g_query, g_key, g_key_peer, g_value, g_value_peer, embed, g_resid, spread, table,
    weights, blocks=2,
):
    rows, width = embed.shape
    block = rows // blocks
    part = pl.BlockSpec((block, width), lambda t, a: (t, 0))
    weight = pl.BlockSpec(weights[0].shape, lambda t, a: (0, 0))
    low = shaped((rows, width), bf16)
    return pl.pallas_call(
        leave_kernel,
        grid_spec=pltpu.PrefetchScalarGridSpec(
            num_scalar_prefetch=1,
            grid=(blocks,),
            in_specs=[part] * 7
            + [
                pl.BlockSpec((None, POS_ROWS, block), lambda t, a: (a[0], 0, t)),
                pl.BlockSpec(table.shape, lambda t, a: (0, 0)),
                *([weight] * 6),
            ],
            out_specs=[part] * 4
            + [
                pl.BlockSpec((8, width), lambda t, a: (0, 0)),
                pl.BlockSpec((POS_ROWS, width), lambda t, a: (0, 0)),
            ],
        ),
        out_shape=[low] * 4 + [shaped((8, width), f32), shaped((POS_ROWS, width), f32)],
        compiler_params=params("arbitrary"),
        cost_estimate=cost(),
        name="leave",
    )(
        at, g_query, g_key, g_key_peer, g_value, g_value_peer, embed, g_resid, spread, table,
        *weights,
    )


def weight_grad_kernel(at_ref, left_ref, right_ref, send_ref, keep_ref, total):
    core = at_ref[0]
    group, rows, _ = send_ref.shape
    total[...] = left_trans(left_ref[...], right_ref[...])
    for h in range(group):
        sent = pl.multiple_of((2 * h + 1 - core) * rows, 8)
        kept = pl.multiple_of((2 * h + core) * rows, 8)
        send_ref[h] = total[pl.ds(sent, rows), :].astype(bf16)
        keep_ref[h] = total[pl.ds(kept, rows), :].astype(bf16)


def weight_grad(at, left, right, his, light=False):
    tokens, m = left.shape
    n = right.shape[1]
    rows = m // (2 * his)
    tall = min(m, 768)
    h = tall // (2 * rows)
    wide = 768
    blocks = n // wide
    out = pl.BlockSpec((h, None, rows, wide), lambda i, j, a: (i, j, 0, 0))
    shape = (his, blocks, rows, wide)
    return pl.pallas_call(
        weight_grad_kernel,
        grid_spec=pltpu.PrefetchScalarGridSpec(
            num_scalar_prefetch=1,
            grid=(m // tall, blocks),
            in_specs=[
                pl.BlockSpec((tokens, tall), lambda i, j, a: (0, i)),
                pl.BlockSpec((tokens, wide), lambda i, j, a: (0, j)),
            ],
            out_specs=[out, out],
            scratch_shapes=[pltpu.VMEM((tall, wide), f32)],
        ),
        out_shape=[shaped(shape, bf16)] * 2,
        compiler_params=params("arbitrary", "arbitrary"),
        cost_estimate=cost(light),
        name="weight_grad",
    )(at, left, right)


def proj_grad_kernel(
    at_ref, in_ref, att_ref, gq_ref, gk_ref, gv_ref, go_ref, small_ref, send_ref, keep_ref, total
):
    core = at_ref[0]
    his, rows, length = send_ref.shape
    width = gq_ref.shape[1]
    turned = [
        small_ref[:, i * 128 : (i + 1) * 128].T for i in range(width // 128)
    ]
    small = jnp.concatenate(turned, axis=0)
    pairs = ((in_ref, gq_ref), (in_ref, gk_ref), (in_ref, gv_ref), (att_ref, go_ref), None)
    for i, pair in enumerate(pairs):
        if pair is None:
            columns = slice(i * width, length)
            total[:, : length - i * width] = small
        else:
            columns = slice(i * width, (i + 1) * width)
            total[...] = left_trans(pair[0][...], pair[1][...])
        size = columns.stop - columns.start
        for h in range(his):
            sent = pl.multiple_of((2 * h + 1 - core) * rows, 8)
            kept = pl.multiple_of((2 * h + core) * rows, 8)
            send_ref[h, :, columns] = total[pl.ds(sent, rows), :size].astype(bf16)
            keep_ref[h, :, columns] = total[pl.ds(kept, rows), :size].astype(bf16)


def proj_grad(at, attn_in, attended, g_query, g_key, g_value, g_resid, small, his):
    tokens, width = attn_in.shape
    rows = width // (2 * his)
    out = (his, rows, 4 * width + small.shape[0])
    return pl.pallas_call(
        proj_grad_kernel,
        grid_spec=pltpu.PrefetchScalarGridSpec(
            num_scalar_prefetch=1,
            grid=(1,),
            in_specs=[whole(attn_in.shape)] * 6 + [whole(small.shape)],
            out_specs=[whole(out)] * 2,
            scratch_shapes=[pltpu.VMEM((width, width), f32)],
        ),
        out_shape=[shaped(out, bf16)] * 2,
        compiler_params=params("arbitrary"),
        cost_estimate=cost(),
        name="proj_grad",
    )(at, attn_in, attended, g_query, g_key, g_value, g_resid, small)


class Place:
    def __init__(self, group):
        self.group = group
        self.images = lax.axis_size("img")
        self.strips = lax.axis_size("strip")
        assert group == 2 and self.strips == 4
        self.img = lax.axis_index("img")
        self.core = self.img % 2
        self.z = lax.axis_index("strip")
        self.bits = [1 << k for k in range(1, self.images.bit_length() - 1)]
        assert self.images == 2 << len(self.bits)

    def flat(self, img, z):
        return img * self.strips + z

    def swap_core(self, values):
        return lax.ppermute(values, "img", [(i, i ^ 1) for i in range(self.images)])

    def across_img(self, values, bit):
        return lax.ppermute(values, "img", [(i, i ^ bit) for i in range(self.images)])

    def along_z(self, values, r):
        return lax.ppermute(values, "strip", [(z, z ^ r) for z in range(self.strips)])


def pick(values, index, axis=0):
    return lax.dynamic_index_in_dim(values, index, axis, keepdims=False)


def after(values, *others):
    return lax.optimization_barrier((values,) + others)[0]


def collect(values, *others):
    values = tuple(values)
    return lax.optimization_barrier(values + others)[: len(values)]


def exchange(values):
    return lax.all_to_all(values, "strip", 0, 0, tiled=True)


class Gather:
    def __init__(self, place, held, bits=()):
        self.place = place
        self.held = held
        self.wide = None
        self.bits = list(bits)

    def halves(self):
        middle = self.held.shape[-1] // 2
        return [
            Gather(self.place, self.held[..., columns], self.bits)
            for columns in (slice(0, middle), slice(middle, None))
        ]

    def widen(self, *others):
        held = after(self.held, *others) if others else self.held
        self.wide = jnp.broadcast_to(held, (self.place.strips,) + held.shape)

    def along_z(self, *others):
        if self.wide is None:
            self.widen(*others)
        self.start = after(self.wide, *others) if others else self.wide
        self.held = exchange(self.start)

    def z_done(self, *others):
        (self.held,) = collect([self.held], *others)

    def over(self, bit, *others):
        if others:
            self.held = after(self.held, *others)
        self.bit = bit
        self.got = self.place.across_img(self.held, bit)

    def done(self, *others):
        (got,) = collect([self.got], *others)
        self.bits = sorted(self.bits + [self.bit], reverse=True)
        axis = self.bits.index(self.bit)
        self.held = join(self.held, got, axis, (self.place.img // self.bit) % 2)

    def last(self, *others):
        if others:
            self.held = after(self.held, *others)
        self.other = self.place.swap_core(self.held)

    def last_done(self, *others):
        (self.other,) = collect([self.other], *others)

    def rows(self, start=0, stop=None):
        axis = len(self.bits)
        full = join(self.held[..., start:stop, :], self.other[..., start:stop, :], axis, self.place.core)
        return full.reshape((-1,) + full.shape[-2:])


def join(mine, other, axis, at):
    spot = [1] * (mine.ndim + 1)
    spot[axis] = 2
    where = jnp.arange(2, dtype=jnp.int32).reshape(spot) == at
    return jnp.where(where, jnp.expand_dims(mine, axis), jnp.expand_dims(other, axis))


def add_low(a, b):
    return (a.astype(f32) + b.astype(f32)).astype(bf16)


class Scatter:
    def __init__(self, place, send, keep):
        self.place = place
        self.bits = place.bits[::-1]
        self.send = send
        self.keep = keep

    def first(self):
        self.got = self.place.swap_core(self.send)

    def first_done(self, *others):
        (got,) = collect([self.got], *others)
        shape = (2,) * len(self.bits) + self.send.shape[1:]
        self.part = add_low(self.keep.reshape(shape), got.reshape(shape))

    def halves(self, middle=None):
        axis = self.part.ndim - 1
        parts = []
        if middle is None:
            middle = self.part.shape[axis] // 2
        for start, stop in ((0, middle), (middle, self.part.shape[axis])):
            one = Scatter(self.place, None, None)
            one.part = lax.slice_in_dim(self.part, start, stop, axis=axis)
            parts.append(one)
        return parts

    def over(self, bit):
        self.bit = bit
        axis = self.bits.index(bit)
        self.sent = pick(self.part, 1 - (self.place.img // bit) % 2, axis)
        self.got = self.place.across_img(self.sent, bit)

    def done(self, *others):
        (got,) = collect([self.got], *others)
        axis = self.bits.index(self.bit)
        self.part = add_low(pick(self.part, (self.place.img // self.bit) % 2, axis), got)
        self.bits = [b for b in self.bits if b != self.bit]

    def by_strip(self):
        blocks, rows, columns = self.part.shape
        part = self.part.reshape(blocks, self.place.strips, -1, columns)
        return part.transpose(1, 0, 2, 3).reshape(self.place.strips, -1, columns)


class Last:
    def __init__(self, values):
        self.sent = values.astype(bf16)
        self.got = exchange(self.sent)

    def done(self, *others):
        (got,) = collect([self.got], *others)
        return jnp.sum(got.astype(f32), axis=0)


def split_rows(place, values):
    images, rows = values.shape[:2]
    values = values.reshape((images, 2, rows // 2) + values.shape[2:])
    return pick(values, place.core, 1), pick(values, 1 - place.core, 1)


def pair_up(place, mine, other):
    return jnp.where(
        place.core == 0, jnp.concatenate([mine, other]), jnp.concatenate([other, mine])
    )


def from_chip(place, moved, shape):
    images, rows = shape[0], shape[1] // 2
    moved = moved.reshape((2, images) + moved.shape[1:])
    mine, sent = pick(moved, place.core), pick(moved, 1 - place.core)
    got = place.swap_core(sent)
    low = jnp.where(place.core == 0, mine, got)
    high = jnp.where(place.core == 0, got, mine)
    return jnp.concatenate([low, high], axis=1)


def body(
    pixels,
    cotangent,
    resize,
    patch_index,
    slot_image,
    strip_rows,
    patch_weight,
    pos_grid,
    patch_bias,
    attention_norm_gain,
    attn_shift,
    query_weight,
    query_bias,
    key_weight,
    value_weight,
    value_bias,
    out_weight,
    out_bias,
    mlp_gain,
    mlp_shift,
    up_weight,
    up_bias,
    down_weight,
    down_bias,
):
    group, capacity, grid, pixel_len = pixels.shape
    width = cotangent.shape[3]
    ff = up_weight.shape[1]
    local_rows = capacity * grid
    tokens = group * local_rows
    place = Place(group)
    devices = place.images * place.strips
    his = place.images // 2
    first_slot = place.img * group
    shard = patch_bias.shape[0]
    ups = up_bias.shape[0]
    columns = width // 2
    bits = place.bits

    vectors = (
        patch_bias,
        attention_norm_gain,
        attn_shift,
        query_bias,
        value_bias,
        out_bias,
        mlp_gain,
        mlp_shift,
        down_bias,
    )
    pieces = ups // shard
    small = jnp.concatenate(
        [
            jnp.stack(vectors + tuple(up_bias[i * shard : (i + 1) * shard] for i in range(pieces))),
            jnp.zeros((POS_AT - VECTORS - pieces, shard), bf16),
            pos_grid,
            jnp.zeros((TABLE - POS_AT - BASE * BASE, shard), bf16),
        ]
    )
    lane = width // (TABLE // 16)
    small = jnp.pad(small, ((0, 0), (0, lane - shard))).reshape(-1, 16, lane)
    small = jnp.concatenate(list(small), axis=1)
    proj = jnp.concatenate([query_weight, key_weight, value_weight, out_weight, small])

    size_count = resize.shape[0]
    slot_ids = lax.dynamic_slice_in_dim(slot_image, first_slot, group)
    picked = slot_ids[:, None] == jnp.arange(patch_index.shape[0], dtype=jnp.int32)[None, :]
    size_index = jnp.sum(jnp.where(picked, patch_index[None, :], 0), axis=1)
    sizes = jnp.append(size_index, size_count).astype(jnp.int32)
    half = grid // 2
    image_counts = pick(strip_rows, (place.img // 2) * 2 * group + place.z)
    starts = jnp.cumsum(image_counts) - image_counts
    at = jnp.concatenate([place.core[None], starts, image_counts]).astype(jnp.int32)

    spread = bilinear(grid, BASE)
    spread = (spread[:, None, :, None] * spread[None, :, None, :]).reshape(2, half * grid, -1)
    spread = np.pad(spread, ((0, 0), (0, 0), (0, POS_ROWS - BASE * BASE)))
    spread_t = jnp.asarray(np.ascontiguousarray(spread.transpose(0, 2, 1)))
    spread = jnp.asarray(spread)

    whole_patch, packed = Gather(place, patch_weight), Gather(place, proj)
    blocks = ff // width
    both = Gather(
        place,
        jnp.concatenate(
            [down_weight]
            + [up_weight[:, i * width : (i + 1) * width] for i in range(blocks)]
        ),
    )
    whole_patch.along_z()
    base_pixels = mix(after(sizes, at), resize, pixels.reshape(group, local_rows, pixel_len))
    whole_patch.z_done(base_pixels)
    left, right = whole_patch.halves()
    for k in range(len(bits)):
        if k == len(bits) - 1:
            packed.along_z(left.held, right.held)
        left.over(bits[k])
        right.over(bits[-1 - k])
        if k == len(bits) - 1:
            cot_mine, cot_sent = split_rows(place, after(cotangent, packed.start))
            cot_got = place.swap_core(cot_sent)
            cot_pair = pair_up(place, cot_mine, cot_got)
            both.widen(packed.start)
            left.done(cot_pair, both.wide)
            right.done(cot_pair, both.wide)
        else:
            left.done()
            right.done()
    packed.z_done()
    left.last(packed.held, right.held)
    right.last(packed.held, left.held)
    left.last_done()
    right.last_done()
    w_left, w_right = left.rows().reshape(-1, columns), right.rows().reshape(-1, columns)
    packs = packed.halves()
    packs[0].over(bits[0], left.other)
    packs[1].over(bits[-1], left.other)
    both.along_z(left.other, right.other)
    patches = embed_patches(base_pixels, w_left, w_right).reshape(group, capacity, grid, width)
    packs[0].done(patches)
    packs[1].done(patches)
    for k in range(1, len(bits)):
        packs[0].over(bits[k])
        packs[1].over(bits[-1 - k])
        packs[0].done()
        packs[1].done()
    both.z_done(patches)
    downs_w = Gather(place, both.held[:, : down_weight.shape[0]], both.bits)
    ups_w = Gather(place, both.held[:, down_weight.shape[0] :], both.bits)
    patch_mine, patch_sent = split_rows(place, after(patches, both.held))
    patch_got = place.swap_core(patch_sent)
    patch_pair = pair_up(place, patch_mine, patch_got)
    patch_moved = exchange(patch_pair)
    packs[0].last(patch_pair)
    packs[1].last(patch_pair)
    ups_w.over(bits[-1], packs[0].held, packs[1].held)
    downs_w.over(bits[0], packs[0].held, packs[1].held)
    for k in range(1, len(bits) - 1):
        ups_w.done()
        downs_w.done()
        ups_w.over(bits[-1 - k])
        downs_w.over(bits[k])

    halves = [
        [p.rows(i * shard, (i + 1) * shard).reshape(width, columns) for p in packs]
        for i in range(4)
    ]
    in_weights = [*halves[0], *halves[1], *halves[2]]
    w_out = halves[3]
    flat = jnp.concatenate([p.rows(4 * shard) for p in packs], axis=-1)
    table = (
        flat.reshape(devices, 16, TABLE // 16, lane)[..., :shard]
        .transpose(2, 1, 0, 3)
        .reshape(TABLE, width)
        .astype(f32)
    )
    b_up = (
        table[UP_AT : UP_AT + pieces]
        .reshape(pieces, devices, shard)
        .transpose(1, 0, 2)
        .reshape(1, ff)
    )
    (patch_moved,) = collect([patch_moved], table, b_up, cot_pair, *in_weights, *w_out)
    ups_w.done(patch_moved)
    downs_w.done(patch_moved)
    patch_peer = place.swap_core(patch_moved)
    patches = gather_rows(at, patch_moved, patch_peer, half).reshape(-1, width)
    if len(bits) > 1:
        ups_w.over(bits[0], patch_moved)
        downs_w.over(bits[-1], patch_moved)
    cot_moved = exchange(after(cot_pair, patch_moved))

    embed, attn_in, query, key, value = enter(at, patches, spread, table, in_weights)
    if len(bits) > 1:
        ups_w.done(query)
        downs_w.done(query)
    (cot_moved,) = collect([cot_moved], query)
    key_peer = place.swap_core(after(key, ups_w.held, downs_w.held, cot_moved))
    value_peer = place.swap_core(after(value, ups_w.held, downs_w.held, cot_moved))
    ups_w.last(key_peer, value_peer)
    downs_w.last(key_peer, value_peer)
    cot_peer = place.swap_core(after(cot_moved, key_peer, value_peer))
    attended, lse = attend(query, key, key_peer, value, value_peer)
    ups_w.last_done(attended)
    downs_w.last_done(attended)
    (cot_peer,) = collect([cot_peer], attended)
    w_up = (
        ups_w.rows()
        .reshape(devices, blocks, shard, width)
        .transpose(1, 0, 2, 3)
        .reshape(blocks, width, width)
    )
    w_down = downs_w.rows().reshape(ff, width)
    resid, mlp_in, hidden, slope, final = mlp(attended, embed, table, w_out, w_up, b_up, w_down)
    final_peer = place.swap_core(final)
    g_out = gather_rows(after(at, final), cot_moved, cot_peer, half).reshape(-1, width)

    early, late = bits[: len(bits) // 2], bits[len(bits) // 2 :][::-1]
    down = Scatter(place, *weight_grad(at, hidden, g_out, his))
    (final_peer,) = collect([final_peer], down.send)
    down.send = after(down.send, final_peer)
    down.first()
    image = (half, grid, width)
    final_pieces = spread_rows(
        at, final.reshape(image), final_peer.reshape(image), place.strips, capacity
    )
    down.first_done(final_pieces)
    for bit in late[:-1]:
        down.over(bit)
        down.done()
    down.over(late[-1])
    final_moved = exchange(after(final_pieces, down.sent))
    g_upper, g_resid, g_resid_low, g_att, sums_two = mlp_back(
        after(g_out, final_pieces, down.sent), slope, resid, table, w_out, w_up, w_down
    )
    g_query, g_key, g_key_peer, g_value, g_value_peer = attend_back(
        query, key, key_peer, value, value_peer, g_att, attended, lse
    )
    down.done(g_query)
    (final_moved,) = collect([final_moved], g_query)
    g_key_got = place.swap_core(after(g_key_peer, down.part, final_moved))
    g_value_got = place.swap_core(after(g_value_peer, down.part, final_moved))
    for bit in early[:-1]:
        down.over(bit)
        down.done()
    if early:
        down.over(early[-1])
    up = Scatter(
        place, *weight_grad(at, mlp_in, after(g_upper, g_query, down.sent, final_moved), his)
    )
    g_key_got, g_value_got = collect([g_key_got, g_value_got], up.send)
    up.send = after(up.send, g_key_got, g_value_got)
    up.first()
    g_query, g_key, g_value, g_embed, sums_one, g_pos = leave(
        at,
        after(g_query, up.send),
        g_key,
        g_key_got,
        g_value,
        g_value_got,
        embed,
        g_resid,
        spread_t,
        table,
        in_weights,
    )
    g_embed_peer = place.swap_core(g_embed)
    if early:
        down.done(g_embed)
    up.first_done(g_embed)
    for bit in late[:-1]:
        up.over(bit)
        up.done()
    up.over(late[-1])
    pieces_back = spread_rows(
        after(at, down.part, up.sent),
        g_embed.reshape(image),
        g_embed_peer.reshape(image),
        place.strips,
        capacity,
    )
    back = exchange(pieces_back)
    up_sums = (
        sums_two[8 : 8 + blocks]
        .reshape(devices, pieces, shard)
        .transpose(1, 0, 2)
        .reshape(pieces, width)
    )
    small = jnp.concatenate([sums_one, sums_two[:8], g_pos, up_sums])
    small = jnp.pad(small, ((0, 128 - small.shape[0]), (0, 0)))
    block_out = from_chip(place, after(final_moved, pieces_back), cotangent.shape)
    proj = Scatter(
        place,
        *(
            part[:, None]
            for part in proj_grad(
                after(at, pieces_back),
                attn_in,
                attended,
                g_query,
                g_key,
                g_value,
                g_resid_low,
                small,
                his,
            )
        ),
    )
    back, up.got = collect([back, up.got], proj.send, block_out)
    up.done()
    proj.send = after(proj.send, back)
    proj.first()
    for bit in early[:-1]:
        up.over(bit)
        up.done()
    if early:
        up.part = after(up.part, back)
        up.over(early[-1])
    down_last = Last(after(down.by_strip(), back))
    g_patches = from_chip(place, back, cotangent.shape).reshape(tokens, width)
    proj.first_done(g_patches)
    projs = proj.halves(2 * width)
    projs[0].over(bits[-1])
    projs[1].over(bits[0])
    patch = Scatter(
        place,
        *weight_grad(
            at,
            base_pixels.reshape(tokens, pixel_len),
            after(g_patches, projs[0].sent, projs[1].sent, down_last.sent),
            his,
        ),
    )
    projs[0].done(patch.send)
    projs[1].done(patch.send)
    if early:
        up.done(patch.send)
    s_down = down_last.done(patch.send)
    patch.send = after(patch.send, projs[0].part, projs[1].part, up.part, s_down)
    patch.first()
    patch.first_done()
    patches = patch.halves()
    patches[0].over(bits[-1])
    patches[1].over(bits[0])
    for k in range(1, len(bits)):
        projs[0].over(bits[-1 - k])
        projs[1].over(bits[k])
        if k + 1 < len(bits):
            projs[0].done()
            projs[1].done()
    up_last = Last(after(up.by_strip(), patches[0].sent))
    pixel_grad = unmix(
        sizes,
        resize,
        w_left,
        w_right,
        after(
            g_patches,
            patches[0].sent,
            patches[1].sent,
            projs[0].sent,
            projs[1].sent,
            up_last.sent,
        ).reshape(group, local_rows, width),
    )
    patches[0].done(pixel_grad)
    patches[1].done(pixel_grad)
    if len(bits) > 1:
        projs[0].done(pixel_grad)
        projs[1].done(pixel_grad)
    s_up = up_last.done(pixel_grad)
    for scatter in patches:
        scatter.part = after(scatter.part, s_up)
    for k in range(1, len(bits)):
        patches[0].over(bits[-1 - k])
        patches[1].over(bits[k])
        if k + 1 < len(bits):
            patches[0].done()
            patches[1].done()
    proj_last = Last(jnp.concatenate([p.by_strip() for p in projs], axis=-1))
    s_proj = proj_last.done()
    if len(bits) > 1:
        patches[0].done(s_proj)
        patches[1].done(s_proj)
    s_patch = Last(jnp.concatenate([p.by_strip() for p in patches], axis=-1)).done()
    pixel_grad = pixel_grad.reshape(pixels.shape)

    s_up = s_up.reshape(blocks, shard, width).transpose(1, 0, 2).reshape(shard, ff)
    own = s_proj[:, 4 * width :].T
    s_query, s_key, s_value, s_out = (
        s_proj[:, i * width : (i + 1) * width] for i in range(4)
    )
    ahead = 8
    behind = 16
    up_at = behind + POS_ROWS

    return (
        block_out,
        pixel_grad,
        s_patch,
        own[behind : behind + BASE * BASE],
        own[0],
        own[1],
        own[2],
        s_query,
        own[3],
        s_key,
        s_value,
        own[4],
        s_out,
        own[ahead],
        own[ahead + 1],
        own[ahead + 2],
        s_up,
        own[up_at : up_at + pieces].reshape(-1),
        s_down,
        own[ahead + 3],
    )


def solution(mesh):
    rows = P(("img", "strip"))
    split_rows = P(("img", "strip"), None)
    split_columns = P(None, ("img", "strip"))
    held = P("img", "strip", None, None)
    return jax.shard_map(
        body,
        mesh=mesh,
        in_specs=(
            held,
            held,
            P(),
            P(),
            P(),
            P(),
            split_rows,
            split_columns,
            rows,
            rows,
            rows,
            split_rows,
            rows,
            split_rows,
            split_rows,
            rows,
            split_rows,
            rows,
            rows,
            rows,
            split_rows,
            rows,
            split_rows,
            rows,
        ),
        out_specs=(
            held,
            held,
            split_rows,
            split_columns,
            rows,
            rows,
            rows,
            split_rows,
            rows,
            split_rows,
            split_rows,
            rows,
            split_rows,
            rows,
            rows,
            rows,
            split_rows,
            rows,
            split_rows,
            rows,
        ),
        check_vma=False,
    )
```

```python
import functools

import jax
import jax.numpy as jnp
import numpy as np
from jax import lax
from jax.experimental import pallas as pl
from jax.experimental.pallas import tpu as pltpu
from jax.sharding import PartitionSpec as P

HEADS = 12
BASE = 7
HIGH_ACCURACY = lax.Precision.HIGHEST
AXES = ("img", "strip")


def bilinear(out_count, in_count):
    source = (np.arange(out_count, dtype=np.float32) + 0.5) * (in_count / out_count) - 0.5
    source = np.clip(source, 0.0, in_count - 1.0)
    target = np.arange(in_count, dtype=np.float32)
    return np.maximum(1.0 - np.abs(source[:, None] - target[None, :]), 0.0).astype(np.float32)


def matmul(left, right):
    return jnp.dot(left, right, preferred_element_type=jnp.float32)


def left_trans(left, right):
    return lax.dot_general(
        left, right, (((0,), (0,)), ((), ())), preferred_element_type=jnp.float32
    )


def right_trans(left, right):
    return lax.dot_general(
        left, right, (((1,), (1,)), ((), ())), preferred_element_type=jnp.float32
    )


f32 = jnp.float32
bf16 = jnp.bfloat16
VMEM_LIMIT = 56 << 20


def params(*semantics):
    return pltpu.CompilerParams(
        dimension_semantics=semantics or None, vmem_limit_bytes=VMEM_LIMIT
    )


def shaped(shape, dtype):
    return jax.ShapeDtypeStruct(shape, dtype)


def cost(light=False):
    flops = 1024 if light else 1 << 32
    return pl.CostEstimate(flops=flops, bytes_accessed=1024, transcendentals=0)


def fill_mixer(mixer, table, size, turned):
    side = table.shape[0]
    span = side * side
    live = lax.broadcasted_iota(jnp.int32, table.shape, 0) < size
    table = jnp.where(live, table, 0.0)
    column = lax.broadcasted_iota(jnp.int32, (side, span), 1)
    row = lax.broadcasted_iota(jnp.int32, (side, span), 0)

    def widen(chosen):
        return lax.dot_general(
            table,
            chosen.astype(f32),
            (((0 if turned else 1,), (0,)), ((), ())),
            precision=HIGH_ACCURACY,
            preferred_element_type=f32,
        )

    wide = widen(column // side == row)
    tall = widen(column % side == row)
    for i in range(side):
        mixer[i * side : (i + 1) * side, :] = (wide[i : i + 1, :] * tall).astype(bf16)


def mix_kernel(sizes_ref, table_ref, pix_ref, out_ref, mixer):
    step = table_ref.shape[0] // sizes_ref[2]
    size = (sizes_ref[pl.program_id(0)] + 1) * step
    fill_mixer(mixer, table_ref[...], size, False)
    span = mixer.shape[0]
    for c in range(pix_ref.shape[-1] // span):
        columns = slice(c * span, (c + 1) * span)
        out_ref[:, columns] = matmul(pix_ref[:, columns], mixer[...]).astype(bf16)


def mix(sizes, resize, pixels):
    group, rows, length = pixels.shape
    side = resize.shape[1]
    span = side * side
    block = pl.BlockSpec((None, rows, length), lambda g, p: (g, 0, 0))
    return pl.pallas_call(
        mix_kernel,
        grid_spec=pltpu.PrefetchScalarGridSpec(
            num_scalar_prefetch=1,
            grid=(group,),
            in_specs=[pl.BlockSpec((None, side, side), lambda g, p: (p[g], 0, 0)), block],
            out_specs=block,
            scratch_shapes=[pltpu.VMEM((span, span), bf16)],
        ),
        out_shape=shaped(pixels.shape, bf16),
        compiler_params=params("arbitrary"),
        cost_estimate=cost(),
        name="mix",
    )(sizes, resize, pixels)


def unmix_kernel(sizes_ref, table_ref, left_ref, right_ref, grad_ref, out_ref, mixer):
    group = grad_ref.shape[0]

    @pl.when(pl.program_id(0) == 0)
    def _():
        step = table_ref.shape[1] // table_ref.shape[0]
        for g in range(group):
            index = sizes_ref[g]
            fill_mixer(mixer.at[g], table_ref[index], (index + 1) * step, True)

    rows = grad_ref.shape[1]
    grad = grad_ref[...].reshape(group * rows, -1)
    g_base = right_trans(grad, side_by_side(left_ref, right_ref)).astype(bf16)
    for g in range(group):
        out_ref[g] = matmul(g_base[g * rows : (g + 1) * rows], mixer[g])


def unmix(sizes, resize, left, right, grad):
    group, rows, width = grad.shape
    side = resize.shape[1]
    span = side * side
    length, columns = left.shape
    return pl.pallas_call(
        unmix_kernel,
        grid_spec=pltpu.PrefetchScalarGridSpec(
            num_scalar_prefetch=1,
            grid=(length // span,),
            in_specs=[
                pl.BlockSpec(resize.shape, lambda c, p: (0, 0, 0)),
                pl.BlockSpec((span, columns), lambda c, p: (c, 0)),
                pl.BlockSpec((span, columns), lambda c, p: (c, 0)),
                pl.BlockSpec((group, rows, width), lambda c, p: (0, 0, 0)),
            ],
            out_specs=pl.BlockSpec((group, rows, span), lambda c, p: (0, 0, c)),
            scratch_shapes=[pltpu.VMEM((group, span, span), bf16)],
        ),
        out_shape=shaped((group, rows, length), f32),
        compiler_params=params("arbitrary"),
        cost_estimate=cost(),
        name="unmix",
    )(sizes, resize, left, right, grad)


def attend_kernel(q_ref, ko_ref, kp_ref, vo_ref, vp_ref, out_ref, lse_ref, *, size, chunk):
    first = lax.broadcasted_iota(jnp.int32, (1, 2 * size), 1) < size
    keys = jnp.concatenate([ko_ref[...], kp_ref[...]], axis=0)
    values = jnp.concatenate([vo_ref[...], vp_ref[...]], axis=0)
    for i in range(q_ref.shape[0] // chunk):
        rows = slice(i * chunk, (i + 1) * chunk)
        query = q_ref[rows, :]
        none = jnp.zeros_like(query)
        outs, sums = [], []
        for e in range(2):
            head = jnp.where(first, query, none) if e == 0 else jnp.where(first, none, query)
            scores = right_trans(head, keys)
            peak = jnp.max(scores, axis=-1, keepdims=True)
            expd = jnp.exp(scores - peak)
            denom = jnp.sum(expd, axis=-1, keepdims=True)
            outs.append(matmul(expd.astype(bf16), values) / denom)
            sums.append(peak + jnp.log(denom))
        out_ref[rows, :] = jnp.where(first, outs[0], outs[1]).astype(bf16)
        lse_ref[rows, :] = jnp.where(first, sums[0], sums[1])


def attend(query, key, key_peer, value, value_peer):
    rows, width = query.shape
    size = width // HEADS
    spec = pl.BlockSpec((rows, 2 * size), lambda h: (0, h))
    return pl.pallas_call(
        functools.partial(attend_kernel, size=size, chunk=min(256, rows)),
        grid=(HEADS // 2,),
        in_specs=[spec] * 5,
        out_specs=[spec] * 2,
        out_shape=[shaped((rows, width), bf16), shaped((rows, width), f32)],
        compiler_params=params("arbitrary"),
        cost_estimate=cost(),
        name="attend",
    )(query, key, key_peer, value, value_peer)


def attend_back_kernel(
    q_ref,
    ko_ref,
    kp_ref,
    vo_ref,
    vp_ref,
    g_ref,
    o_ref,
    lse_ref,
    gq_ref,
    gko_ref,
    gkp_ref,
    gvo_ref,
    gvp_ref,
    *,
    size,
    chunk,
):
    rows = q_ref.shape[0]
    upper = lax.broadcasted_iota(jnp.int32, (2 * size, 1), 0) < size
    first = lax.broadcasted_iota(jnp.int32, (1, 2 * size), 1) < size
    query = q_ref[...]
    grad = g_ref[...]
    query_t = query.astype(f32).T
    grad_t = grad.astype(f32).T
    inner_t = grad_t * o_ref[...].astype(f32).T
    lse_t = lse_ref[...].T
    queries, grads, inners, sums, g_query = [], [], [], [], []
    for e in range(2):
        mine = upper if e == 0 else jnp.logical_not(upper)
        queries.append(jnp.where(mine, query_t, 0.0).astype(bf16))
        grads.append(jnp.where(mine, grad_t, 0.0).astype(bf16))
        inners.append(jnp.sum(inner_t[e * size : (e + 1) * size], axis=0, keepdims=True))
        sums.append(lse_t[e * size : e * size + 1])
        g_query.append(jnp.zeros((size, rows), f32))
    for k_ref, v_ref, gk_ref, gv_ref in (
        (ko_ref, vo_ref, gko_ref, gvo_ref),
        (kp_ref, vp_ref, gkp_ref, gvp_ref),
    ):
        for i in range(k_ref.shape[0] // chunk):
            part = slice(i * chunk, (i + 1) * chunk)
            key = k_ref[part, :]
            value = v_ref[part, :]
            key_t = key.astype(f32).T.astype(bf16)
            g_key, g_value = [], []
            for e in range(2):
                probs = jnp.exp(matmul(key, queries[e]) - sums[e])
                g_scores = (probs * (matmul(value, grads[e]) - inners[e])).astype(bf16)
                g_key.append(matmul(g_scores, query))
                g_value.append(matmul(probs.astype(bf16), grad))
                g_query[e] = g_query[e] + matmul(key_t[e * size : (e + 1) * size], g_scores)
            gk_ref[part, :] = jnp.where(first, g_key[0], g_key[1]).astype(gk_ref.dtype)
            gv_ref[part, :] = jnp.where(first, g_value[0], g_value[1]).astype(gv_ref.dtype)
    gq_ref[...] = jnp.concatenate(g_query, axis=0).T.astype(gq_ref.dtype)


def attend_back(query, key, key_peer, value, value_peer, grad, attended, lse):
    rows, width = query.shape
    size = width // HEADS
    spec = pl.BlockSpec((rows, 2 * size), lambda h: (0, h))
    low, full = shaped((rows, width), bf16), shaped((rows, width), f32)
    return pl.pallas_call(
        functools.partial(attend_back_kernel, size=size, chunk=rows),
        grid=(HEADS // 2,),
        in_specs=[spec] * 8,
        out_specs=[spec] * 5,
        out_shape=[low, full, low, full, low],
        compiler_params=params("arbitrary"),
        cost_estimate=cost(True),
        name="attend_back",
    )(query, key, key_peer, value, value_peer, grad, attended, lse)


def side_by_side(left_ref, right_ref):
    return jnp.concatenate([left_ref[...], right_ref[...]], axis=1)


def whole(shape):
    return pl.BlockSpec(shape, lambda i, s: (0,) * len(shape))


def gather_rows_kernel(at_ref, own_ref, peer_ref, out_ref, rows_ref):
    core = at_ref[0]
    strips, part = own_ref.shape[:2]
    half = out_ref.shape[0]
    for j in range(strips):
        start, count = at_ref[1 + j], at_ref[1 + strips + j]
        for ref, which in ((own_ref, core), (peer_ref, 1 - core)):
            for i in range(part):
                local = which * part + i
                row = start + local - core * half
                here = jnp.logical_and(local < count, jnp.logical_and(row >= 0, row < half))
                rows_ref[jnp.where(here, row, half)] = ref[j, i]
    out_ref[...] = rows_ref[:half]


def gather_rows(at, own, peer, half):
    strips, part, grid, width = own.shape
    out = (half, grid, width)
    return pl.pallas_call(
        gather_rows_kernel,
        grid_spec=pltpu.PrefetchScalarGridSpec(
            num_scalar_prefetch=1,
            grid=(1,),
            in_specs=[whole(own.shape)] * 2,
            out_specs=whole(out),
            scratch_shapes=[pltpu.VMEM((half + 1, grid, width), bf16)],
        ),
        out_shape=shaped(out, bf16),
        compiler_params=params("arbitrary"),
        cost_estimate=cost(),
        name="gather_rows",
    )(at, own, peer)


def spread_rows_kernel(at_ref, own_ref, peer_ref, out_ref, rows_ref):
    core = at_ref[0]
    strips, part = out_ref.shape[:2]
    half = own_ref.shape[0]
    rows_ref[pl.ds(core * half, half)] = own_ref[...]
    rows_ref[pl.ds((1 - core) * half, half)] = peer_ref[...]
    rows_ref[2 * half] = jnp.zeros(rows_ref.shape[1:], bf16)
    for j in range(strips):
        start, count = at_ref[1 + j], at_ref[1 + strips + j]
        for i in range(part):
            local = core * part + i
            out_ref[j, i] = rows_ref[jnp.where(local < count, start + local, 2 * half)]


def spread_rows(at, own, peer, strips, capacity):
    half, grid, width = own.shape
    out = (strips, capacity // 2, grid, width)
    return pl.pallas_call(
        spread_rows_kernel,
        grid_spec=pltpu.PrefetchScalarGridSpec(
            num_scalar_prefetch=1,
            grid=(1,),
            in_specs=[whole(own.shape)] * 2,
            out_specs=whole(out),
            scratch_shapes=[pltpu.VMEM((2 * half + 1, grid, width), bf16)],
        ),
        out_shape=shaped(out, bf16),
        compiler_params=params("arbitrary"),
        cost_estimate=cost(),
        name="spread_rows",
    )(at, own, peer)


def normalise(values):
    centred = values - jnp.mean(values, axis=-1, keepdims=True)
    scale = lax.rsqrt(jnp.mean(centred * centred, axis=-1, keepdims=True) + 1e-06)
    return centred * scale, scale


def norm_back(grad, normed, scale):
    return scale * (
        grad
        - jnp.mean(grad, axis=-1, keepdims=True)
        - normed * jnp.mean(grad * normed, axis=-1, keepdims=True)
    )


def column_sum(values):
    return jnp.sum(values, axis=0, keepdims=True)


PATCH, GAIN1, SHIFT1, QUERY, VALUE, OUT, GAIN2, SHIFT2, DOWN = range(9)
VECTORS = 9
UP_AT = 9
POS_AT = 16
TABLE = 96
POS_ROWS = 64


def patch_kernel(base_ref, left_ref, right_ref, out_ref):
    out_ref[...] = matmul(base_ref[...], side_by_side(left_ref, right_ref)).astype(bf16)


def embed_patches(base, left, right):
    group, rows, length = base.shape
    half = left.shape[1]
    return pl.pallas_call(
        patch_kernel,
        grid=(group,),
        in_specs=[
            pl.BlockSpec((None, rows, length), lambda t: (t, 0, 0)),
            pl.BlockSpec((length, half), lambda t: (0, 0)),
            pl.BlockSpec((length, half), lambda t: (0, 0)),
        ],
        out_specs=pl.BlockSpec((None, rows, 2 * half), lambda t: (t, 0, 0)),
        out_shape=shaped((group, rows, 2 * half), bf16),
        compiler_params=params("arbitrary"),
        cost_estimate=cost(),
        name="embed_patches",
    )(base, left, right)


def enter_kernel(
    at_ref, patches_ref, spread_ref, table_ref, ql_ref, qr_ref, kl_ref, kr_ref, vl_ref, vr_ref,
    embed_ref, in_ref, q_ref, k_ref, v_ref,
):
    def vector(row):
        return table_ref[row : row + 1, :]

    place_rows = jnp.dot(
        spread_ref[...],
        table_ref[POS_AT : POS_AT + POS_ROWS, :],
        precision=HIGH_ACCURACY,
        preferred_element_type=f32,
    )
    embed = patches_ref[...].astype(f32) + vector(PATCH) + place_rows
    embed_ref[...] = embed
    normed, _ = normalise(embed)
    attn_in = (normed * vector(GAIN1) + vector(SHIFT1)).astype(bf16)
    in_ref[...] = attn_in
    query = matmul(attn_in, side_by_side(ql_ref, qr_ref))
    q_ref[...] = ((query + vector(QUERY)) * 0.125).astype(bf16)
    k_ref[...] = matmul(attn_in, side_by_side(kl_ref, kr_ref)).astype(bf16)
    v_ref[...] = (matmul(attn_in, side_by_side(vl_ref, vr_ref)) + vector(VALUE)).astype(bf16)


def enter(at, patches, spread, table, weights, blocks=1):
    rows, width = patches.shape
    block = rows // blocks
    part = pl.BlockSpec((block, width), lambda t, a: (t, 0))
    weight = pl.BlockSpec(weights[0].shape, lambda t, a: (0, 0))
    low = shaped((rows, width), bf16)
    return pl.pallas_call(
        enter_kernel,
        grid_spec=pltpu.PrefetchScalarGridSpec(
            num_scalar_prefetch=1,
            grid=(blocks,),
            in_specs=[
                part,
                pl.BlockSpec((None, block, POS_ROWS), lambda t, a: (a[0], t, 0)),
                pl.BlockSpec(table.shape, lambda t, a: (0, 0)),
                *([weight] * 6),
            ],
            out_specs=[part] * 5,
        ),
        out_shape=[shaped((rows, width), f32), low, low, low, low],
        compiler_params=params("arbitrary"),
        cost_estimate=cost(),
        name="enter",
    )(at, patches, spread, table, *weights)


def mlp_kernel(
    attended_ref, embed_ref, table_ref, ol_ref, or_ref, up_ref, bias_ref, down_ref,
    resid_ref, in_ref, hidden_ref, slope_ref, out_ref, total,
):
    step = pl.program_id(0)

    def vector(row):
        return table_ref[row : row + 1, :]

    @pl.when(step == 0)
    def _():
        resid = (
            embed_ref[...]
            + matmul(attended_ref[...], side_by_side(ol_ref, or_ref))
            + vector(OUT)
        )
        resid_ref[...] = resid
        normed, _ = normalise(resid)
        in_ref[...] = (normed * vector(GAIN2) + vector(SHIFT2)).astype(bf16)
        total[...] = resid + vector(DOWN)

    upper = matmul(in_ref[...], up_ref[...]) + bias_ref[...]
    below = 0.5 + 0.5 * lax.erf(upper * 0.7071067811865476)
    hidden = (upper * below).astype(bf16)
    hidden_ref[...] = hidden
    slope_ref[...] = (below + upper * (0.3989422804014327 * jnp.exp(-0.5 * upper * upper))).astype(
        slope_ref.dtype
    )
    total[...] += matmul(hidden, down_ref[...])

    @pl.when(step == pl.num_programs(0) - 1)
    def _():
        out_ref[...] = total[...].astype(bf16)


def mlp(attended, embed, table, w_out, w_up, b_up, w_down):
    rows, width = embed.shape
    blocks = w_up.shape[0]
    ff = blocks * width
    fixed = pl.BlockSpec((rows, width), lambda t: (0, 0))
    columns = pl.BlockSpec((rows, width), lambda t: (0, t))
    return pl.pallas_call(
        mlp_kernel,
        grid=(blocks,),
        in_specs=[
            fixed,
            fixed,
            pl.BlockSpec(table.shape, lambda t: (0, 0)),
            *([pl.BlockSpec(w_out[0].shape, lambda t: (0, 0))] * 2),
            pl.BlockSpec((None, width, width), lambda t: (t, 0, 0)),
            pl.BlockSpec((1, width), lambda t: (0, t)),
            pl.BlockSpec((width, width), lambda t: (t, 0)),
        ],
        out_specs=[fixed, fixed, columns, columns, fixed],
        out_shape=[
            shaped((rows, width), f32),
            shaped((rows, width), bf16),
            shaped((rows, ff), bf16),
            shaped((rows, ff), bf16),
            shaped((rows, width), bf16),
        ],
        scratch_shapes=[pltpu.VMEM((rows, width), f32)],
        compiler_params=params("arbitrary"),
        cost_estimate=cost(),
        name="mlp",
    )(attended, embed, table, *w_out, w_up, b_up, w_down)


def mlp_back_kernel(
    g_ref, slope_ref, resid_ref, table_ref, ol_ref, or_ref, up_ref, down_ref,
    upper_ref, resid_grad_ref, low_ref, att_ref, sums_ref, total,
):
    step = pl.program_id(0)

    @pl.when(step == 0)
    def _():
        total[...] = jnp.zeros_like(total)
        sums_ref[...] = jnp.zeros_like(sums_ref)

    g_upper = slope_ref[...].astype(f32) * right_trans(g_ref[...], down_ref[...])
    sums_ref[pl.ds(8 + step, 1), :] = column_sum(g_upper)
    g_upper_low = g_upper.astype(bf16)
    upper_ref[...] = g_upper_low
    total[...] += right_trans(g_upper_low, up_ref[...])

    @pl.when(step == pl.num_programs(0) - 1)
    def _():
        grad = total[...]
        g_out = g_ref[...].astype(f32)
        normed, scale = normalise(resid_ref[...])
        g_resid = g_out + norm_back(grad * table_ref[GAIN2 : GAIN2 + 1, :], normed, scale)
        resid_grad_ref[...] = g_resid
        g_resid_low = g_resid.astype(bf16)
        low_ref[...] = g_resid_low
        att_ref[...] = right_trans(g_resid_low, side_by_side(ol_ref, or_ref)).astype(bf16)
        sums_ref[0:1, :] = column_sum(g_resid)
        sums_ref[1:2, :] = column_sum(grad * normed)
        sums_ref[2:3, :] = column_sum(grad)
        sums_ref[3:4, :] = column_sum(g_out)


def mlp_back(g_out, slope, resid, table, w_out, w_up, w_down):
    rows, width = g_out.shape
    blocks = w_up.shape[0]
    ff = blocks * width
    fixed = pl.BlockSpec((rows, width), lambda t: (0, 0))
    columns = pl.BlockSpec((rows, width), lambda t: (0, t))
    sums = (8 + 8 * (-(-blocks // 8)), width)
    return pl.pallas_call(
        mlp_back_kernel,
        grid=(blocks,),
        in_specs=[
            fixed,
            columns,
            fixed,
            pl.BlockSpec(table.shape, lambda t: (0, 0)),
            *([pl.BlockSpec(w_out[0].shape, lambda t: (0, 0))] * 2),
            pl.BlockSpec((None, width, width), lambda t: (t, 0, 0)),
            pl.BlockSpec((width, width), lambda t: (t, 0)),
        ],
        out_specs=[columns, fixed, fixed, fixed, pl.BlockSpec(sums, lambda t: (0, 0))],
        out_shape=[
            shaped((rows, ff), bf16),
            shaped((rows, width), f32),
            shaped((rows, width), bf16),
            shaped((rows, width), bf16),
            shaped(sums, f32),
        ],
        scratch_shapes=[pltpu.VMEM((rows, width), f32)],
        compiler_params=params("arbitrary"),
        cost_estimate=cost(True),
        name="mlp_back",
    )(g_out, slope, resid, table, *w_out, w_up, w_down)


def leave_kernel(
    at_ref, gq_ref, gk_ref, gkp_ref, gv_ref, gvp_ref, embed_ref, resid_ref, spread_ref, table_ref,
    ql_ref, qr_ref, kl_ref, kr_ref, vl_ref, vr_ref, q_ref, k_ref, v_ref, out_ref, sums_ref, pos_ref,
):
    @pl.when(pl.program_id(0) == 0)
    def _():
        sums_ref[...] = jnp.zeros_like(sums_ref)
        pos_ref[...] = jnp.zeros_like(pos_ref)

    g_query = gq_ref[...].astype(f32) * 0.125
    g_query_low = g_query.astype(bf16)
    g_key_low = (gk_ref[...] + gkp_ref[...].astype(f32)).astype(bf16)
    g_value_low = (gv_ref[...] + gvp_ref[...].astype(f32)).astype(bf16)
    q_ref[...] = g_query_low
    k_ref[...] = g_key_low
    v_ref[...] = g_value_low
    grad = (
        right_trans(g_query_low, side_by_side(ql_ref, qr_ref))
        + right_trans(g_key_low, side_by_side(kl_ref, kr_ref))
        + right_trans(g_value_low, side_by_side(vl_ref, vr_ref))
    )
    normed, scale = normalise(embed_ref[...])
    g_embed = resid_ref[...] + norm_back(grad * table_ref[GAIN1 : GAIN1 + 1, :], normed, scale)
    out_ref[...] = g_embed.astype(bf16)
    sums_ref[0:1, :] += column_sum(g_embed)
    sums_ref[1:2, :] += column_sum(grad * normed)
    sums_ref[2:3, :] += column_sum(grad)
    sums_ref[3:4, :] += column_sum(g_query)
    sums_ref[4:5, :] += column_sum(g_value_low.astype(f32))
    pos_ref[...] += jnp.dot(
        spread_ref[...], g_embed, precision=HIGH_ACCURACY, preferred_element_type=f32
    )


def leave(
    at, g_query, g_key, g_key_peer, g_value, g_value_peer, embed, g_resid, spread, table,
    weights, blocks=1,
):
    rows, width = embed.shape
    block = rows // blocks
    part = pl.BlockSpec((block, width), lambda t, a: (t, 0))
    weight = pl.BlockSpec(weights[0].shape, lambda t, a: (0, 0))
    low = shaped((rows, width), bf16)
    return pl.pallas_call(
        leave_kernel,
        grid_spec=pltpu.PrefetchScalarGridSpec(
            num_scalar_prefetch=1,
            grid=(blocks,),
            in_specs=[part] * 7
            + [
                pl.BlockSpec((None, POS_ROWS, block), lambda t, a: (a[0], 0, t)),
                pl.BlockSpec(table.shape, lambda t, a: (0, 0)),
                *([weight] * 6),
            ],
            out_specs=[part] * 4
            + [
                pl.BlockSpec((8, width), lambda t, a: (0, 0)),
                pl.BlockSpec((POS_ROWS, width), lambda t, a: (0, 0)),
            ],
        ),
        out_shape=[low] * 4 + [shaped((8, width), f32), shaped((POS_ROWS, width), f32)],
        compiler_params=params("arbitrary"),
        cost_estimate=cost(),
        name="leave",
    )(
        at, g_query, g_key, g_key_peer, g_value, g_value_peer, embed, g_resid, spread, table,
        *weights,
    )


def weight_grad_kernel(at_ref, left_ref, right_ref, send_ref, keep_ref, *scratch):
    core = at_ref[0]
    group, rows, _ = send_ref.shape
    if not scratch:
        for ref, which in ((send_ref, 1 - core), (keep_ref, core)):
            for h in range(group):
                columns = pl.ds(pl.multiple_of((2 * h + which) * rows, 128), rows)
                ref[h] = left_trans(left_ref[:, columns], right_ref[...]).astype(bf16)
        return
    total = scratch[0]
    total[...] = left_trans(left_ref[...], right_ref[...])
    for h in range(group):
        sent = pl.multiple_of((2 * h + 1 - core) * rows, 8)
        kept = pl.multiple_of((2 * h + core) * rows, 8)
        send_ref[h] = total[pl.ds(sent, rows), :].astype(bf16)
        keep_ref[h] = total[pl.ds(kept, rows), :].astype(bf16)


def weight_grad(at, left, right, his, light=False):
    tokens, m = left.shape
    n = right.shape[1]
    rows = m // (2 * his)
    tall = min(m, 768)
    h = tall // (2 * rows)
    wide = 768
    blocks = n // wide
    out = pl.BlockSpec((h, None, rows, wide), lambda i, j, a: (i, j, 0, 0))
    shape = (his, blocks, rows, wide)
    return pl.pallas_call(
        weight_grad_kernel,
        grid_spec=pltpu.PrefetchScalarGridSpec(
            num_scalar_prefetch=1,
            grid=(m // tall, blocks),
            in_specs=[
                pl.BlockSpec((tokens, tall), lambda i, j, a: (0, i)),
                pl.BlockSpec((tokens, wide), lambda i, j, a: (0, j)),
            ],
            out_specs=[out, out],
            scratch_shapes=[pltpu.VMEM((tall, wide), f32)] if rows % 128 else [],
        ),
        out_shape=[shaped(shape, bf16)] * 2,
        compiler_params=params("arbitrary", "arbitrary"),
        cost_estimate=cost(light),
        name="weight_grad",
    )(at, left, right)


def proj_grad_kernel(
    at_ref, in_ref, att_ref, gq_ref, gk_ref, gv_ref, go_ref, small_ref, send_ref, keep_ref, total
):
    core = at_ref[0]
    his, rows, length = send_ref.shape
    width = gq_ref.shape[1]
    turned = [
        small_ref[:, i * 128 : (i + 1) * 128].T for i in range(width // 128)
    ]
    small = jnp.concatenate(turned, axis=0)
    pairs = ((in_ref, gq_ref), (in_ref, gk_ref), (in_ref, gv_ref), (att_ref, go_ref), None)
    for i, pair in enumerate(pairs):
        if pair is None:
            columns = slice(i * width, length)
            total[:, : length - i * width] = small
        else:
            columns = slice(i * width, (i + 1) * width)
            total[...] = left_trans(pair[0][...], pair[1][...])
        size = columns.stop - columns.start
        for h in range(his):
            sent = pl.multiple_of((2 * h + 1 - core) * rows, 8)
            kept = pl.multiple_of((2 * h + core) * rows, 8)
            send_ref[h, :, columns] = total[pl.ds(sent, rows), :size].astype(bf16)
            keep_ref[h, :, columns] = total[pl.ds(kept, rows), :size].astype(bf16)


def proj_grad(at, attn_in, attended, g_query, g_key, g_value, g_resid, small, his):
    tokens, width = attn_in.shape
    rows = width // (2 * his)
    out = (his, rows, 4 * width + small.shape[0])
    return pl.pallas_call(
        proj_grad_kernel,
        grid_spec=pltpu.PrefetchScalarGridSpec(
            num_scalar_prefetch=1,
            grid=(1,),
            in_specs=[whole(attn_in.shape)] * 6 + [whole(small.shape)],
            out_specs=[whole(out)] * 2,
            scratch_shapes=[pltpu.VMEM((width, width), f32)],
        ),
        out_shape=[shaped(out, bf16)] * 2,
        compiler_params=params("arbitrary"),
        cost_estimate=cost(),
        name="proj_grad",
    )(at, attn_in, attended, g_query, g_key, g_value, g_resid, small)


class Place:
    def __init__(self, group):
        self.group = group
        self.images = lax.axis_size("img")
        self.strips = lax.axis_size("strip")
        assert group == 2 and self.strips == 4
        self.img = lax.axis_index("img")
        self.core = self.img % 2
        self.z = lax.axis_index("strip")
        self.bits = [1 << k for k in range(1, self.images.bit_length() - 1)]
        assert self.images == 2 << len(self.bits)

    def flat(self, img, z):
        return img * self.strips + z

    def swap_core(self, values):
        return lax.ppermute(values, "img", [(i, i ^ 1) for i in range(self.images)])

    def across_img(self, values, bit):
        return lax.ppermute(values, "img", [(i, i ^ bit) for i in range(self.images)])

    def along_z(self, values, r):
        return lax.ppermute(values, "strip", [(z, z ^ r) for z in range(self.strips)])


def pick(values, index, axis=0):
    return lax.dynamic_index_in_dim(values, index, axis, keepdims=False)


def after(values, *others):
    return lax.optimization_barrier((values,) + others)[0]


def collect(values, *others):
    values = tuple(values)
    return lax.optimization_barrier(values + others)[: len(values)]


def exchange(values):
    return lax.all_to_all(values, "strip", 0, 0, tiled=True)


class Gather:
    def __init__(self, place, held, bits=()):
        self.place = place
        self.held = held
        self.wide = None
        self.bits = list(bits)

    def halves(self):
        middle = self.held.shape[-1] // 2
        return [
            Gather(self.place, self.held[..., columns], self.bits)
            for columns in (slice(0, middle), slice(middle, None))
        ]

    def widen(self, *others):
        held = after(self.held, *others) if others else self.held
        self.wide = jnp.broadcast_to(held, (self.place.strips,) + held.shape)

    def along_z(self, *others):
        if self.wide is None:
            self.widen(*others)
        self.start = after(self.wide, *others) if others else self.wide
        self.held = exchange(self.start)

    def z_done(self, *others):
        (self.held,) = collect([self.held], *others)

    def over(self, bit, *others):
        if others:
            self.held = after(self.held, *others)
        self.bit = bit
        self.got = self.place.across_img(self.held, bit)

    def done(self, *others):
        (got,) = collect([self.got], *others)
        self.bits = sorted(self.bits + [self.bit], reverse=True)
        axis = self.bits.index(self.bit)
        self.held = join(self.held, got, axis, (self.place.img // self.bit) % 2)

    def last(self, *others):
        if others:
            self.held = after(self.held, *others)
        self.other = self.place.swap_core(self.held)

    def last_done(self, *others):
        (self.other,) = collect([self.other], *others)

    def rows(self, start=0, stop=None):
        axis = len(self.bits)
        full = join(self.held[..., start:stop, :], self.other[..., start:stop, :], axis, self.place.core)
        return full.reshape((-1,) + full.shape[-2:])


def join(mine, other, axis, at):
    spot = [1] * (mine.ndim + 1)
    spot[axis] = 2
    where = jnp.arange(2, dtype=jnp.int32).reshape(spot) == at
    return jnp.where(where, jnp.expand_dims(mine, axis), jnp.expand_dims(other, axis))


def add_low(a, b):
    return (a.astype(f32) + b.astype(f32)).astype(bf16)


class Scatter:
    def __init__(self, place, send, keep):
        self.place = place
        self.bits = place.bits[::-1]
        self.send = send
        self.keep = keep

    def first(self):
        self.got = self.place.swap_core(self.send)

    def first_done(self, *others):
        (got,) = collect([self.got], *others)
        shape = (2,) * len(self.bits) + self.send.shape[1:]
        self.part = add_low(self.keep.reshape(shape), got.reshape(shape))

    def halves(self, middle=None):
        axis = self.part.ndim - 1
        parts = []
        if middle is None:
            middle = self.part.shape[axis] // 2
        for start, stop in ((0, middle), (middle, self.part.shape[axis])):
            one = Scatter(self.place, None, None)
            one.part = lax.slice_in_dim(self.part, start, stop, axis=axis)
            parts.append(one)
        return parts

    def over(self, bit):
        self.bit = bit
        axis = self.bits.index(bit)
        self.sent = pick(self.part, 1 - (self.place.img // bit) % 2, axis)
        self.got = self.place.across_img(self.sent, bit)

    def done(self, *others):
        (self.got,) = collect([self.got], *others)
        axis = self.bits.index(self.bit)
        self.part = add_low(pick(self.part, (self.place.img // self.bit) % 2, axis), self.got)
        self.bits = [b for b in self.bits if b != self.bit]

    def by_strip(self):
        blocks, rows, columns = self.part.shape
        part = self.part.reshape(blocks, self.place.strips, -1, columns)
        return part.transpose(1, 0, 2, 3).reshape(self.place.strips, -1, columns)


class Last:
    def __init__(self, values):
        self.sent = values.astype(bf16)
        self.got = exchange(self.sent)

    def done(self, *others):
        (self.got,) = collect([self.got], *others)
        return jnp.sum(self.got.astype(f32), axis=0)


def split_rows(place, values):
    images, rows = values.shape[:2]
    values = values.reshape((images, 2, rows // 2) + values.shape[2:])
    return pick(values, place.core, 1), pick(values, 1 - place.core, 1)


def pair_up(place, mine, other):
    return jnp.where(
        place.core == 0, jnp.concatenate([mine, other]), jnp.concatenate([other, mine])
    )


def from_chip(place, moved, shape):
    images, rows = shape[0], shape[1] // 2
    moved = moved.reshape((2, images) + moved.shape[1:])
    mine, sent = pick(moved, place.core), pick(moved, 1 - place.core)
    got = place.swap_core(sent)
    low = jnp.where(place.core == 0, mine, got)
    high = jnp.where(place.core == 0, got, mine)
    return jnp.concatenate([low, high], axis=1)


def body(
    pixels,
    cotangent,
    resize,
    patch_index,
    slot_image,
    strip_rows,
    patch_weight,
    pos_grid,
    patch_bias,
    attention_norm_gain,
    attn_shift,
    query_weight,
    query_bias,
    key_weight,
    value_weight,
    value_bias,
    out_weight,
    out_bias,
    mlp_gain,
    mlp_shift,
    up_weight,
    up_bias,
    down_weight,
    down_bias,
):
    group, capacity, grid, pixel_len = pixels.shape
    width = cotangent.shape[3]
    ff = up_weight.shape[1]
    local_rows = capacity * grid
    tokens = group * local_rows
    place = Place(group)
    devices = place.images * place.strips
    his = place.images // 2
    first_slot = place.img * group
    shard = patch_bias.shape[0]
    ups = up_bias.shape[0]
    columns = width // 2
    bits = place.bits

    vectors = (
        patch_bias,
        attention_norm_gain,
        attn_shift,
        query_bias,
        value_bias,
        out_bias,
        mlp_gain,
        mlp_shift,
        down_bias,
    )
    pieces = ups // shard
    small = jnp.concatenate(
        [
            jnp.stack(vectors + tuple(up_bias[i * shard : (i + 1) * shard] for i in range(pieces))),
            jnp.zeros((POS_AT - VECTORS - pieces, shard), bf16),
            pos_grid,
            jnp.zeros((TABLE - POS_AT - BASE * BASE, shard), bf16),
        ]
    )
    lane = width // (TABLE // 16)
    small = jnp.pad(small, ((0, 0), (0, lane - shard))).reshape(-1, 16, lane)
    small = jnp.concatenate(list(small), axis=1)
    proj = jnp.concatenate([query_weight, key_weight, value_weight, out_weight, small])

    size_count = resize.shape[0]
    slot_ids = lax.dynamic_slice_in_dim(slot_image, first_slot, group)
    picked = slot_ids[:, None] == jnp.arange(patch_index.shape[0], dtype=jnp.int32)[None, :]
    size_index = jnp.sum(jnp.where(picked, patch_index[None, :], 0), axis=1)
    sizes = jnp.append(size_index, size_count).astype(jnp.int32)
    half = grid // 2
    image_counts = pick(strip_rows, (place.img // 2) * 2 * group + place.z)
    starts = jnp.cumsum(image_counts) - image_counts
    at = jnp.concatenate([place.core[None], starts, image_counts]).astype(jnp.int32)

    spread = bilinear(grid, BASE)
    spread = (spread[:, None, :, None] * spread[None, :, None, :]).reshape(2, half * grid, -1)
    spread = np.pad(spread, ((0, 0), (0, 0), (0, POS_ROWS - BASE * BASE)))
    spread_t = jnp.asarray(np.ascontiguousarray(spread.transpose(0, 2, 1)))
    spread = jnp.asarray(spread)

    whole_patch, packed = Gather(place, patch_weight), Gather(place, proj)
    blocks = ff // width
    both = Gather(
        place,
        jnp.concatenate(
            [down_weight]
            + [up_weight[:, i * width : (i + 1) * width] for i in range(blocks)]
        ),
    )
    whole_patch.along_z()
    base_pixels = mix(after(sizes, at), resize, pixels.reshape(group, local_rows, pixel_len))
    whole_patch.z_done(base_pixels)
    left, right = whole_patch.halves()
    for k in range(len(bits)):
        if k == len(bits) - 1:
            packed.along_z(left.held, right.held)
        left.over(bits[k])
        right.over(bits[-1 - k])
        if k == len(bits) - 1:
            cot_mine, cot_sent = split_rows(place, after(cotangent, packed.start))
            cot_got = place.swap_core(cot_sent)
            cot_pair = pair_up(place, cot_mine, cot_got)
            both.widen(packed.start)
            left.done(cot_pair, both.wide)
            right.done(cot_pair, both.wide)
        else:
            left.done()
            right.done()
    packed.z_done()
    left.last(packed.held, right.held)
    right.last(packed.held, left.held)
    left.last_done()
    right.last_done()
    w_left, w_right = left.rows().reshape(-1, columns), right.rows().reshape(-1, columns)
    packs = packed.halves()
    packs[0].over(bits[0], left.other)
    packs[1].over(bits[-1], left.other)
    both.along_z(packed.held)
    patches = embed_patches(base_pixels, w_left, w_right).reshape(group, capacity, grid, width)
    packs[0].done(patches)
    packs[1].done(patches)
    for k in range(1, len(bits)):
        packs[0].over(bits[k])
        packs[1].over(bits[-1 - k])
        packs[0].done()
        packs[1].done()
    both.z_done(patches)
    downs_w = Gather(place, both.held[:, : down_weight.shape[0]], both.bits)
    ups_w = Gather(place, both.held[:, down_weight.shape[0] :], both.bits)
    patch_mine, patch_sent = split_rows(place, after(patches, both.held))
    patch_got = place.swap_core(patch_sent)
    patch_pair = pair_up(place, patch_mine, patch_got)
    patch_moved = exchange(patch_pair)
    packs[0].last(patch_pair)
    packs[1].last(patch_pair)
    ups_w.over(bits[-1], packs[0].held, packs[1].held)
    downs_w.over(bits[0], packs[0].held, packs[1].held)
    for k in range(1, len(bits) - 1):
        ups_w.done()
        downs_w.done()
        ups_w.over(bits[-1 - k])
        downs_w.over(bits[k])

    halves = [
        [p.rows(i * shard, (i + 1) * shard).reshape(width, columns) for p in packs]
        for i in range(4)
    ]
    in_weights = [*halves[0], *halves[1], *halves[2]]
    w_out = halves[3]
    flat = jnp.concatenate([p.rows(4 * shard) for p in packs], axis=-1)
    table = (
        flat.reshape(devices, 16, TABLE // 16, lane)[..., :shard]
        .transpose(2, 1, 0, 3)
        .reshape(TABLE, width)
        .astype(f32)
    )
    b_up = (
        table[UP_AT : UP_AT + pieces]
        .reshape(pieces, devices, shard)
        .transpose(1, 0, 2)
        .reshape(1, ff)
    )
    (patch_moved,) = collect([patch_moved], table, b_up, cot_pair, *in_weights, *w_out)
    ups_w.done(patch_moved)
    downs_w.done(patch_moved)
    patch_peer = place.swap_core(patch_moved)
    patches = gather_rows(at, patch_moved, patch_peer, half).reshape(-1, width)
    if len(bits) > 1:
        ups_w.over(bits[0], patch_moved)
        downs_w.over(bits[-1], patch_moved)
    cot_moved = exchange(after(cot_pair, patch_moved))

    embed, attn_in, query, key, value = enter(at, patches, spread, table, in_weights)
    if len(bits) > 1:
        ups_w.done(query)
        downs_w.done(query)
    (cot_moved,) = collect([cot_moved], query)
    key_peer = place.swap_core(after(key, ups_w.held, downs_w.held, cot_moved))
    value_peer = place.swap_core(after(value, ups_w.held, downs_w.held, cot_moved))
    ups_w.last(key_peer, value_peer)
    downs_w.last(key_peer, value_peer)
    cot_peer = place.swap_core(after(cot_moved, key_peer, value_peer))
    attended, lse = attend(query, key, key_peer, value, value_peer)
    ups_w.last_done(attended)
    downs_w.last_done(attended)
    (cot_peer,) = collect([cot_peer], attended)
    w_up = (
        ups_w.rows()
        .reshape(devices, blocks, shard, width)
        .transpose(1, 0, 2, 3)
        .reshape(blocks, width, width)
    )
    w_down = downs_w.rows().reshape(ff, width)
    resid, mlp_in, hidden, slope, final = mlp(attended, embed, table, w_out, w_up, b_up, w_down)
    final_peer = place.swap_core(final)
    g_out = gather_rows(after(at, final), cot_moved, cot_peer, half).reshape(-1, width)

    early, late = bits[: len(bits) // 2], bits[len(bits) // 2 :][::-1]
    down = Scatter(place, *weight_grad(at, hidden, g_out, his))
    (final_peer,) = collect([final_peer], down.send)
    down.send = after(down.send, final_peer)
    down.first()
    image = (half, grid, width)
    final_pieces = spread_rows(
        at, final.reshape(image), final_peer.reshape(image), place.strips, capacity
    )
    down.first_done(final_pieces)
    for bit in late[:-1]:
        down.over(bit)
        down.done()
    down.over(late[-1])
    final_moved = exchange(after(final_pieces, down.sent))
    g_upper, g_resid, g_resid_low, g_att, sums_two = mlp_back(
        after(g_out, final_pieces, down.sent), slope, resid, table, w_out, w_up, w_down
    )
    g_query, g_key, g_key_peer, g_value, g_value_peer = attend_back(
        query, key, key_peer, value, value_peer, g_att, attended, lse
    )
    down.done(g_query)
    (final_moved,) = collect([final_moved], g_query)
    g_key_got = place.swap_core(after(g_key_peer, down.part, final_moved))
    g_value_got = place.swap_core(after(g_value_peer, down.part, final_moved))
    for bit in early[:-1]:
        down.over(bit)
        down.done()
    if early:
        down.over(early[-1])
    up = Scatter(
        place, *weight_grad(at, mlp_in, after(g_upper, g_query, down.sent, final_moved), his)
    )
    g_key_got, g_value_got = collect([g_key_got, g_value_got], up.send)
    up.send = after(up.send, g_key_got, g_value_got)
    up.first()
    g_query, g_key, g_value, g_embed, sums_one, g_pos = leave(
        at,
        after(g_query, up.send),
        g_key,
        g_key_got,
        g_value,
        g_value_got,
        embed,
        g_resid,
        spread_t,
        table,
        in_weights,
    )
    g_embed_peer = place.swap_core(g_embed)
    pieces_back = spread_rows(
        at,
        g_embed.reshape(image),
        g_embed_peer.reshape(image),
        place.strips,
        capacity,
    )
    back = exchange(pieces_back)
    up.first_done(pieces_back)
    for bit in late[:-1]:
        up.over(bit)
        up.done()
    up.over(late[-1])
    up_sums = (
        sums_two[8 : 8 + blocks]
        .reshape(devices, pieces, shard)
        .transpose(1, 0, 2)
        .reshape(pieces, width)
    )
    small = jnp.concatenate([sums_one, sums_two[:8], g_pos, up_sums])
    small = jnp.pad(small, ((0, 128 - small.shape[0]), (0, 0)))
    block_out = from_chip(place, after(final_moved, pieces_back), cotangent.shape)
    proj = Scatter(
        place,
        *(
            part[:, None]
            for part in proj_grad(
                after(at, pieces_back),
                attn_in,
                attended,
                g_query,
                g_key,
                g_value,
                g_resid_low,
                small,
                his,
            )
        ),
    )
    back, up.got, down.got = collect([back, up.got, down.got], proj.send, block_out)
    if early:
        down.done()
    up.done()
    proj.send = after(proj.send, back)
    proj.first()
    for bit in early[:-1]:
        up.over(bit)
        up.done()
    if early:
        up.part = after(up.part, back)
        up.over(early[-1])
    down_last = Last(after(down.by_strip(), back))
    g_patches = from_chip(place, back, cotangent.shape).reshape(tokens, width)
    proj.first_done(g_patches)
    projs = proj.halves(2 * width)
    projs[0].over(bits[-1])
    projs[1].over(bits[0])
    patch = Scatter(
        place,
        *weight_grad(
            at,
            base_pixels.reshape(tokens, pixel_len),
            after(g_patches, projs[0].sent, projs[1].sent, down_last.sent),
            his,
        ),
    )
    projs[0].done(patch.send)
    projs[1].done(patch.send)
    if early:
        up.done(patch.send)
    s_down = down_last.done(patch.send)
    patch.send = after(patch.send, projs[0].got, projs[1].got, up.got, down_last.got)
    patch.first()
    patch.first_done()
    patches = patch.halves()
    patches[0].over(bits[-1])
    patches[1].over(bits[0])
    for k in range(1, len(bits)):
        projs[0].over(bits[-1 - k])
        projs[1].over(bits[k])
        if k + 1 < len(bits):
            projs[0].done()
            projs[1].done()
    up_last = Last(after(up.by_strip(), patches[0].sent))
    pixel_grad = unmix(
        sizes,
        resize,
        w_left,
        w_right,
        after(
            g_patches,
            patches[0].sent,
            patches[1].sent,
            projs[0].sent,
            projs[1].sent,
            up_last.sent,
        ).reshape(group, local_rows, width),
    )
    patches[0].done(pixel_grad)
    patches[1].done(pixel_grad)
    if len(bits) > 1:
        projs[0].done(pixel_grad)
        projs[1].done(pixel_grad)
    s_up = up_last.done(pixel_grad)
    for scatter in patches:
        scatter.part = after(scatter.part, s_up)
    for k in range(1, len(bits)):
        patches[0].over(bits[-1 - k])
        patches[1].over(bits[k])
        if k + 1 < len(bits):
            patches[0].done()
            patches[1].done()
    proj_last = Last(jnp.concatenate([p.by_strip() for p in projs], axis=-1))
    s_proj = proj_last.done()
    if len(bits) > 1:
        patches[0].done(s_proj)
        patches[1].done(s_proj)
    s_patch = Last(jnp.concatenate([p.by_strip() for p in patches], axis=-1)).done()
    pixel_grad = pixel_grad.reshape(pixels.shape)

    s_up = s_up.reshape(blocks, shard, width).transpose(1, 0, 2).reshape(shard, ff)
    own = s_proj[:, 4 * width :].T
    s_query, s_key, s_value, s_out = (
        s_proj[:, i * width : (i + 1) * width] for i in range(4)
    )
    ahead = 8
    behind = 16
    up_at = behind + POS_ROWS

    return (
        block_out,
        pixel_grad,
        s_patch,
        own[behind : behind + BASE * BASE],
        own[0],
        own[1],
        own[2],
        s_query,
        own[3],
        s_key,
        s_value,
        own[4],
        s_out,
        own[ahead],
        own[ahead + 1],
        own[ahead + 2],
        s_up,
        own[up_at : up_at + pieces].reshape(-1),
        s_down,
        own[ahead + 3],
    )


def solution(mesh):
    rows = P(("img", "strip"))
    split_rows = P(("img", "strip"), None)
    split_columns = P(None, ("img", "strip"))
    held = P("img", "strip", None, None)
    return jax.shard_map(
        body,
        mesh=mesh,
        in_specs=(
            held,
            held,
            P(),
            P(),
            P(),
            P(),
            split_rows,
            split_columns,
            rows,
            rows,
            rows,
            split_rows,
            rows,
            split_rows,
            split_rows,
            rows,
            split_rows,
            rows,
            rows,
            rows,
            split_rows,
            rows,
            split_rows,
            rows,
        ),
        out_specs=(
            held,
            held,
            split_rows,
            split_columns,
            rows,
            rows,
            rows,
            split_rows,
            rows,
            split_rows,
            split_rows,
            rows,
            split_rows,
            rows,
            rows,
            rows,
            split_rows,
            rows,
            split_rows,
            rows,
        ),
        check_vma=False,
    )
```

```python
import functools

import jax
import jax.numpy as jnp
import numpy as np
from jax import lax
from jax.experimental import pallas as pl
from jax.experimental.pallas import tpu as pltpu
from jax.sharding import PartitionSpec as P

HEADS = 12
BASE = 7
HIGH_ACCURACY = lax.Precision.HIGHEST
AXES = ("img", "strip")


def bilinear(out_count, in_count):
    source = (np.arange(out_count, dtype=np.float32) + 0.5) * (in_count / out_count) - 0.5
    source = np.clip(source, 0.0, in_count - 1.0)
    target = np.arange(in_count, dtype=np.float32)
    return np.maximum(1.0 - np.abs(source[:, None] - target[None, :]), 0.0).astype(np.float32)


def matmul(left, right):
    return jnp.dot(left, right, preferred_element_type=jnp.float32)


def left_trans(left, right):
    return lax.dot_general(
        left, right, (((0,), (0,)), ((), ())), preferred_element_type=jnp.float32
    )


def right_trans(left, right):
    return lax.dot_general(
        left, right, (((1,), (1,)), ((), ())), preferred_element_type=jnp.float32
    )


f32 = jnp.float32
bf16 = jnp.bfloat16
VMEM_LIMIT = 56 << 20


def params(*semantics):
    return pltpu.CompilerParams(
        dimension_semantics=semantics or None, vmem_limit_bytes=VMEM_LIMIT
    )


def shaped(shape, dtype):
    return jax.ShapeDtypeStruct(shape, dtype)


def cost(light=False):
    flops = 1024 if light else 1 << 32
    return pl.CostEstimate(flops=flops, bytes_accessed=1024, transcendentals=0)


def fill_mixer(mixer, table, size, turned):
    side = table.shape[0]
    span = side * side
    live = lax.broadcasted_iota(jnp.int32, table.shape, 0) < size
    table = jnp.where(live, table, 0.0)
    column = lax.broadcasted_iota(jnp.int32, (side, span), 1)
    row = lax.broadcasted_iota(jnp.int32, (side, span), 0)

    def widen(chosen):
        return lax.dot_general(
            table,
            chosen.astype(f32),
            (((0 if turned else 1,), (0,)), ((), ())),
            precision=HIGH_ACCURACY,
            preferred_element_type=f32,
        )

    wide = widen(column // side == row)
    tall = widen(column % side == row)
    for i in range(side):
        mixer[i * side : (i + 1) * side, :] = (wide[i : i + 1, :] * tall).astype(bf16)


def mix_kernel(sizes_ref, table_ref, pix_ref, out_ref, mixer):
    step = table_ref.shape[0] // sizes_ref[2]
    size = (sizes_ref[pl.program_id(0)] + 1) * step
    fill_mixer(mixer, table_ref[...], size, False)
    span = mixer.shape[0]
    for c in range(pix_ref.shape[-1] // span):
        columns = slice(c * span, (c + 1) * span)
        out_ref[:, columns] = matmul(pix_ref[:, columns], mixer[...]).astype(bf16)


def mix(sizes, resize, pixels):
    group, rows, length = pixels.shape
    side = resize.shape[1]
    span = side * side
    block = pl.BlockSpec((None, rows, length), lambda g, p: (g, 0, 0))
    return pl.pallas_call(
        mix_kernel,
        grid_spec=pltpu.PrefetchScalarGridSpec(
            num_scalar_prefetch=1,
            grid=(group,),
            in_specs=[pl.BlockSpec((None, side, side), lambda g, p: (p[g], 0, 0)), block],
            out_specs=block,
            scratch_shapes=[pltpu.VMEM((span, span), bf16)],
        ),
        out_shape=shaped(pixels.shape, bf16),
        compiler_params=params("arbitrary"),
        cost_estimate=cost(),
        name="mix",
    )(sizes, resize, pixels)


def unmix_kernel(sizes_ref, table_ref, left_ref, right_ref, grad_ref, out_ref, mixer):
    group = grad_ref.shape[0]

    @pl.when(pl.program_id(0) == 0)
    def _():
        step = table_ref.shape[1] // table_ref.shape[0]
        for g in range(group):
            index = sizes_ref[g]
            fill_mixer(mixer.at[g], table_ref[index], (index + 1) * step, True)

    rows = grad_ref.shape[1]
    grad = grad_ref[...].reshape(group * rows, -1)
    g_base = right_trans(grad, side_by_side(left_ref, right_ref)).astype(bf16)
    for g in range(group):
        out_ref[g] = matmul(g_base[g * rows : (g + 1) * rows], mixer[g])


def unmix(sizes, resize, left, right, grad):
    group, rows, width = grad.shape
    side = resize.shape[1]
    span = side * side
    length, columns = left.shape
    return pl.pallas_call(
        unmix_kernel,
        grid_spec=pltpu.PrefetchScalarGridSpec(
            num_scalar_prefetch=1,
            grid=(length // span,),
            in_specs=[
                pl.BlockSpec(resize.shape, lambda c, p: (0, 0, 0)),
                pl.BlockSpec((span, columns), lambda c, p: (c, 0)),
                pl.BlockSpec((span, columns), lambda c, p: (c, 0)),
                pl.BlockSpec((group, rows, width), lambda c, p: (0, 0, 0)),
            ],
            out_specs=pl.BlockSpec((group, rows, span), lambda c, p: (0, 0, c)),
            scratch_shapes=[pltpu.VMEM((group, span, span), bf16)],
        ),
        out_shape=shaped((group, rows, length), f32),
        compiler_params=params("arbitrary"),
        cost_estimate=cost(),
        name="unmix",
    )(sizes, resize, left, right, grad)


def attend_kernel(q_ref, ko_ref, kp_ref, vo_ref, vp_ref, out_ref, lse_ref, *, size, chunk):
    first = lax.broadcasted_iota(jnp.int32, (1, 2 * size), 1) < size
    keys = jnp.concatenate([ko_ref[...], kp_ref[...]], axis=0)
    values = jnp.concatenate([vo_ref[...], vp_ref[...]], axis=0)
    for i in range(q_ref.shape[0] // chunk):
        rows = slice(i * chunk, (i + 1) * chunk)
        query = q_ref[rows, :]
        none = jnp.zeros_like(query)
        outs, sums = [], []
        for e in range(2):
            head = jnp.where(first, query, none) if e == 0 else jnp.where(first, none, query)
            scores = right_trans(head, keys)
            peak = jnp.max(scores, axis=-1, keepdims=True)
            expd = jnp.exp(scores - peak)
            denom = jnp.sum(expd, axis=-1, keepdims=True)
            outs.append(matmul(expd.astype(bf16), values) / denom)
            sums.append(peak + jnp.log(denom))
        out_ref[rows, :] = jnp.where(first, outs[0], outs[1]).astype(bf16)
        lse_ref[rows, :] = jnp.where(first, sums[0], sums[1])


def attend(query, key, key_peer, value, value_peer):
    rows, width = query.shape
    size = width // HEADS
    spec = pl.BlockSpec((rows, 2 * size), lambda h: (0, h))
    return pl.pallas_call(
        functools.partial(attend_kernel, size=size, chunk=min(256, rows)),
        grid=(HEADS // 2,),
        in_specs=[spec] * 5,
        out_specs=[spec] * 2,
        out_shape=[shaped((rows, width), bf16), shaped((rows, width), f32)],
        compiler_params=params("arbitrary"),
        cost_estimate=cost(),
        name="attend",
    )(query, key, key_peer, value, value_peer)


def attend_back_kernel(
    q_ref,
    ko_ref,
    kp_ref,
    vo_ref,
    vp_ref,
    g_ref,
    o_ref,
    lse_ref,
    gq_ref,
    gko_ref,
    gkp_ref,
    gvo_ref,
    gvp_ref,
    *,
    size,
    chunk,
):
    rows = q_ref.shape[0]
    upper = lax.broadcasted_iota(jnp.int32, (2 * size, 1), 0) < size
    first = lax.broadcasted_iota(jnp.int32, (1, 2 * size), 1) < size
    query = q_ref[...]
    grad = g_ref[...]
    query_t = query.astype(f32).T
    grad_t = grad.astype(f32).T
    inner_t = grad_t * o_ref[...].astype(f32).T
    lse_t = lse_ref[...].T
    queries, grads, inners, sums, g_query = [], [], [], [], []
    for e in range(2):
        mine = upper if e == 0 else jnp.logical_not(upper)
        queries.append(jnp.where(mine, query_t, 0.0).astype(bf16))
        grads.append(jnp.where(mine, grad_t, 0.0).astype(bf16))
        inners.append(jnp.sum(inner_t[e * size : (e + 1) * size], axis=0, keepdims=True))
        sums.append(lse_t[e * size : e * size + 1])
        g_query.append(jnp.zeros((size, rows), f32))
    for k_ref, v_ref, gk_ref, gv_ref in (
        (ko_ref, vo_ref, gko_ref, gvo_ref),
        (kp_ref, vp_ref, gkp_ref, gvp_ref),
    ):
        for i in range(k_ref.shape[0] // chunk):
            part = slice(i * chunk, (i + 1) * chunk)
            key = k_ref[part, :]
            value = v_ref[part, :]
            key_t = key.astype(f32).T.astype(bf16)
            g_key, g_value = [], []
            for e in range(2):
                probs = jnp.exp(matmul(key, queries[e]) - sums[e])
                g_scores = (probs * (matmul(value, grads[e]) - inners[e])).astype(bf16)
                g_key.append(matmul(g_scores, query))
                g_value.append(matmul(probs.astype(bf16), grad))
                g_query[e] = g_query[e] + matmul(key_t[e * size : (e + 1) * size], g_scores)
            gk_ref[part, :] = jnp.where(first, g_key[0], g_key[1]).astype(gk_ref.dtype)
            gv_ref[part, :] = jnp.where(first, g_value[0], g_value[1]).astype(gv_ref.dtype)
    gq_ref[...] = jnp.concatenate(g_query, axis=0).T.astype(gq_ref.dtype)


def attend_back(query, key, key_peer, value, value_peer, grad, attended, lse):
    rows, width = query.shape
    size = width // HEADS
    spec = pl.BlockSpec((rows, 2 * size), lambda h: (0, h))
    low, full = shaped((rows, width), bf16), shaped((rows, width), f32)
    return pl.pallas_call(
        functools.partial(attend_back_kernel, size=size, chunk=rows),
        grid=(HEADS // 2,),
        in_specs=[spec] * 8,
        out_specs=[spec] * 5,
        out_shape=[low, full, low, full, low],
        compiler_params=params("arbitrary"),
        cost_estimate=cost(True),
        name="attend_back",
    )(query, key, key_peer, value, value_peer, grad, attended, lse)


def side_by_side(left_ref, right_ref):
    return jnp.concatenate([left_ref[...], right_ref[...]], axis=1)


def whole(shape):
    return pl.BlockSpec(shape, lambda i, s: (0,) * len(shape))


def gather_rows_kernel(at_ref, own_ref, peer_ref, out_ref, rows_ref):
    core = at_ref[0]
    strips, part = own_ref.shape[:2]
    half = out_ref.shape[0]
    for j in range(strips):
        start, count = at_ref[1 + j], at_ref[1 + strips + j]
        for ref, which in ((own_ref, core), (peer_ref, 1 - core)):
            for i in range(part):
                local = which * part + i
                row = start + local - core * half
                here = jnp.logical_and(local < count, jnp.logical_and(row >= 0, row < half))
                rows_ref[jnp.where(here, row, half)] = ref[j, i]
    out_ref[...] = rows_ref[:half]


def gather_rows(at, own, peer, half):
    strips, part, grid, width = own.shape
    out = (half, grid, width)
    return pl.pallas_call(
        gather_rows_kernel,
        grid_spec=pltpu.PrefetchScalarGridSpec(
            num_scalar_prefetch=1,
            grid=(1,),
            in_specs=[whole(own.shape)] * 2,
            out_specs=whole(out),
            scratch_shapes=[pltpu.VMEM((half + 1, grid, width), bf16)],
        ),
        out_shape=shaped(out, bf16),
        compiler_params=params("arbitrary"),
        cost_estimate=cost(),
        name="gather_rows",
    )(at, own, peer)


def spread_rows_kernel(at_ref, own_ref, peer_ref, out_ref, rows_ref):
    core = at_ref[0]
    strips, part = out_ref.shape[:2]
    half = own_ref.shape[0]
    rows_ref[pl.ds(core * half, half)] = own_ref[...]
    rows_ref[pl.ds((1 - core) * half, half)] = peer_ref[...]
    rows_ref[2 * half] = jnp.zeros(rows_ref.shape[1:], bf16)
    for j in range(strips):
        start, count = at_ref[1 + j], at_ref[1 + strips + j]
        for i in range(part):
            local = core * part + i
            out_ref[j, i] = rows_ref[jnp.where(local < count, start + local, 2 * half)]


def spread_rows(at, own, peer, strips, capacity):
    half, grid, width = own.shape
    out = (strips, capacity // 2, grid, width)
    return pl.pallas_call(
        spread_rows_kernel,
        grid_spec=pltpu.PrefetchScalarGridSpec(
            num_scalar_prefetch=1,
            grid=(1,),
            in_specs=[whole(own.shape)] * 2,
            out_specs=whole(out),
            scratch_shapes=[pltpu.VMEM((2 * half + 1, grid, width), bf16)],
        ),
        out_shape=shaped(out, bf16),
        compiler_params=params("arbitrary"),
        cost_estimate=cost(),
        name="spread_rows",
    )(at, own, peer)


def normalise(values):
    centred = values - jnp.mean(values, axis=-1, keepdims=True)
    scale = lax.rsqrt(jnp.mean(centred * centred, axis=-1, keepdims=True) + 1e-06)
    return centred * scale, scale


def norm_back(grad, normed, scale):
    return scale * (
        grad
        - jnp.mean(grad, axis=-1, keepdims=True)
        - normed * jnp.mean(grad * normed, axis=-1, keepdims=True)
    )


def column_sum(values):
    return jnp.sum(values, axis=0, keepdims=True)


PATCH, GAIN1, SHIFT1, QUERY, VALUE, OUT, GAIN2, SHIFT2, DOWN = range(9)
VECTORS = 9
UP_AT = 9
POS_AT = 16
TABLE = 96
POS_ROWS = 64


def patch_kernel(base_ref, left_ref, right_ref, out_ref):
    out_ref[...] = matmul(base_ref[...], side_by_side(left_ref, right_ref)).astype(bf16)


def embed_patches(base, left, right):
    group, rows, length = base.shape
    half = left.shape[1]
    return pl.pallas_call(
        patch_kernel,
        grid=(group,),
        in_specs=[
            pl.BlockSpec((None, rows, length), lambda t: (t, 0, 0)),
            pl.BlockSpec((length, half), lambda t: (0, 0)),
            pl.BlockSpec((length, half), lambda t: (0, 0)),
        ],
        out_specs=pl.BlockSpec((None, rows, 2 * half), lambda t: (t, 0, 0)),
        out_shape=shaped((group, rows, 2 * half), bf16),
        compiler_params=params("arbitrary"),
        cost_estimate=cost(),
        name="embed_patches",
    )(base, left, right)


def enter_kernel(
    at_ref, patches_ref, spread_ref, table_ref, ql_ref, qr_ref, kl_ref, kr_ref, vl_ref, vr_ref,
    embed_ref, in_ref, q_ref, k_ref, v_ref,
):
    def vector(row):
        return table_ref[row : row + 1, :]

    place_rows = jnp.dot(
        spread_ref[...],
        table_ref[POS_AT : POS_AT + POS_ROWS, :],
        precision=HIGH_ACCURACY,
        preferred_element_type=f32,
    )
    embed = patches_ref[...].astype(f32) + vector(PATCH) + place_rows
    embed_ref[...] = embed
    normed, _ = normalise(embed)
    attn_in = (normed * vector(GAIN1) + vector(SHIFT1)).astype(bf16)
    in_ref[...] = attn_in
    query = matmul(attn_in, side_by_side(ql_ref, qr_ref))
    q_ref[...] = ((query + vector(QUERY)) * 0.125).astype(bf16)
    k_ref[...] = matmul(attn_in, side_by_side(kl_ref, kr_ref)).astype(bf16)
    v_ref[...] = (matmul(attn_in, side_by_side(vl_ref, vr_ref)) + vector(VALUE)).astype(bf16)


def enter(at, patches, spread, table, weights, blocks=1):
    rows, width = patches.shape
    block = rows // blocks
    part = pl.BlockSpec((block, width), lambda t, a: (t, 0))
    weight = pl.BlockSpec(weights[0].shape, lambda t, a: (0, 0))
    low = shaped((rows, width), bf16)
    return pl.pallas_call(
        enter_kernel,
        grid_spec=pltpu.PrefetchScalarGridSpec(
            num_scalar_prefetch=1,
            grid=(blocks,),
            in_specs=[
                part,
                pl.BlockSpec((None, block, POS_ROWS), lambda t, a: (a[0], t, 0)),
                pl.BlockSpec(table.shape, lambda t, a: (0, 0)),
                *([weight] * 6),
            ],
            out_specs=[part] * 5,
        ),
        out_shape=[shaped((rows, width), f32), low, low, low, low],
        compiler_params=params("arbitrary"),
        cost_estimate=cost(),
        name="enter",
    )(at, patches, spread, table, *weights)


def mlp_kernel(
    attended_ref, embed_ref, table_ref, ol_ref, or_ref, up_ref, bias_ref, down_ref,
    resid_ref, in_ref, hidden_ref, slope_ref, out_ref, total,
):
    step = pl.program_id(0)

    def vector(row):
        return table_ref[row : row + 1, :]

    @pl.when(step == 0)
    def _():
        resid = (
            embed_ref[...]
            + matmul(attended_ref[...], side_by_side(ol_ref, or_ref))
            + vector(OUT)
        )
        resid_ref[...] = resid
        normed, _ = normalise(resid)
        in_ref[...] = (normed * vector(GAIN2) + vector(SHIFT2)).astype(bf16)
        total[...] = resid + vector(DOWN)

    upper = matmul(in_ref[...], up_ref[...]) + bias_ref[...]
    below = 0.5 + 0.5 * lax.erf(upper * 0.7071067811865476)
    hidden = (upper * below).astype(bf16)
    hidden_ref[...] = hidden
    slope_ref[...] = (below + upper * (0.3989422804014327 * jnp.exp(-0.5 * upper * upper))).astype(
        slope_ref.dtype
    )
    total[...] += matmul(hidden, down_ref[...])

    @pl.when(step == pl.num_programs(0) - 1)
    def _():
        out_ref[...] = total[...].astype(bf16)


def mlp(attended, embed, table, w_out, w_up, b_up, w_down):
    rows, width = embed.shape
    blocks = w_up.shape[0]
    ff = blocks * width
    fixed = pl.BlockSpec((rows, width), lambda t: (0, 0))
    columns = pl.BlockSpec((rows, width), lambda t: (0, t))
    return pl.pallas_call(
        mlp_kernel,
        grid=(blocks,),
        in_specs=[
            fixed,
            fixed,
            pl.BlockSpec(table.shape, lambda t: (0, 0)),
            *([pl.BlockSpec(w_out[0].shape, lambda t: (0, 0))] * 2),
            pl.BlockSpec((None, width, width), lambda t: (t, 0, 0)),
            pl.BlockSpec((1, width), lambda t: (0, t)),
            pl.BlockSpec((width, width), lambda t: (t, 0)),
        ],
        out_specs=[fixed, fixed, columns, columns, fixed],
        out_shape=[
            shaped((rows, width), f32),
            shaped((rows, width), bf16),
            shaped((rows, ff), bf16),
            shaped((rows, ff), bf16),
            shaped((rows, width), bf16),
        ],
        scratch_shapes=[pltpu.VMEM((rows, width), f32)],
        compiler_params=params("arbitrary"),
        cost_estimate=cost(),
        name="mlp",
    )(attended, embed, table, *w_out, w_up, b_up, w_down)


def mlp_back_kernel(
    g_ref, slope_ref, resid_ref, table_ref, ol_ref, or_ref, up_ref, down_ref,
    upper_ref, resid_grad_ref, low_ref, att_ref, sums_ref, total,
):
    step = pl.program_id(0)

    @pl.when(step == 0)
    def _():
        total[...] = jnp.zeros_like(total)
        sums_ref[...] = jnp.zeros_like(sums_ref)

    g_upper = slope_ref[...].astype(f32) * right_trans(g_ref[...], down_ref[...])
    sums_ref[pl.ds(8 + step, 1), :] = column_sum(g_upper)
    g_upper_low = g_upper.astype(bf16)
    upper_ref[...] = g_upper_low
    total[...] += right_trans(g_upper_low, up_ref[...])

    @pl.when(step == pl.num_programs(0) - 1)
    def _():
        grad = total[...]
        g_out = g_ref[...].astype(f32)
        normed, scale = normalise(resid_ref[...])
        g_resid = g_out + norm_back(grad * table_ref[GAIN2 : GAIN2 + 1, :], normed, scale)
        resid_grad_ref[...] = g_resid
        g_resid_low = g_resid.astype(bf16)
        low_ref[...] = g_resid_low
        att_ref[...] = right_trans(g_resid_low, side_by_side(ol_ref, or_ref)).astype(bf16)
        sums_ref[0:1, :] = column_sum(g_resid)
        sums_ref[1:2, :] = column_sum(grad * normed)
        sums_ref[2:3, :] = column_sum(grad)
        sums_ref[3:4, :] = column_sum(g_out)


def mlp_back(g_out, slope, resid, table, w_out, w_up, w_down):
    rows, width = g_out.shape
    blocks = w_up.shape[0]
    ff = blocks * width
    fixed = pl.BlockSpec((rows, width), lambda t: (0, 0))
    columns = pl.BlockSpec((rows, width), lambda t: (0, t))
    sums = (8 + 8 * (-(-blocks // 8)), width)
    return pl.pallas_call(
        mlp_back_kernel,
        grid=(blocks,),
        in_specs=[
            fixed,
            columns,
            fixed,
            pl.BlockSpec(table.shape, lambda t: (0, 0)),
            *([pl.BlockSpec(w_out[0].shape, lambda t: (0, 0))] * 2),
            pl.BlockSpec((None, width, width), lambda t: (t, 0, 0)),
            pl.BlockSpec((width, width), lambda t: (t, 0)),
        ],
        out_specs=[columns, fixed, fixed, fixed, pl.BlockSpec(sums, lambda t: (0, 0))],
        out_shape=[
            shaped((rows, ff), bf16),
            shaped((rows, width), f32),
            shaped((rows, width), bf16),
            shaped((rows, width), bf16),
            shaped(sums, f32),
        ],
        scratch_shapes=[pltpu.VMEM((rows, width), f32)],
        compiler_params=params("arbitrary"),
        cost_estimate=cost(True),
        name="mlp_back",
    )(g_out, slope, resid, table, *w_out, w_up, w_down)


def leave_kernel(
    at_ref, gq_ref, gk_ref, gkp_ref, gv_ref, gvp_ref, embed_ref, resid_ref, spread_ref, table_ref,
    ql_ref, qr_ref, kl_ref, kr_ref, vl_ref, vr_ref, q_ref, k_ref, v_ref, out_ref, sums_ref, pos_ref,
):
    @pl.when(pl.program_id(0) == 0)
    def _():
        sums_ref[...] = jnp.zeros_like(sums_ref)
        pos_ref[...] = jnp.zeros_like(pos_ref)

    g_query = gq_ref[...].astype(f32) * 0.125
    g_query_low = g_query.astype(bf16)
    g_key_low = (gk_ref[...] + gkp_ref[...].astype(f32)).astype(bf16)
    g_value_low = (gv_ref[...] + gvp_ref[...].astype(f32)).astype(bf16)
    q_ref[...] = g_query_low
    k_ref[...] = g_key_low
    v_ref[...] = g_value_low
    grad = (
        right_trans(g_query_low, side_by_side(ql_ref, qr_ref))
        + right_trans(g_key_low, side_by_side(kl_ref, kr_ref))
        + right_trans(g_value_low, side_by_side(vl_ref, vr_ref))
    )
    normed, scale = normalise(embed_ref[...])
    g_embed = resid_ref[...] + norm_back(grad * table_ref[GAIN1 : GAIN1 + 1, :], normed, scale)
    out_ref[...] = g_embed.astype(bf16)
    sums_ref[0:1, :] += column_sum(g_embed)
    sums_ref[1:2, :] += column_sum(grad * normed)
    sums_ref[2:3, :] += column_sum(grad)
    sums_ref[3:4, :] += column_sum(g_query)
    sums_ref[4:5, :] += column_sum(g_value_low.astype(f32))
    pos_ref[...] += jnp.dot(
        spread_ref[...], g_embed, precision=HIGH_ACCURACY, preferred_element_type=f32
    )


def leave(
    at, g_query, g_key, g_key_peer, g_value, g_value_peer, embed, g_resid, spread, table,
    weights, blocks=1,
):
    rows, width = embed.shape
    block = rows // blocks
    part = pl.BlockSpec((block, width), lambda t, a: (t, 0))
    weight = pl.BlockSpec(weights[0].shape, lambda t, a: (0, 0))
    low = shaped((rows, width), bf16)
    return pl.pallas_call(
        leave_kernel,
        grid_spec=pltpu.PrefetchScalarGridSpec(
            num_scalar_prefetch=1,
            grid=(blocks,),
            in_specs=[part] * 7
            + [
                pl.BlockSpec((None, POS_ROWS, block), lambda t, a: (a[0], 0, t)),
                pl.BlockSpec(table.shape, lambda t, a: (0, 0)),
                *([weight] * 6),
            ],
            out_specs=[part] * 4
            + [
                pl.BlockSpec((8, width), lambda t, a: (0, 0)),
                pl.BlockSpec((POS_ROWS, width), lambda t, a: (0, 0)),
            ],
        ),
        out_shape=[low] * 4 + [shaped((8, width), f32), shaped((POS_ROWS, width), f32)],
        compiler_params=params("arbitrary"),
        cost_estimate=cost(),
        name="leave",
    )(
        at, g_query, g_key, g_key_peer, g_value, g_value_peer, embed, g_resid, spread, table,
        *weights,
    )


def weight_grad_kernel(at_ref, left_ref, right_ref, send_ref, keep_ref, *scratch):
    core = at_ref[0]
    group, rows, _ = send_ref.shape
    if not scratch:
        for ref, which in ((send_ref, 1 - core), (keep_ref, core)):
            for h in range(group):
                columns = pl.ds(pl.multiple_of((2 * h + which) * rows, 128), rows)
                ref[h] = left_trans(left_ref[:, columns], right_ref[...]).astype(bf16)
        return
    total = scratch[0]
    total[...] = left_trans(left_ref[...], right_ref[...])
    for h in range(group):
        sent = pl.multiple_of((2 * h + 1 - core) * rows, 8)
        kept = pl.multiple_of((2 * h + core) * rows, 8)
        send_ref[h] = total[pl.ds(sent, rows), :].astype(bf16)
        keep_ref[h] = total[pl.ds(kept, rows), :].astype(bf16)


def weight_grad(at, left, right, his, light=False):
    tokens, m = left.shape
    n = right.shape[1]
    rows = m // (2 * his)
    tall = min(m, 768)
    h = tall // (2 * rows)
    wide = 768
    blocks = n // wide
    out = pl.BlockSpec((h, None, rows, wide), lambda i, j, a: (i, j, 0, 0))
    shape = (his, blocks, rows, wide)
    return pl.pallas_call(
        weight_grad_kernel,
        grid_spec=pltpu.PrefetchScalarGridSpec(
            num_scalar_prefetch=1,
            grid=(m // tall, blocks),
            in_specs=[
                pl.BlockSpec((tokens, tall), lambda i, j, a: (0, i)),
                pl.BlockSpec((tokens, wide), lambda i, j, a: (0, j)),
            ],
            out_specs=[out, out],
            scratch_shapes=[pltpu.VMEM((tall, wide), f32)] if rows % 128 else [],
        ),
        out_shape=[shaped(shape, bf16)] * 2,
        compiler_params=params("arbitrary", "arbitrary"),
        cost_estimate=cost(light),
        name="weight_grad",
    )(at, left, right)


def proj_grad_kernel(
    at_ref, in_ref, att_ref, gq_ref, gk_ref, gv_ref, go_ref, small_ref, send_ref, keep_ref, total
):
    core = at_ref[0]
    his, rows, length = send_ref.shape
    width = gq_ref.shape[1]
    turned = [
        small_ref[:, i * 128 : (i + 1) * 128].T for i in range(width // 128)
    ]
    small = jnp.concatenate(turned, axis=0)
    pairs = ((in_ref, gq_ref), (in_ref, gk_ref), (in_ref, gv_ref), (att_ref, go_ref), None)
    for i, pair in enumerate(pairs):
        if pair is None:
            columns = slice(i * width, length)
            total[:, : length - i * width] = small
        else:
            columns = slice(i * width, (i + 1) * width)
            total[...] = left_trans(pair[0][...], pair[1][...])
        size = columns.stop - columns.start
        for h in range(his):
            sent = pl.multiple_of((2 * h + 1 - core) * rows, 8)
            kept = pl.multiple_of((2 * h + core) * rows, 8)
            send_ref[h, :, columns] = total[pl.ds(sent, rows), :size].astype(bf16)
            keep_ref[h, :, columns] = total[pl.ds(kept, rows), :size].astype(bf16)


def proj_grad(at, attn_in, attended, g_query, g_key, g_value, g_resid, small, his):
    tokens, width = attn_in.shape
    rows = width // (2 * his)
    out = (his, rows, 4 * width + small.shape[0])
    return pl.pallas_call(
        proj_grad_kernel,
        grid_spec=pltpu.PrefetchScalarGridSpec(
            num_scalar_prefetch=1,
            grid=(1,),
            in_specs=[whole(attn_in.shape)] * 6 + [whole(small.shape)],
            out_specs=[whole(out)] * 2,
            scratch_shapes=[pltpu.VMEM((width, width), f32)],
        ),
        out_shape=[shaped(out, bf16)] * 2,
        compiler_params=params("arbitrary"),
        cost_estimate=cost(),
        name="proj_grad",
    )(at, attn_in, attended, g_query, g_key, g_value, g_resid, small)


class Place:
    def __init__(self, group):
        self.group = group
        self.images = lax.axis_size("img")
        self.strips = lax.axis_size("strip")
        assert group == 2 and self.strips == 4
        self.img = lax.axis_index("img")
        self.core = self.img % 2
        self.z = lax.axis_index("strip")
        self.bits = [1 << k for k in range(1, self.images.bit_length() - 1)]
        assert self.images == 2 << len(self.bits)

    def flat(self, img, z):
        return img * self.strips + z

    def swap_core(self, values):
        return lax.ppermute(values, "img", [(i, i ^ 1) for i in range(self.images)])

    def across_img(self, values, bit):
        return lax.ppermute(values, "img", [(i, i ^ bit) for i in range(self.images)])

    def along_z(self, values, r):
        return lax.ppermute(values, "strip", [(z, z ^ r) for z in range(self.strips)])


def pick(values, index, axis=0):
    return lax.dynamic_index_in_dim(values, index, axis, keepdims=False)


def after(values, *others):
    return lax.optimization_barrier((values,) + others)[0]


def collect(values, *others):
    values = tuple(values)
    return lax.optimization_barrier(values + others)[: len(values)]


def exchange(values):
    return lax.all_to_all(values, "strip", 0, 0, tiled=True)


class Gather:
    def __init__(self, place, held, bits=()):
        self.place = place
        self.held = held
        self.wide = None
        self.bits = list(bits)

    def halves(self):
        middle = self.held.shape[-1] // 2
        return [
            Gather(self.place, self.held[..., columns], self.bits)
            for columns in (slice(0, middle), slice(middle, None))
        ]

    def widen(self, *others):
        held = after(self.held, *others) if others else self.held
        self.wide = jnp.broadcast_to(held, (self.place.strips,) + held.shape)

    def along_z(self, *others):
        if self.wide is None:
            self.widen(*others)
        self.start = after(self.wide, *others) if others else self.wide
        self.held = exchange(self.start)

    def z_done(self, *others):
        (self.held,) = collect([self.held], *others)

    def over(self, bit, *others):
        if others:
            self.held = after(self.held, *others)
        self.bit = bit
        self.got = self.place.across_img(self.held, bit)

    def done(self, *others):
        (got,) = collect([self.got], *others)
        self.bits = sorted(self.bits + [self.bit], reverse=True)
        axis = self.bits.index(self.bit)
        self.held = join(self.held, got, axis, (self.place.img // self.bit) % 2)

    def last(self, *others):
        if others:
            self.held = after(self.held, *others)
        self.other = self.place.swap_core(self.held)

    def last_done(self, *others):
        (self.other,) = collect([self.other], *others)

    def rows(self, start=0, stop=None):
        axis = len(self.bits)
        full = join(self.held[..., start:stop, :], self.other[..., start:stop, :], axis, self.place.core)
        return full.reshape((-1,) + full.shape[-2:])


def join(mine, other, axis, at):
    spot = [1] * (mine.ndim + 1)
    spot[axis] = 2
    where = jnp.arange(2, dtype=jnp.int32).reshape(spot) == at
    return jnp.where(where, jnp.expand_dims(mine, axis), jnp.expand_dims(other, axis))


def add_low(a, b):
    return (a.astype(f32) + b.astype(f32)).astype(bf16)


class Scatter:
    def __init__(self, place, send, keep):
        self.place = place
        self.bits = place.bits[::-1]
        self.send = send
        self.keep = keep

    def first(self):
        self.got = self.place.swap_core(self.send)

    def first_done(self, *others):
        (got,) = collect([self.got], *others)
        shape = (2,) * len(self.bits) + self.send.shape[1:]
        self.part = add_low(self.keep.reshape(shape), got.reshape(shape))

    def halves(self, middle=None):
        axis = self.part.ndim - 1
        parts = []
        if middle is None:
            middle = self.part.shape[axis] // 2
        for start, stop in ((0, middle), (middle, self.part.shape[axis])):
            one = Scatter(self.place, None, None)
            one.part = lax.slice_in_dim(self.part, start, stop, axis=axis)
            parts.append(one)
        return parts

    def over(self, bit):
        self.bit = bit
        axis = self.bits.index(bit)
        self.sent = pick(self.part, 1 - (self.place.img // bit) % 2, axis)
        self.got = self.place.across_img(self.sent, bit)

    def done(self, *others):
        (self.got,) = collect([self.got], *others)
        axis = self.bits.index(self.bit)
        self.part = add_low(pick(self.part, (self.place.img // self.bit) % 2, axis), self.got)
        self.bits = [b for b in self.bits if b != self.bit]

    def by_strip(self):
        blocks, rows, columns = self.part.shape
        part = self.part.reshape(blocks, self.place.strips, -1, columns)
        return part.transpose(1, 0, 2, 3).reshape(self.place.strips, -1, columns)


class Last:
    def __init__(self, values):
        self.sent = values.astype(bf16)
        self.got = exchange(self.sent)

    def done(self, *others):
        (self.got,) = collect([self.got], *others)
        return jnp.sum(self.got.astype(f32), axis=0)


def split_rows(place, values):
    images, rows = values.shape[:2]
    values = values.reshape((images, 2, rows // 2) + values.shape[2:])
    return pick(values, place.core, 1), pick(values, 1 - place.core, 1)


def pair_up(place, mine, other):
    return jnp.where(
        place.core == 0, jnp.concatenate([mine, other]), jnp.concatenate([other, mine])
    )


def from_chip(place, moved, shape):
    images, rows = shape[0], shape[1] // 2
    moved = moved.reshape((2, images) + moved.shape[1:])
    mine, sent = pick(moved, place.core), pick(moved, 1 - place.core)
    got = place.swap_core(sent)
    low = jnp.where(place.core == 0, mine, got)
    high = jnp.where(place.core == 0, got, mine)
    return jnp.concatenate([low, high], axis=1)


def body(
    pixels,
    cotangent,
    resize,
    patch_index,
    slot_image,
    strip_rows,
    patch_weight,
    pos_grid,
    patch_bias,
    attention_norm_gain,
    attn_shift,
    query_weight,
    query_bias,
    key_weight,
    value_weight,
    value_bias,
    out_weight,
    out_bias,
    mlp_gain,
    mlp_shift,
    up_weight,
    up_bias,
    down_weight,
    down_bias,
):
    group, capacity, grid, pixel_len = pixels.shape
    width = cotangent.shape[3]
    ff = up_weight.shape[1]
    local_rows = capacity * grid
    tokens = group * local_rows
    place = Place(group)
    devices = place.images * place.strips
    his = place.images // 2
    first_slot = place.img * group
    shard = patch_bias.shape[0]
    ups = up_bias.shape[0]
    columns = width // 2
    bits = place.bits

    vectors = (
        patch_bias,
        attention_norm_gain,
        attn_shift,
        query_bias,
        value_bias,
        out_bias,
        mlp_gain,
        mlp_shift,
        down_bias,
    )
    pieces = ups // shard
    small = jnp.concatenate(
        [
            jnp.stack(vectors + tuple(up_bias[i * shard : (i + 1) * shard] for i in range(pieces))),
            jnp.zeros((POS_AT - VECTORS - pieces, shard), bf16),
            pos_grid,
            jnp.zeros((TABLE - POS_AT - BASE * BASE, shard), bf16),
        ]
    )
    lane = width // (TABLE // 16)
    small = jnp.pad(small, ((0, 0), (0, lane - shard))).reshape(-1, 16, lane)
    small = jnp.concatenate(list(small), axis=1)
    proj = jnp.concatenate([query_weight, key_weight, value_weight, out_weight, small])

    size_count = resize.shape[0]
    slot_ids = lax.dynamic_slice_in_dim(slot_image, first_slot, group)
    picked = slot_ids[:, None] == jnp.arange(patch_index.shape[0], dtype=jnp.int32)[None, :]
    size_index = jnp.sum(jnp.where(picked, patch_index[None, :], 0), axis=1)
    sizes = jnp.append(size_index, size_count).astype(jnp.int32)
    half = grid // 2
    image_counts = pick(strip_rows, (place.img // 2) * 2 * group + place.z)
    starts = jnp.cumsum(image_counts) - image_counts
    at = jnp.concatenate([place.core[None], starts, image_counts]).astype(jnp.int32)

    spread = bilinear(grid, BASE)
    spread = (spread[:, None, :, None] * spread[None, :, None, :]).reshape(2, half * grid, -1)
    spread = np.pad(spread, ((0, 0), (0, 0), (0, POS_ROWS - BASE * BASE)))
    spread_t = jnp.asarray(np.ascontiguousarray(spread.transpose(0, 2, 1)))
    spread = jnp.asarray(spread)

    whole_patch, packed = Gather(place, patch_weight), Gather(place, proj)
    blocks = ff // width
    both = Gather(
        place,
        jnp.concatenate(
            [down_weight]
            + [up_weight[:, i * width : (i + 1) * width] for i in range(blocks)]
        ),
    )
    whole_patch.along_z()
    base_pixels = mix(after(sizes, at), resize, pixels.reshape(group, local_rows, pixel_len))
    whole_patch.z_done(base_pixels)
    left, right = whole_patch.halves()
    for k in range(len(bits)):
        if k == len(bits) - 1:
            packed.along_z(left.held, right.held)
        left.over(bits[k])
        right.over(bits[-1 - k])
        if k == len(bits) - 1:
            cot_mine, cot_sent = split_rows(place, after(cotangent, packed.start))
            cot_got = place.swap_core(cot_sent)
            cot_pair = pair_up(place, cot_mine, cot_got)
            both.widen(packed.start)
            left.done(cot_pair, both.wide)
            right.done(cot_pair, both.wide)
        else:
            left.done()
            right.done()
    packed.z_done()
    left.last(packed.held, right.held)
    right.last(packed.held, left.held)
    left.last_done()
    right.last_done()
    w_left, w_right = left.rows().reshape(-1, columns), right.rows().reshape(-1, columns)
    packs = packed.halves()
    packs[0].over(bits[0], left.other)
    packs[1].over(bits[-1], left.other)
    both.along_z(packed.held)
    patches = embed_patches(base_pixels, w_left, w_right).reshape(group, capacity, grid, width)
    packs[0].done(patches)
    packs[1].done(patches)
    for k in range(1, len(bits)):
        packs[0].over(bits[k])
        packs[1].over(bits[-1 - k])
        packs[0].done()
        packs[1].done()
    both.z_done(patches)
    downs_w = Gather(place, both.held[:, : down_weight.shape[0]], both.bits)
    ups_w = Gather(place, both.held[:, down_weight.shape[0] :], both.bits)
    patch_mine, patch_sent = split_rows(place, after(patches, both.held))
    patch_got = place.swap_core(patch_sent)
    patch_pair = pair_up(place, patch_mine, patch_got)
    patch_moved = exchange(patch_pair)
    packs[0].last(patch_pair)
    packs[1].last(patch_pair)
    ups_w.over(bits[-1], packs[0].held, packs[1].held)
    downs_w.over(bits[0], packs[0].held, packs[1].held)
    for k in range(1, len(bits) - 1):
        ups_w.done()
        downs_w.done()
        ups_w.over(bits[-1 - k])
        downs_w.over(bits[k])

    halves = [
        [p.rows(i * shard, (i + 1) * shard).reshape(width, columns) for p in packs]
        for i in range(4)
    ]
    in_weights = [*halves[0], *halves[1], *halves[2]]
    w_out = halves[3]
    flat = jnp.concatenate([p.rows(4 * shard) for p in packs], axis=-1)
    table = (
        flat.reshape(devices, 16, TABLE // 16, lane)[..., :shard]
        .transpose(2, 1, 0, 3)
        .reshape(TABLE, width)
        .astype(f32)
    )
    b_up = (
        table[UP_AT : UP_AT + pieces]
        .reshape(pieces, devices, shard)
        .transpose(1, 0, 2)
        .reshape(1, ff)
    )
    (patch_moved,) = collect([patch_moved], table, b_up, cot_pair, *in_weights, *w_out)
    ups_w.done(patch_moved)
    downs_w.done(patch_moved)
    patch_peer = place.swap_core(patch_moved)
    patches = gather_rows(at, patch_moved, patch_peer, half).reshape(-1, width)
    if len(bits) > 1:
        ups_w.over(bits[0], patch_moved)
        downs_w.over(bits[-1], patch_moved)
    cot_moved = exchange(after(cot_pair, patch_moved))

    embed, attn_in, query, key, value = enter(at, patches, spread, table, in_weights)
    if len(bits) > 1:
        ups_w.done(query)
        downs_w.done(query)
    (cot_moved,) = collect([cot_moved], query)
    key_peer = place.swap_core(after(key, ups_w.held, downs_w.held, cot_moved))
    value_peer = place.swap_core(after(value, ups_w.held, downs_w.held, cot_moved))
    ups_w.last(key_peer, value_peer)
    downs_w.last(key_peer, value_peer)
    cot_peer = place.swap_core(after(cot_moved, key_peer, value_peer))
    attended, lse = attend(query, key, key_peer, value, value_peer)
    ups_w.last_done(attended)
    downs_w.last_done(attended)
    (cot_peer,) = collect([cot_peer], attended)
    w_up = (
        ups_w.rows()
        .reshape(devices, blocks, shard, width)
        .transpose(1, 0, 2, 3)
        .reshape(blocks, width, width)
    )
    w_down = downs_w.rows().reshape(ff, width)
    resid, mlp_in, hidden, slope, final = mlp(attended, embed, table, w_out, w_up, b_up, w_down)
    final_peer = place.swap_core(final)
    g_out = gather_rows(after(at, final), cot_moved, cot_peer, half).reshape(-1, width)

    early, late = bits[: len(bits) // 2], bits[len(bits) // 2 :][::-1]
    down = Scatter(place, *weight_grad(at, hidden, g_out, his))
    (final_peer,) = collect([final_peer], down.send)
    down.send = after(down.send, final_peer)
    down.first()
    image = (half, grid, width)
    final_pieces = spread_rows(
        at, final.reshape(image), final_peer.reshape(image), place.strips, capacity
    )
    down.first_done(final_pieces)
    for bit in late[:-1]:
        down.over(bit)
        down.done()
    down.over(late[-1])
    final_moved = exchange(after(final_pieces, down.sent))
    g_upper, g_resid, g_resid_low, g_att, sums_two = mlp_back(
        after(g_out, final_pieces, down.sent), slope, resid, table, w_out, w_up, w_down
    )
    g_query, g_key, g_key_peer, g_value, g_value_peer = attend_back(
        query, key, key_peer, value, value_peer, g_att, attended, lse
    )
    down.done(g_query)
    (final_moved,) = collect([final_moved], g_query)
    g_key_got = place.swap_core(after(g_key_peer, down.part, final_moved))
    g_value_got = place.swap_core(after(g_value_peer, down.part, final_moved))
    for bit in early[:-1]:
        down.over(bit)
        down.done()
    if early:
        down.over(early[-1])
    up = Scatter(
        place, *weight_grad(at, mlp_in, after(g_upper, g_query, down.sent, final_moved), his)
    )
    g_key_got, g_value_got = collect([g_key_got, g_value_got], up.send)
    up.send = after(up.send, g_key_got, g_value_got)
    up.first()
    g_query, g_key, g_value, g_embed, sums_one, g_pos = leave(
        at,
        after(g_query, up.send),
        g_key,
        g_key_got,
        g_value,
        g_value_got,
        embed,
        g_resid,
        spread_t,
        table,
        in_weights,
    )
    g_embed_peer = place.swap_core(g_embed)
    pieces_back = spread_rows(
        at,
        g_embed.reshape(image),
        g_embed_peer.reshape(image),
        place.strips,
        capacity,
    )
    back = exchange(pieces_back)
    up.first_done(pieces_back)
    for bit in late[:-1]:
        up.over(bit)
        up.done()
    up.over(late[-1])
    up_sums = (
        sums_two[8 : 8 + blocks]
        .reshape(devices, pieces, shard)
        .transpose(1, 0, 2)
        .reshape(pieces, width)
    )
    small = jnp.concatenate([sums_one, sums_two[:8], g_pos, up_sums])
    small = jnp.pad(small, ((0, 128 - small.shape[0]), (0, 0)))
    block_out = from_chip(place, after(final_moved, pieces_back), cotangent.shape)
    proj = Scatter(
        place,
        *(
            part[:, None]
            for part in proj_grad(
                after(at, pieces_back),
                attn_in,
                attended,
                g_query,
                g_key,
                g_value,
                g_resid_low,
                small,
                his,
            )
        ),
    )
    back, up.got, down.got = collect([back, up.got, down.got], proj.send, block_out)
    if early:
        down.done()
    up.done()
    proj.send = after(proj.send, back)
    proj.first()
    for bit in early[:-1]:
        up.over(bit)
        up.done()
    if early:
        up.part = after(up.part, back)
        up.over(early[-1])
    down_last = Last(after(down.by_strip(), back))
    g_patches = from_chip(place, back, cotangent.shape).reshape(tokens, width)
    proj.first_done(g_patches)
    projs = proj.halves(2 * width)
    projs[0].over(bits[-1])
    projs[1].over(bits[0])
    patch = Scatter(
        place,
        *weight_grad(
            at,
            base_pixels.reshape(tokens, pixel_len),
            after(g_patches, projs[0].sent, projs[1].sent, down_last.sent),
            his,
        ),
    )
    projs[0].done(patch.send)
    projs[1].done(patch.send)
    if early:
        up.done(patch.send)
    s_down = down_last.done(patch.send)
    patch.send = after(patch.send, projs[0].got, projs[1].got, up.got, down_last.got)
    patch.first()
    patch.first_done()
    patches = patch.halves()
    patches[0].over(bits[-1])
    patches[1].over(bits[0])
    for k in range(1, len(bits)):
        projs[0].over(bits[-1 - k])
        projs[1].over(bits[k])
        if k + 1 < len(bits):
            projs[0].done()
            projs[1].done()
    up_last = Last(after(up.by_strip(), patches[0].sent, patches[1].sent))
    pixel_grad = unmix(
        sizes,
        resize,
        w_left,
        w_right,
        after(
            g_patches,
            patches[0].sent,
            patches[1].sent,
            projs[0].sent,
            projs[1].sent,
            up_last.sent,
        ).reshape(group, local_rows, width),
    )
    patches[0].done(pixel_grad)
    patches[1].done(pixel_grad)
    if len(bits) > 1:
        projs[0].done(pixel_grad)
        projs[1].done(pixel_grad)
    s_up = up_last.done(pixel_grad)
    for scatter in patches:
        scatter.part = after(scatter.part, up_last.got)
    for k in range(1, len(bits)):
        patches[0].over(bits[-1 - k])
        patches[1].over(bits[k])
        if k + 1 < len(bits):
            patches[0].done()
            patches[1].done()
    proj_last = Last(jnp.concatenate([p.by_strip() for p in projs], axis=-1))
    s_proj = proj_last.done()
    if len(bits) > 1:
        patches[0].done(proj_last.got)
        patches[1].done(proj_last.got)
    s_patch = Last(jnp.concatenate([p.by_strip() for p in patches], axis=-1)).done()
    pixel_grad = pixel_grad.reshape(pixels.shape)

    s_up = s_up.reshape(blocks, shard, width).transpose(1, 0, 2).reshape(shard, ff)
    own = s_proj[:, 4 * width :].T
    s_query, s_key, s_value, s_out = (
        s_proj[:, i * width : (i + 1) * width] for i in range(4)
    )
    ahead = 8
    behind = 16
    up_at = behind + POS_ROWS

    return (
        block_out,
        pixel_grad,
        s_patch,
        own[behind : behind + BASE * BASE],
        own[0],
        own[1],
        own[2],
        s_query,
        own[3],
        s_key,
        s_value,
        own[4],
        s_out,
        own[ahead],
        own[ahead + 1],
        own[ahead + 2],
        s_up,
        own[up_at : up_at + pieces].reshape(-1),
        s_down,
        own[ahead + 3],
    )


def solution(mesh):
    rows = P(("img", "strip"))
    split_rows = P(("img", "strip"), None)
    split_columns = P(None, ("img", "strip"))
    held = P("img", "strip", None, None)
    return jax.shard_map(
        body,
        mesh=mesh,
        in_specs=(
            held,
            held,
            P(),
            P(),
            P(),
            P(),
            split_rows,
            split_columns,
            rows,
            rows,
            rows,
            split_rows,
            rows,
            split_rows,
            split_rows,
            rows,
            split_rows,
            rows,
            rows,
            rows,
            split_rows,
            rows,
            split_rows,
            rows,
        ),
        out_specs=(
            held,
            held,
            split_rows,
            split_columns,
            rows,
            rows,
            rows,
            split_rows,
            rows,
            split_rows,
            split_rows,
            rows,
            split_rows,
            rows,
            rows,
            rows,
            split_rows,
            rows,
            split_rows,
            rows,
        ),
        check_vma=False,
    )
```

```python
import functools

import jax
import jax.numpy as jnp
import numpy as np
from jax import lax
from jax.experimental import pallas as pl
from jax.experimental.pallas import tpu as pltpu
from jax.sharding import PartitionSpec as P

HEADS = 12
BASE = 7
HIGH_ACCURACY = lax.Precision.HIGHEST
AXES = ("img", "strip")


def bilinear(out_count, in_count):
    source = (np.arange(out_count, dtype=np.float32) + 0.5) * (in_count / out_count) - 0.5
    source = np.clip(source, 0.0, in_count - 1.0)
    target = np.arange(in_count, dtype=np.float32)
    return np.maximum(1.0 - np.abs(source[:, None] - target[None, :]), 0.0).astype(np.float32)


def matmul(left, right):
    return jnp.dot(left, right, preferred_element_type=jnp.float32)


def left_trans(left, right):
    return lax.dot_general(
        left, right, (((0,), (0,)), ((), ())), preferred_element_type=jnp.float32
    )


def right_trans(left, right):
    return lax.dot_general(
        left, right, (((1,), (1,)), ((), ())), preferred_element_type=jnp.float32
    )


f32 = jnp.float32
bf16 = jnp.bfloat16
VMEM_LIMIT = 56 << 20


def params(*semantics):
    return pltpu.CompilerParams(
        dimension_semantics=semantics or None, vmem_limit_bytes=VMEM_LIMIT
    )


def shaped(shape, dtype):
    return jax.ShapeDtypeStruct(shape, dtype)


def cost(light=False):
    flops = 1024 if light else 1 << 32
    return pl.CostEstimate(flops=flops, bytes_accessed=1024, transcendentals=0)


def fill_mixer(mixer, table, size, turned):
    side = table.shape[0]
    span = side * side
    live = lax.broadcasted_iota(jnp.int32, table.shape, 0) < size
    table = jnp.where(live, table, 0.0)
    column = lax.broadcasted_iota(jnp.int32, (side, span), 1)
    row = lax.broadcasted_iota(jnp.int32, (side, span), 0)

    def widen(chosen):
        return lax.dot_general(
            table,
            chosen.astype(f32),
            (((0 if turned else 1,), (0,)), ((), ())),
            precision=HIGH_ACCURACY,
            preferred_element_type=f32,
        )

    wide = widen(column // side == row)
    tall = widen(column % side == row)
    for i in range(side):
        mixer[i * side : (i + 1) * side, :] = (wide[i : i + 1, :] * tall).astype(bf16)


def mix_kernel(sizes_ref, table_ref, pix_ref, out_ref, mixer):
    step = table_ref.shape[0] // sizes_ref[2]
    size = (sizes_ref[pl.program_id(0)] + 1) * step
    fill_mixer(mixer, table_ref[...], size, False)
    span = mixer.shape[0]
    for c in range(pix_ref.shape[-1] // span):
        columns = slice(c * span, (c + 1) * span)
        out_ref[:, columns] = matmul(pix_ref[:, columns], mixer[...]).astype(bf16)


def mix(sizes, resize, pixels):
    group, rows, length = pixels.shape
    side = resize.shape[1]
    span = side * side
    block = pl.BlockSpec((None, rows, length), lambda g, p: (g, 0, 0))
    return pl.pallas_call(
        mix_kernel,
        grid_spec=pltpu.PrefetchScalarGridSpec(
            num_scalar_prefetch=1,
            grid=(group,),
            in_specs=[pl.BlockSpec((None, side, side), lambda g, p: (p[g], 0, 0)), block],
            out_specs=block,
            scratch_shapes=[pltpu.VMEM((span, span), bf16)],
        ),
        out_shape=shaped(pixels.shape, bf16),
        compiler_params=params("arbitrary"),
        cost_estimate=cost(),
        name="mix",
    )(sizes, resize, pixels)


def unmix_kernel(sizes_ref, table_ref, left_ref, right_ref, grad_ref, out_ref, mixer):
    group = grad_ref.shape[0]

    @pl.when(pl.program_id(0) == 0)
    def _():
        step = table_ref.shape[1] // table_ref.shape[0]
        for g in range(group):
            index = sizes_ref[g]
            fill_mixer(mixer.at[g], table_ref[index], (index + 1) * step, True)

    rows = grad_ref.shape[1]
    grad = grad_ref[...].reshape(group * rows, -1)
    g_base = right_trans(grad, side_by_side(left_ref, right_ref)).astype(bf16)
    for g in range(group):
        out_ref[g] = matmul(g_base[g * rows : (g + 1) * rows], mixer[g])


def unmix(sizes, resize, left, right, grad):
    group, rows, width = grad.shape
    side = resize.shape[1]
    span = side * side
    length, columns = left.shape
    return pl.pallas_call(
        unmix_kernel,
        grid_spec=pltpu.PrefetchScalarGridSpec(
            num_scalar_prefetch=1,
            grid=(length // span,),
            in_specs=[
                pl.BlockSpec(resize.shape, lambda c, p: (0, 0, 0)),
                pl.BlockSpec((span, columns), lambda c, p: (c, 0)),
                pl.BlockSpec((span, columns), lambda c, p: (c, 0)),
                pl.BlockSpec((group, rows, width), lambda c, p: (0, 0, 0)),
            ],
            out_specs=pl.BlockSpec((group, rows, span), lambda c, p: (0, 0, c)),
            scratch_shapes=[pltpu.VMEM((group, span, span), bf16)],
        ),
        out_shape=shaped((group, rows, length), f32),
        compiler_params=params("arbitrary"),
        cost_estimate=cost(),
        name="unmix",
    )(sizes, resize, left, right, grad)


def attend_kernel(q_ref, ko_ref, kp_ref, vo_ref, vp_ref, out_ref, lse_ref, *, size, chunk):
    first = lax.broadcasted_iota(jnp.int32, (1, 2 * size), 1) < size
    keys = jnp.concatenate([ko_ref[...], kp_ref[...]], axis=0)
    values = jnp.concatenate([vo_ref[...], vp_ref[...]], axis=0)
    for i in range(q_ref.shape[0] // chunk):
        rows = slice(i * chunk, (i + 1) * chunk)
        query = q_ref[rows, :]
        none = jnp.zeros_like(query)
        outs, sums = [], []
        for e in range(2):
            head = jnp.where(first, query, none) if e == 0 else jnp.where(first, none, query)
            scores = right_trans(head, keys)
            peak = jnp.max(scores, axis=-1, keepdims=True)
            expd = jnp.exp(scores - peak)
            denom = jnp.sum(expd, axis=-1, keepdims=True)
            outs.append(matmul(expd.astype(bf16), values) / denom)
            sums.append(peak + jnp.log(denom))
        out_ref[rows, :] = jnp.where(first, outs[0], outs[1]).astype(bf16)
        lse_ref[rows, :] = jnp.where(first, sums[0], sums[1])


def attend(query, key, key_peer, value, value_peer):
    rows, width = query.shape
    size = width // HEADS
    spec = pl.BlockSpec((rows, 2 * size), lambda h: (0, h))
    return pl.pallas_call(
        functools.partial(attend_kernel, size=size, chunk=min(256, rows)),
        grid=(HEADS // 2,),
        in_specs=[spec] * 5,
        out_specs=[spec] * 2,
        out_shape=[shaped((rows, width), bf16), shaped((rows, width), f32)],
        compiler_params=params("arbitrary"),
        cost_estimate=cost(),
        name="attend",
    )(query, key, key_peer, value, value_peer)


def attend_back_kernel(
    q_ref,
    ko_ref,
    kp_ref,
    vo_ref,
    vp_ref,
    g_ref,
    o_ref,
    lse_ref,
    gq_ref,
    gko_ref,
    gkp_ref,
    gvo_ref,
    gvp_ref,
    *,
    size,
    chunk,
):
    rows = q_ref.shape[0]
    upper = lax.broadcasted_iota(jnp.int32, (2 * size, 1), 0) < size
    first = lax.broadcasted_iota(jnp.int32, (1, 2 * size), 1) < size
    query = q_ref[...]
    grad = g_ref[...]
    query_t = query.astype(f32).T
    grad_t = grad.astype(f32).T
    inner_t = grad_t * o_ref[...].astype(f32).T
    lse_t = lse_ref[...].T
    queries, grads, inners, sums, g_query = [], [], [], [], []
    for e in range(2):
        mine = upper if e == 0 else jnp.logical_not(upper)
        queries.append(jnp.where(mine, query_t, 0.0).astype(bf16))
        grads.append(jnp.where(mine, grad_t, 0.0).astype(bf16))
        inners.append(jnp.sum(inner_t[e * size : (e + 1) * size], axis=0, keepdims=True))
        sums.append(lse_t[e * size : e * size + 1])
        g_query.append(jnp.zeros((size, rows), f32))
    for k_ref, v_ref, gk_ref, gv_ref in (
        (ko_ref, vo_ref, gko_ref, gvo_ref),
        (kp_ref, vp_ref, gkp_ref, gvp_ref),
    ):
        for i in range(k_ref.shape[0] // chunk):
            part = slice(i * chunk, (i + 1) * chunk)
            key = k_ref[part, :]
            value = v_ref[part, :]
            key_t = key.astype(f32).T.astype(bf16)
            g_key, g_value = [], []
            for e in range(2):
                probs = jnp.exp(matmul(key, queries[e]) - sums[e])
                g_scores = (probs * (matmul(value, grads[e]) - inners[e])).astype(bf16)
                g_key.append(matmul(g_scores, query))
                g_value.append(matmul(probs.astype(bf16), grad))
                g_query[e] = g_query[e] + matmul(key_t[e * size : (e + 1) * size], g_scores)
            gk_ref[part, :] = jnp.where(first, g_key[0], g_key[1]).astype(gk_ref.dtype)
            gv_ref[part, :] = jnp.where(first, g_value[0], g_value[1]).astype(gv_ref.dtype)
    gq_ref[...] = jnp.concatenate(g_query, axis=0).T.astype(gq_ref.dtype)


def attend_back(query, key, key_peer, value, value_peer, grad, attended, lse):
    rows, width = query.shape
    size = width // HEADS
    spec = pl.BlockSpec((rows, 2 * size), lambda h: (0, h))
    low, full = shaped((rows, width), bf16), shaped((rows, width), f32)
    return pl.pallas_call(
        functools.partial(attend_back_kernel, size=size, chunk=rows),
        grid=(HEADS // 2,),
        in_specs=[spec] * 8,
        out_specs=[spec] * 5,
        out_shape=[low, full, low, full, low],
        compiler_params=params("arbitrary"),
        cost_estimate=cost(True),
        name="attend_back",
    )(query, key, key_peer, value, value_peer, grad, attended, lse)


def side_by_side(left_ref, right_ref):
    return jnp.concatenate([left_ref[...], right_ref[...]], axis=1)


def whole(shape):
    return pl.BlockSpec(shape, lambda i, s: (0,) * len(shape))


def gather_rows_kernel(at_ref, own_ref, peer_ref, out_ref, rows_ref):
    core = at_ref[0]
    strips, part = own_ref.shape[:2]
    half = out_ref.shape[0]
    for j in range(strips):
        start, count = at_ref[1 + j], at_ref[1 + strips + j]
        for ref, which in ((own_ref, core), (peer_ref, 1 - core)):
            for i in range(part):
                local = which * part + i
                row = start + local - core * half
                here = jnp.logical_and(local < count, jnp.logical_and(row >= 0, row < half))
                rows_ref[jnp.where(here, row, half)] = ref[j, i]
    out_ref[...] = rows_ref[:half]


def gather_rows(at, own, peer, half):
    strips, part, grid, width = own.shape
    out = (half, grid, width)
    return pl.pallas_call(
        gather_rows_kernel,
        grid_spec=pltpu.PrefetchScalarGridSpec(
            num_scalar_prefetch=1,
            grid=(1,),
            in_specs=[whole(own.shape)] * 2,
            out_specs=whole(out),
            scratch_shapes=[pltpu.VMEM((half + 1, grid, width), bf16)],
        ),
        out_shape=shaped(out, bf16),
        compiler_params=params("arbitrary"),
        cost_estimate=cost(),
        name="gather_rows",
    )(at, own, peer)


def spread_rows_kernel(at_ref, own_ref, peer_ref, out_ref, rows_ref):
    core = at_ref[0]
    strips, part = out_ref.shape[:2]
    half = own_ref.shape[0]
    rows_ref[pl.ds(core * half, half)] = own_ref[...]
    rows_ref[pl.ds((1 - core) * half, half)] = peer_ref[...]
    rows_ref[2 * half] = jnp.zeros(rows_ref.shape[1:], bf16)
    for j in range(strips):
        start, count = at_ref[1 + j], at_ref[1 + strips + j]
        for i in range(part):
            local = core * part + i
            out_ref[j, i] = rows_ref[jnp.where(local < count, start + local, 2 * half)]


def spread_rows(at, own, peer, strips, capacity):
    half, grid, width = own.shape
    out = (strips, capacity // 2, grid, width)
    return pl.pallas_call(
        spread_rows_kernel,
        grid_spec=pltpu.PrefetchScalarGridSpec(
            num_scalar_prefetch=1,
            grid=(1,),
            in_specs=[whole(own.shape)] * 2,
            out_specs=whole(out),
            scratch_shapes=[pltpu.VMEM((2 * half + 1, grid, width), bf16)],
        ),
        out_shape=shaped(out, bf16),
        compiler_params=params("arbitrary"),
        cost_estimate=cost(),
        name="spread_rows",
    )(at, own, peer)


def normalise(values):
    centred = values - jnp.mean(values, axis=-1, keepdims=True)
    scale = lax.rsqrt(jnp.mean(centred * centred, axis=-1, keepdims=True) + 1e-06)
    return centred * scale, scale


def norm_back(grad, normed, scale):
    return scale * (
        grad
        - jnp.mean(grad, axis=-1, keepdims=True)
        - normed * jnp.mean(grad * normed, axis=-1, keepdims=True)
    )


def column_sum(values):
    return jnp.sum(values, axis=0, keepdims=True)


PATCH, GAIN1, SHIFT1, QUERY, VALUE, OUT, GAIN2, SHIFT2, DOWN = range(9)
VECTORS = 9
UP_AT = 9
POS_AT = 16
TABLE = 96
POS_ROWS = 64


def patch_kernel(base_ref, left_ref, right_ref, out_ref):
    out_ref[...] = matmul(base_ref[...], side_by_side(left_ref, right_ref)).astype(bf16)


def embed_patches(base, left, right):
    group, rows, length = base.shape
    half = left.shape[1]
    return pl.pallas_call(
        patch_kernel,
        grid=(group,),
        in_specs=[
            pl.BlockSpec((None, rows, length), lambda t: (t, 0, 0)),
            pl.BlockSpec((length, half), lambda t: (0, 0)),
            pl.BlockSpec((length, half), lambda t: (0, 0)),
        ],
        out_specs=pl.BlockSpec((None, rows, 2 * half), lambda t: (t, 0, 0)),
        out_shape=shaped((group, rows, 2 * half), bf16),
        compiler_params=params("arbitrary"),
        cost_estimate=cost(),
        name="embed_patches",
    )(base, left, right)


def enter_kernel(
    at_ref, patches_ref, spread_ref, table_ref, ql_ref, qr_ref, kl_ref, kr_ref, vl_ref, vr_ref,
    embed_ref, in_ref, q_ref, k_ref, v_ref,
):
    def vector(row):
        return table_ref[row : row + 1, :]

    place_rows = jnp.dot(
        spread_ref[...],
        table_ref[POS_AT : POS_AT + POS_ROWS, :],
        precision=HIGH_ACCURACY,
        preferred_element_type=f32,
    )
    embed = patches_ref[...].astype(f32) + vector(PATCH) + place_rows
    embed_ref[...] = embed
    normed, _ = normalise(embed)
    attn_in = (normed * vector(GAIN1) + vector(SHIFT1)).astype(bf16)
    in_ref[...] = attn_in
    query = matmul(attn_in, side_by_side(ql_ref, qr_ref))
    q_ref[...] = ((query + vector(QUERY)) * 0.125).astype(bf16)
    k_ref[...] = matmul(attn_in, side_by_side(kl_ref, kr_ref)).astype(bf16)
    v_ref[...] = (matmul(attn_in, side_by_side(vl_ref, vr_ref)) + vector(VALUE)).astype(bf16)


def enter(at, patches, spread, table, weights, blocks=1):
    rows, width = patches.shape
    block = rows // blocks
    part = pl.BlockSpec((block, width), lambda t, a: (t, 0))
    weight = pl.BlockSpec(weights[0].shape, lambda t, a: (0, 0))
    low = shaped((rows, width), bf16)
    return pl.pallas_call(
        enter_kernel,
        grid_spec=pltpu.PrefetchScalarGridSpec(
            num_scalar_prefetch=1,
            grid=(blocks,),
            in_specs=[
                part,
                pl.BlockSpec((None, block, POS_ROWS), lambda t, a: (a[0], t, 0)),
                pl.BlockSpec(table.shape, lambda t, a: (0, 0)),
                *([weight] * 6),
            ],
            out_specs=[part] * 5,
        ),
        out_shape=[shaped((rows, width), f32), low, low, low, low],
        compiler_params=params("arbitrary"),
        cost_estimate=cost(),
        name="enter",
    )(at, patches, spread, table, *weights)


def mlp_kernel(
    attended_ref, embed_ref, table_ref, ol_ref, or_ref, up_ref, bias_ref, down_ref,
    resid_ref, in_ref, hidden_ref, slope_ref, out_ref, total,
):
    step = pl.program_id(0)

    def vector(row):
        return table_ref[row : row + 1, :]

    @pl.when(step == 0)
    def _():
        resid = (
            embed_ref[...]
            + matmul(attended_ref[...], side_by_side(ol_ref, or_ref))
            + vector(OUT)
        )
        resid_ref[...] = resid
        normed, _ = normalise(resid)
        in_ref[...] = (normed * vector(GAIN2) + vector(SHIFT2)).astype(bf16)
        total[...] = resid + vector(DOWN)

    upper = matmul(in_ref[...], up_ref[...]) + bias_ref[...]
    below = 0.5 + 0.5 * lax.erf(upper * 0.7071067811865476)
    hidden = (upper * below).astype(bf16)
    hidden_ref[...] = hidden
    slope_ref[...] = (below + upper * (0.3989422804014327 * jnp.exp(-0.5 * upper * upper))).astype(
        slope_ref.dtype
    )
    total[...] += matmul(hidden, down_ref[...])

    @pl.when(step == pl.num_programs(0) - 1)
    def _():
        out_ref[...] = total[...].astype(bf16)


def mlp(attended, embed, table, w_out, w_up, b_up, w_down):
    rows, width = embed.shape
    blocks = w_up.shape[0]
    ff = blocks * width
    fixed = pl.BlockSpec((rows, width), lambda t: (0, 0))
    columns = pl.BlockSpec((rows, width), lambda t: (0, t))
    return pl.pallas_call(
        mlp_kernel,
        grid=(blocks,),
        in_specs=[
            fixed,
            fixed,
            pl.BlockSpec(table.shape, lambda t: (0, 0)),
            *([pl.BlockSpec(w_out[0].shape, lambda t: (0, 0))] * 2),
            pl.BlockSpec((None, width, width), lambda t: (t, 0, 0)),
            pl.BlockSpec((1, width), lambda t: (0, t)),
            pl.BlockSpec((width, width), lambda t: (t, 0)),
        ],
        out_specs=[fixed, fixed, columns, columns, fixed],
        out_shape=[
            shaped((rows, width), f32),
            shaped((rows, width), bf16),
            shaped((rows, ff), bf16),
            shaped((rows, ff), bf16),
            shaped((rows, width), bf16),
        ],
        scratch_shapes=[pltpu.VMEM((rows, width), f32)],
        compiler_params=params("arbitrary"),
        cost_estimate=cost(),
        name="mlp",
    )(attended, embed, table, *w_out, w_up, b_up, w_down)


def mlp_back_kernel(
    g_ref, slope_ref, resid_ref, table_ref, ol_ref, or_ref, up_ref, down_ref,
    upper_ref, resid_grad_ref, low_ref, att_ref, sums_ref, total,
):
    step = pl.program_id(0)

    @pl.when(step == 0)
    def _():
        total[...] = jnp.zeros_like(total)
        sums_ref[...] = jnp.zeros_like(sums_ref)

    g_upper = slope_ref[...].astype(f32) * right_trans(g_ref[...], down_ref[...])
    sums_ref[pl.ds(8 + step, 1), :] = column_sum(g_upper)
    g_upper_low = g_upper.astype(bf16)
    upper_ref[...] = g_upper_low
    total[...] += right_trans(g_upper_low, up_ref[...])

    @pl.when(step == pl.num_programs(0) - 1)
    def _():
        grad = total[...]
        g_out = g_ref[...].astype(f32)
        normed, scale = normalise(resid_ref[...])
        g_resid = g_out + norm_back(grad * table_ref[GAIN2 : GAIN2 + 1, :], normed, scale)
        resid_grad_ref[...] = g_resid
        g_resid_low = g_resid.astype(bf16)
        low_ref[...] = g_resid_low
        att_ref[...] = right_trans(g_resid_low, side_by_side(ol_ref, or_ref)).astype(bf16)
        sums_ref[0:1, :] = column_sum(g_resid)
        sums_ref[1:2, :] = column_sum(grad * normed)
        sums_ref[2:3, :] = column_sum(grad)
        sums_ref[3:4, :] = column_sum(g_out)


def mlp_back(g_out, slope, resid, table, w_out, w_up, w_down):
    rows, width = g_out.shape
    blocks = w_up.shape[0]
    ff = blocks * width
    fixed = pl.BlockSpec((rows, width), lambda t: (0, 0))
    columns = pl.BlockSpec((rows, width), lambda t: (0, t))
    sums = (8 + 8 * (-(-blocks // 8)), width)
    return pl.pallas_call(
        mlp_back_kernel,
        grid=(blocks,),
        in_specs=[
            fixed,
            columns,
            fixed,
            pl.BlockSpec(table.shape, lambda t: (0, 0)),
            *([pl.BlockSpec(w_out[0].shape, lambda t: (0, 0))] * 2),
            pl.BlockSpec((None, width, width), lambda t: (t, 0, 0)),
            pl.BlockSpec((width, width), lambda t: (t, 0)),
        ],
        out_specs=[columns, fixed, fixed, fixed, pl.BlockSpec(sums, lambda t: (0, 0))],
        out_shape=[
            shaped((rows, ff), bf16),
            shaped((rows, width), f32),
            shaped((rows, width), bf16),
            shaped((rows, width), bf16),
            shaped(sums, f32),
        ],
        scratch_shapes=[pltpu.VMEM((rows, width), f32)],
        compiler_params=params("arbitrary"),
        cost_estimate=cost(True),
        name="mlp_back",
    )(g_out, slope, resid, table, *w_out, w_up, w_down)


def leave_kernel(
    at_ref, gq_ref, gk_ref, gkp_ref, gv_ref, gvp_ref, embed_ref, resid_ref, spread_ref, table_ref,
    ql_ref, qr_ref, kl_ref, kr_ref, vl_ref, vr_ref, q_ref, k_ref, v_ref, out_ref, sums_ref, pos_ref,
):
    @pl.when(pl.program_id(0) == 0)
    def _():
        sums_ref[...] = jnp.zeros_like(sums_ref)
        pos_ref[...] = jnp.zeros_like(pos_ref)

    g_query = gq_ref[...].astype(f32) * 0.125
    g_query_low = g_query.astype(bf16)
    g_key_low = (gk_ref[...] + gkp_ref[...].astype(f32)).astype(bf16)
    g_value_low = (gv_ref[...] + gvp_ref[...].astype(f32)).astype(bf16)
    q_ref[...] = g_query_low
    k_ref[...] = g_key_low
    v_ref[...] = g_value_low
    grad = (
        right_trans(g_query_low, side_by_side(ql_ref, qr_ref))
        + right_trans(g_key_low, side_by_side(kl_ref, kr_ref))
        + right_trans(g_value_low, side_by_side(vl_ref, vr_ref))
    )
    normed, scale = normalise(embed_ref[...])
    g_embed = resid_ref[...] + norm_back(grad * table_ref[GAIN1 : GAIN1 + 1, :], normed, scale)
    out_ref[...] = g_embed.astype(bf16)
    sums_ref[0:1, :] += column_sum(g_embed)
    sums_ref[1:2, :] += column_sum(grad * normed)
    sums_ref[2:3, :] += column_sum(grad)
    sums_ref[3:4, :] += column_sum(g_query)
    sums_ref[4:5, :] += column_sum(g_value_low.astype(f32))
    pos_ref[...] += jnp.dot(
        spread_ref[...], g_embed, precision=HIGH_ACCURACY, preferred_element_type=f32
    )


def leave(
    at, g_query, g_key, g_key_peer, g_value, g_value_peer, embed, g_resid, spread, table,
    weights, blocks=1,
):
    rows, width = embed.shape
    block = rows // blocks
    part = pl.BlockSpec((block, width), lambda t, a: (t, 0))
    weight = pl.BlockSpec(weights[0].shape, lambda t, a: (0, 0))
    low = shaped((rows, width), bf16)
    return pl.pallas_call(
        leave_kernel,
        grid_spec=pltpu.PrefetchScalarGridSpec(
            num_scalar_prefetch=1,
            grid=(blocks,),
            in_specs=[part] * 7
            + [
                pl.BlockSpec((None, POS_ROWS, block), lambda t, a: (a[0], 0, t)),
                pl.BlockSpec(table.shape, lambda t, a: (0, 0)),
                *([weight] * 6),
            ],
            out_specs=[part] * 4
            + [
                pl.BlockSpec((8, width), lambda t, a: (0, 0)),
                pl.BlockSpec((POS_ROWS, width), lambda t, a: (0, 0)),
            ],
        ),
        out_shape=[low] * 4 + [shaped((8, width), f32), shaped((POS_ROWS, width), f32)],
        compiler_params=params("arbitrary"),
        cost_estimate=cost(),
        name="leave",
    )(
        at, g_query, g_key, g_key_peer, g_value, g_value_peer, embed, g_resid, spread, table,
        *weights,
    )


def weight_grad_kernel(at_ref, left_ref, right_ref, send_ref, keep_ref, *scratch):
    core = at_ref[0]
    group, rows, _ = send_ref.shape
    if not scratch:
        for ref, which in ((send_ref, 1 - core), (keep_ref, core)):
            for h in range(group):
                columns = pl.ds(pl.multiple_of((2 * h + which) * rows, 128), rows)
                ref[h] = left_trans(left_ref[:, columns], right_ref[...]).astype(bf16)
        return
    total, turned = scratch

    @pl.when(pl.program_id(1) == 0)
    def _():
        turned[...] = left_ref[...].astype(f32).T.astype(bf16)

    total[...] = matmul(turned[...], right_ref[...])
    for h in range(group):
        sent = pl.multiple_of((2 * h + 1 - core) * rows, 8)
        kept = pl.multiple_of((2 * h + core) * rows, 8)
        send_ref[h] = total[pl.ds(sent, rows), :].astype(bf16)
        keep_ref[h] = total[pl.ds(kept, rows), :].astype(bf16)


def weight_grad(at, left, right, his, light=False):
    tokens, m = left.shape
    n = right.shape[1]
    rows = m // (2 * his)
    tall = min(m, 768)
    h = tall // (2 * rows)
    wide = 768
    blocks = n // wide
    out = pl.BlockSpec((h, None, rows, wide), lambda i, j, a: (i, j, 0, 0))
    shape = (his, blocks, rows, wide)
    return pl.pallas_call(
        weight_grad_kernel,
        grid_spec=pltpu.PrefetchScalarGridSpec(
            num_scalar_prefetch=1,
            grid=(m // tall, blocks),
            in_specs=[
                pl.BlockSpec((tokens, tall), lambda i, j, a: (0, i)),
                pl.BlockSpec((tokens, wide), lambda i, j, a: (0, j)),
            ],
            out_specs=[out, out],
            scratch_shapes=[pltpu.VMEM((tall, wide), f32), pltpu.VMEM((tall, tokens), bf16)]
            if rows % 128
            else [],
        ),
        out_shape=[shaped(shape, bf16)] * 2,
        compiler_params=params("arbitrary", "arbitrary"),
        cost_estimate=cost(light),
        name="weight_grad",
    )(at, left, right)


def proj_grad_kernel(
    at_ref, in_ref, att_ref, gq_ref, gk_ref, gv_ref, go_ref, small_ref, send_ref, keep_ref, total
):
    core = at_ref[0]
    his, rows, length = send_ref.shape
    width = gq_ref.shape[1]
    turned = [
        small_ref[:, i * 128 : (i + 1) * 128].T for i in range(width // 128)
    ]
    small = jnp.concatenate(turned, axis=0)
    pairs = ((in_ref, gq_ref), (in_ref, gk_ref), (in_ref, gv_ref), (att_ref, go_ref), None)
    for i, pair in enumerate(pairs):
        if pair is None:
            columns = slice(i * width, length)
            total[:, : length - i * width] = small
        else:
            columns = slice(i * width, (i + 1) * width)
            total[...] = left_trans(pair[0][...], pair[1][...])
        size = columns.stop - columns.start
        for h in range(his):
            sent = pl.multiple_of((2 * h + 1 - core) * rows, 8)
            kept = pl.multiple_of((2 * h + core) * rows, 8)
            send_ref[h, :, columns] = total[pl.ds(sent, rows), :size].astype(bf16)
            keep_ref[h, :, columns] = total[pl.ds(kept, rows), :size].astype(bf16)


def proj_grad(at, attn_in, attended, g_query, g_key, g_value, g_resid, small, his):
    tokens, width = attn_in.shape
    rows = width // (2 * his)
    out = (his, rows, 4 * width + small.shape[0])
    return pl.pallas_call(
        proj_grad_kernel,
        grid_spec=pltpu.PrefetchScalarGridSpec(
            num_scalar_prefetch=1,
            grid=(1,),
            in_specs=[whole(attn_in.shape)] * 6 + [whole(small.shape)],
            out_specs=[whole(out)] * 2,
            scratch_shapes=[pltpu.VMEM((width, width), f32)],
        ),
        out_shape=[shaped(out, bf16)] * 2,
        compiler_params=params("arbitrary"),
        cost_estimate=cost(),
        name="proj_grad",
    )(at, attn_in, attended, g_query, g_key, g_value, g_resid, small)


class Place:
    def __init__(self, group):
        self.group = group
        self.images = lax.axis_size("img")
        self.strips = lax.axis_size("strip")
        assert group == 2 and self.strips == 4
        self.img = lax.axis_index("img")
        self.core = self.img % 2
        self.z = lax.axis_index("strip")
        self.bits = [1 << k for k in range(1, self.images.bit_length() - 1)]
        assert self.images == 2 << len(self.bits)

    def flat(self, img, z):
        return img * self.strips + z

    def swap_core(self, values):
        return lax.ppermute(values, "img", [(i, i ^ 1) for i in range(self.images)])

    def across_img(self, values, bit):
        return lax.ppermute(values, "img", [(i, i ^ bit) for i in range(self.images)])

    def along_z(self, values, r):
        return lax.ppermute(values, "strip", [(z, z ^ r) for z in range(self.strips)])


def pick(values, index, axis=0):
    return lax.dynamic_index_in_dim(values, index, axis, keepdims=False)


def after(values, *others):
    return lax.optimization_barrier((values,) + others)[0]


def collect(values, *others):
    values = tuple(values)
    return lax.optimization_barrier(values + others)[: len(values)]


def exchange(values):
    return lax.all_to_all(values, "strip", 0, 0, tiled=True)


class Gather:
    def __init__(self, place, held, bits=()):
        self.place = place
        self.held = held
        self.wide = None
        self.bits = list(bits)

    def halves(self):
        middle = self.held.shape[-1] // 2
        return [
            Gather(self.place, self.held[..., columns], self.bits)
            for columns in (slice(0, middle), slice(middle, None))
        ]

    def widen(self, *others):
        held = after(self.held, *others) if others else self.held
        self.wide = jnp.broadcast_to(held, (self.place.strips,) + held.shape)

    def along_z(self, *others):
        if self.wide is None:
            self.widen(*others)
        self.start = after(self.wide, *others) if others else self.wide
        self.held = exchange(self.start)

    def z_done(self, *others):
        (self.held,) = collect([self.held], *others)

    def over(self, bit, *others):
        if others:
            self.held = after(self.held, *others)
        self.bit = bit
        self.got = self.place.across_img(self.held, bit)

    def done(self, *others):
        (got,) = collect([self.got], *others)
        self.bits = sorted(self.bits + [self.bit], reverse=True)
        axis = self.bits.index(self.bit)
        self.held = join(self.held, got, axis, (self.place.img // self.bit) % 2)

    def last(self, *others):
        if others:
            self.held = after(self.held, *others)
        self.other = self.place.swap_core(self.held)

    def last_done(self, *others):
        (self.other,) = collect([self.other], *others)

    def rows(self, start=0, stop=None):
        axis = len(self.bits)
        full = join(self.held[..., start:stop, :], self.other[..., start:stop, :], axis, self.place.core)
        return full.reshape((-1,) + full.shape[-2:])


def join(mine, other, axis, at):
    spot = [1] * (mine.ndim + 1)
    spot[axis] = 2
    where = jnp.arange(2, dtype=jnp.int32).reshape(spot) == at
    return jnp.where(where, jnp.expand_dims(mine, axis), jnp.expand_dims(other, axis))


def add_low(a, b):
    return (a.astype(f32) + b.astype(f32)).astype(bf16)


class Scatter:
    def __init__(self, place, send, keep):
        self.place = place
        self.bits = place.bits[::-1]
        self.send = send
        self.keep = keep

    def first(self):
        self.got = self.place.swap_core(self.send)

    def first_done(self, *others):
        (got,) = collect([self.got], *others)
        shape = (2,) * len(self.bits) + self.send.shape[1:]
        self.part = add_low(self.keep.reshape(shape), got.reshape(shape))

    def halves(self, middle=None):
        axis = self.part.ndim - 1
        parts = []
        if middle is None:
            middle = self.part.shape[axis] // 2
        for start, stop in ((0, middle), (middle, self.part.shape[axis])):
            one = Scatter(self.place, None, None)
            one.part = lax.slice_in_dim(self.part, start, stop, axis=axis)
            parts.append(one)
        return parts

    def over(self, bit):
        self.bit = bit
        axis = self.bits.index(bit)
        self.sent = pick(self.part, 1 - (self.place.img // bit) % 2, axis)
        self.got = self.place.across_img(self.sent, bit)

    def done(self, *others):
        (self.got,) = collect([self.got], *others)
        axis = self.bits.index(self.bit)
        self.part = add_low(pick(self.part, (self.place.img // self.bit) % 2, axis), self.got)
        self.bits = [b for b in self.bits if b != self.bit]

    def by_strip(self):
        blocks, rows, columns = self.part.shape
        part = self.part.reshape(blocks, self.place.strips, -1, columns)
        return part.transpose(1, 0, 2, 3).reshape(self.place.strips, -1, columns)


class Last:
    def __init__(self, values):
        self.sent = values.astype(bf16)
        self.got = exchange(self.sent)

    def done(self, *others):
        (self.got,) = collect([self.got], *others)
        return jnp.sum(self.got.astype(f32), axis=0)


def split_rows(place, values):
    images, rows = values.shape[:2]
    values = values.reshape((images, 2, rows // 2) + values.shape[2:])
    return pick(values, place.core, 1), pick(values, 1 - place.core, 1)


def pair_up(place, mine, other):
    return jnp.where(
        place.core == 0, jnp.concatenate([mine, other]), jnp.concatenate([other, mine])
    )


def from_chip(place, moved, shape):
    images, rows = shape[0], shape[1] // 2
    moved = moved.reshape((2, images) + moved.shape[1:])
    mine, sent = pick(moved, place.core), pick(moved, 1 - place.core)
    got = place.swap_core(sent)
    low = jnp.where(place.core == 0, mine, got)
    high = jnp.where(place.core == 0, got, mine)
    return jnp.concatenate([low, high], axis=1)


def body(
    pixels,
    cotangent,
    resize,
    patch_index,
    slot_image,
    strip_rows,
    patch_weight,
    pos_grid,
    patch_bias,
    attention_norm_gain,
    attn_shift,
    query_weight,
    query_bias,
    key_weight,
    value_weight,
    value_bias,
    out_weight,
    out_bias,
    mlp_gain,
    mlp_shift,
    up_weight,
    up_bias,
    down_weight,
    down_bias,
):
    group, capacity, grid, pixel_len = pixels.shape
    width = cotangent.shape[3]
    ff = up_weight.shape[1]
    local_rows = capacity * grid
    tokens = group * local_rows
    place = Place(group)
    devices = place.images * place.strips
    his = place.images // 2
    first_slot = place.img * group
    shard = patch_bias.shape[0]
    ups = up_bias.shape[0]
    columns = width // 2
    bits = place.bits

    vectors = (
        patch_bias,
        attention_norm_gain,
        attn_shift,
        query_bias,
        value_bias,
        out_bias,
        mlp_gain,
        mlp_shift,
        down_bias,
    )
    pieces = ups // shard
    small = jnp.concatenate(
        [
            jnp.stack(vectors + tuple(up_bias[i * shard : (i + 1) * shard] for i in range(pieces))),
            jnp.zeros((POS_AT - VECTORS - pieces, shard), bf16),
            pos_grid,
            jnp.zeros((TABLE - POS_AT - BASE * BASE, shard), bf16),
        ]
    )
    lane = width // (TABLE // 16)
    small = jnp.pad(small, ((0, 0), (0, lane - shard))).reshape(-1, 16, lane)
    small = jnp.concatenate(list(small), axis=1)
    proj = jnp.concatenate([query_weight, key_weight, value_weight, out_weight, small])

    size_count = resize.shape[0]
    slot_ids = lax.dynamic_slice_in_dim(slot_image, first_slot, group)
    picked = slot_ids[:, None] == jnp.arange(patch_index.shape[0], dtype=jnp.int32)[None, :]
    size_index = jnp.sum(jnp.where(picked, patch_index[None, :], 0), axis=1)
    sizes = jnp.append(size_index, size_count).astype(jnp.int32)
    half = grid // 2
    image_counts = pick(strip_rows, (place.img // 2) * 2 * group + place.z)
    starts = jnp.cumsum(image_counts) - image_counts
    at = jnp.concatenate([place.core[None], starts, image_counts]).astype(jnp.int32)

    spread = bilinear(grid, BASE)
    spread = (spread[:, None, :, None] * spread[None, :, None, :]).reshape(2, half * grid, -1)
    spread = np.pad(spread, ((0, 0), (0, 0), (0, POS_ROWS - BASE * BASE)))
    spread_t = jnp.asarray(np.ascontiguousarray(spread.transpose(0, 2, 1)))
    spread = jnp.asarray(spread)

    whole_patch, packed = Gather(place, patch_weight), Gather(place, proj)
    blocks = ff // width
    both = Gather(
        place,
        jnp.concatenate(
            [down_weight]
            + [up_weight[:, i * width : (i + 1) * width] for i in range(blocks)]
        ),
    )
    whole_patch.along_z()
    base_pixels = mix(after(sizes, at), resize, pixels.reshape(group, local_rows, pixel_len))
    whole_patch.z_done(base_pixels)
    left, right = whole_patch.halves()
    for k in range(len(bits)):
        if k == len(bits) - 1:
            packed.along_z(left.held, right.held)
        left.over(bits[k])
        right.over(bits[-1 - k])
        if k == len(bits) - 1:
            cot_mine, cot_sent = split_rows(place, after(cotangent, packed.start))
            cot_got = place.swap_core(cot_sent)
            cot_pair = pair_up(place, cot_mine, cot_got)
            both.widen(packed.start)
            left.done(cot_pair, both.wide)
            right.done(cot_pair, both.wide)
        else:
            left.done()
            right.done()
    packed.z_done()
    left.last(packed.held, right.held)
    right.last(packed.held, left.held)
    left.last_done()
    right.last_done()
    w_left, w_right = left.rows().reshape(-1, columns), right.rows().reshape(-1, columns)
    packs = packed.halves()
    packs[0].over(bits[0], left.other)
    packs[1].over(bits[-1], left.other)
    both.along_z(packed.held)
    patches = embed_patches(base_pixels, w_left, w_right).reshape(group, capacity, grid, width)
    packs[0].done(patches)
    packs[1].done(patches)
    for k in range(1, len(bits)):
        packs[0].over(bits[k])
        packs[1].over(bits[-1 - k])
        packs[0].done()
        packs[1].done()
    both.z_done(patches)
    downs_w = Gather(place, both.held[:, : down_weight.shape[0]], both.bits)
    ups_w = Gather(place, both.held[:, down_weight.shape[0] :], both.bits)
    patch_mine, patch_sent = split_rows(place, after(patches, both.held))
    patch_got = place.swap_core(patch_sent)
    patch_pair = pair_up(place, patch_mine, patch_got)
    patch_moved = exchange(patch_pair)
    packs[0].last(patch_pair)
    packs[1].last(patch_pair)
    ups_w.over(bits[-1], packs[0].held, packs[1].held)
    downs_w.over(bits[0], packs[0].held, packs[1].held)
    for k in range(1, len(bits) - 1):
        ups_w.done()
        downs_w.done()
        ups_w.over(bits[-1 - k])
        downs_w.over(bits[k])

    halves = [
        [p.rows(i * shard, (i + 1) * shard).reshape(width, columns) for p in packs]
        for i in range(4)
    ]
    in_weights = [*halves[0], *halves[1], *halves[2]]
    w_out = halves[3]
    flat = jnp.concatenate([p.rows(4 * shard) for p in packs], axis=-1)
    table = (
        flat.reshape(devices, 16, TABLE // 16, lane)[..., :shard]
        .transpose(2, 1, 0, 3)
        .reshape(TABLE, width)
        .astype(f32)
    )
    b_up = (
        table[UP_AT : UP_AT + pieces]
        .reshape(pieces, devices, shard)
        .transpose(1, 0, 2)
        .reshape(1, ff)
    )
    (patch_moved,) = collect([patch_moved], table, b_up, cot_pair, *in_weights, *w_out)
    ups_w.done(patch_moved)
    downs_w.done(patch_moved)
    patch_peer = place.swap_core(patch_moved)
    patches = gather_rows(at, patch_moved, patch_peer, half).reshape(-1, width)
    if len(bits) > 1:
        ups_w.over(bits[0], patch_moved)
        downs_w.over(bits[-1], patch_moved)
    cot_moved = exchange(after(cot_pair, patch_moved))

    embed, attn_in, query, key, value = enter(at, patches, spread, table, in_weights)
    if len(bits) > 1:
        ups_w.done(query)
        downs_w.done(query)
    (cot_moved,) = collect([cot_moved], query)
    key_peer = place.swap_core(after(key, ups_w.held, downs_w.held, cot_moved))
    value_peer = place.swap_core(after(value, ups_w.held, downs_w.held, cot_moved))
    ups_w.last(key_peer, value_peer)
    downs_w.last(key_peer, value_peer)
    cot_peer = place.swap_core(after(cot_moved, key_peer, value_peer))
    attended, lse = attend(query, key, key_peer, value, value_peer)
    ups_w.last_done(attended)
    downs_w.last_done(attended)
    (cot_peer,) = collect([cot_peer], attended)
    w_up = (
        ups_w.rows()
        .reshape(devices, blocks, shard, width)
        .transpose(1, 0, 2, 3)
        .reshape(blocks, width, width)
    )
    w_down = downs_w.rows().reshape(ff, width)
    resid, mlp_in, hidden, slope, final = mlp(attended, embed, table, w_out, w_up, b_up, w_down)
    final_peer = place.swap_core(final)
    g_out = gather_rows(after(at, final), cot_moved, cot_peer, half).reshape(-1, width)

    early, late = bits[: len(bits) // 2], bits[len(bits) // 2 :][::-1]
    down = Scatter(place, *weight_grad(at, hidden, g_out, his))
    (final_peer,) = collect([final_peer], down.send)
    down.send = after(down.send, final_peer)
    down.first()
    image = (half, grid, width)
    final_pieces = spread_rows(
        at, final.reshape(image), final_peer.reshape(image), place.strips, capacity
    )
    down.first_done(final_pieces)
    for bit in late[:-1]:
        down.over(bit)
        down.done()
    down.over(late[-1])
    final_moved = exchange(after(final_pieces, down.sent))
    g_upper, g_resid, g_resid_low, g_att, sums_two = mlp_back(
        after(g_out, final_pieces, down.sent), slope, resid, table, w_out, w_up, w_down
    )
    g_query, g_key, g_key_peer, g_value, g_value_peer = attend_back(
        query, key, key_peer, value, value_peer, g_att, attended, lse
    )
    down.done(g_query)
    (final_moved,) = collect([final_moved], g_query)
    g_key_got = place.swap_core(after(g_key_peer, down.part, final_moved))
    g_value_got = place.swap_core(after(g_value_peer, down.part, final_moved))
    for bit in early[:-1]:
        down.over(bit)
        down.done()
    if early:
        down.over(early[-1])
    up = Scatter(
        place, *weight_grad(at, mlp_in, after(g_upper, g_query, down.sent, final_moved), his)
    )
    g_key_got, g_value_got = collect([g_key_got, g_value_got], up.send)
    up.send = after(up.send, g_key_got, g_value_got)
    up.first()
    g_query, g_key, g_value, g_embed, sums_one, g_pos = leave(
        at,
        after(g_query, up.send),
        g_key,
        g_key_got,
        g_value,
        g_value_got,
        embed,
        g_resid,
        spread_t,
        table,
        in_weights,
    )
    g_embed_peer = place.swap_core(g_embed)
    pieces_back = spread_rows(
        at,
        g_embed.reshape(image),
        g_embed_peer.reshape(image),
        place.strips,
        capacity,
    )
    back = exchange(pieces_back)
    up.first_done(pieces_back)
    for bit in late[:-1]:
        up.over(bit)
        up.done()
    up.over(late[-1])
    up_sums = (
        sums_two[8 : 8 + blocks]
        .reshape(devices, pieces, shard)
        .transpose(1, 0, 2)
        .reshape(pieces, width)
    )
    small = jnp.concatenate([sums_one, sums_two[:8], g_pos, up_sums])
    small = jnp.pad(small, ((0, 128 - small.shape[0]), (0, 0)))
    block_out = from_chip(place, after(final_moved, pieces_back), cotangent.shape)
    proj = Scatter(
        place,
        *(
            part[:, None]
            for part in proj_grad(
                after(at, pieces_back),
                attn_in,
                attended,
                g_query,
                g_key,
                g_value,
                g_resid_low,
                small,
                his,
            )
        ),
    )
    back, up.got, down.got = collect([back, up.got, down.got], proj.send, block_out)
    if early:
        down.done()
    up.done()
    proj.send = after(proj.send, back)
    proj.first()
    for bit in early[:-1]:
        up.over(bit)
        up.done()
    if early:
        up.part = after(up.part, back)
        up.over(early[-1])
    down_last = Last(after(down.by_strip(), back))
    g_patches = from_chip(place, back, cotangent.shape).reshape(tokens, width)
    proj.first_done(g_patches)
    projs = proj.halves(2 * width)
    projs[0].over(bits[-1])
    projs[1].over(bits[0])
    patch = Scatter(
        place,
        *weight_grad(
            at,
            base_pixels.reshape(tokens, pixel_len),
            after(g_patches, projs[0].sent, projs[1].sent, down_last.sent),
            his,
        ),
    )
    projs[0].done(patch.send)
    projs[1].done(patch.send)
    if early:
        up.done(patch.send)
    s_down = down_last.done(patch.send)
    patch.send = after(patch.send, projs[0].got, projs[1].got, up.got, down_last.got)
    patch.first()
    patch.first_done()
    patches = patch.halves()
    patches[0].over(bits[-1])
    patches[1].over(bits[0])
    for k in range(1, len(bits)):
        projs[0].over(bits[-1 - k])
        projs[1].over(bits[k])
        if k + 1 < len(bits):
            projs[0].done()
            projs[1].done()
    up_last = Last(after(up.by_strip(), patches[0].sent, patches[1].sent))
    pixel_grad = unmix(
        sizes,
        resize,
        w_left,
        w_right,
        after(
            g_patches,
            patches[0].sent,
            patches[1].sent,
            projs[0].sent,
            projs[1].sent,
            up_last.sent,
        ).reshape(group, local_rows, width),
    )
    patches[0].done(pixel_grad)
    patches[1].done(pixel_grad)
    if len(bits) > 1:
        projs[0].done(pixel_grad)
        projs[1].done(pixel_grad)
    s_up = up_last.done(pixel_grad)
    for scatter in patches:
        scatter.part = after(scatter.part, up_last.got)
    for k in range(1, len(bits)):
        patches[0].over(bits[-1 - k])
        patches[1].over(bits[k])
        if k + 1 < len(bits):
            patches[0].done()
            patches[1].done()
    proj_last = Last(jnp.concatenate([p.by_strip() for p in projs], axis=-1))
    s_proj = proj_last.done()
    if len(bits) > 1:
        patches[0].done(proj_last.got)
        patches[1].done(proj_last.got)
    s_patch = Last(jnp.concatenate([p.by_strip() for p in patches], axis=-1)).done()
    pixel_grad = pixel_grad.reshape(pixels.shape)

    s_up = s_up.reshape(blocks, shard, width).transpose(1, 0, 2).reshape(shard, ff)
    own = s_proj[:, 4 * width :].T
    s_query, s_key, s_value, s_out = (
        s_proj[:, i * width : (i + 1) * width] for i in range(4)
    )
    ahead = 8
    behind = 16
    up_at = behind + POS_ROWS

    return (
        block_out,
        pixel_grad,
        s_patch,
        own[behind : behind + BASE * BASE],
        own[0],
        own[1],
        own[2],
        s_query,
        own[3],
        s_key,
        s_value,
        own[4],
        s_out,
        own[ahead],
        own[ahead + 1],
        own[ahead + 2],
        s_up,
        own[up_at : up_at + pieces].reshape(-1),
        s_down,
        own[ahead + 3],
    )


def solution(mesh):
    rows = P(("img", "strip"))
    split_rows = P(("img", "strip"), None)
    split_columns = P(None, ("img", "strip"))
    held = P("img", "strip", None, None)
    return jax.shard_map(
        body,
        mesh=mesh,
        in_specs=(
            held,
            held,
            P(),
            P(),
            P(),
            P(),
            split_rows,
            split_columns,
            rows,
            rows,
            rows,
            split_rows,
            rows,
            split_rows,
            split_rows,
            rows,
            split_rows,
            rows,
            rows,
            rows,
            split_rows,
            rows,
            split_rows,
            rows,
        ),
        out_specs=(
            held,
            held,
            split_rows,
            split_columns,
            rows,
            rows,
            rows,
            split_rows,
            rows,
            split_rows,
            split_rows,
            rows,
            split_rows,
            rows,
            rows,
            rows,
            split_rows,
            rows,
            split_rows,
            rows,
        ),
        check_vma=False,
    )
```
